128 devices in a mesh: user: 8 (over z, core), item: 16 (over x, y).
Axes of the slice: x: 4, y: 4, z: 4, core: 2. Of those that a mesh axis runs over, the one named last changes fastest.
Arguments:
- table: bfloat16 [65536, 512], P(('user', 'item')), may hold values from -6 to 6
- tower_first: bfloat16 [512, 512], replicated, may hold values from -0.25 to 0.25
- tower_second: bfloat16 [512, 512], replicated, may hold values from -0.25 to 0.25
- w_input: bfloat16 [512, 2048], replicated, may hold values from -0.25 to 0.25
- w_output: bfloat16 [512, 512], replicated, may hold values from -0.25 to 0.25
- norm_gain: float32 [512], replicated, may hold values from 0.1 to 1.9
- head_vec: float32 [512], replicated, may hold values from -0.25 to 0.25
- time_bias: float32 [4, 16], replicated, may hold values from -3 to 3
- look_owner: int32 [128, 768, 1], P(('user', 'item')), may hold values from 0 to 127; in each aligned block of 768 rows (0 to 767, 768 to 1535, ..., all dimensions but the last counted through in order) at most 12 rows name the same one
- look_row: int32 [128, 768], P(('user', 'item')), may hold values from 0 to 511
- event_time: int32 [128, 768], P(('user', 'item')), may hold values from 0 to 130624, as said below
- labels: int32 [128, 768], P(('user', 'item')), may hold values 0 or 1
Outputs:
- table_grad: float32 [65536, 512], P(('user', 'item'))
- tower_first_grad: float32 [512, 512], replicated
- tower_second_grad: float32 [512, 512], replicated
- input_grad: float32 [512, 2048], replicated
- output_grad: float32 [512, 512], replicated
- user_loss: float32 [128], P(('user', 'item'))
The draws below stay inside these ranges and needn't reach their ends.
Inputs may be any that keep to these rules, and one draw needn't show every extreme that they name: `look_owner`: within one user's 768 lookups no owner is named more than 12 times; some owner is named exactly 12 times. `event_time`: history timestamps never fall; all candidates carry the request time, which is the largest value, later than every history event.
All inputs are finite; a program needn't handle non-finite values. No bound on the sum of `labels` on one device may be relied on, other than what follows from the above.
Results may differ from the reference program's by a relative error of at most 0.0095.
Values may be sent and summed in bfloat16 or wider, within the bound.
A program may use at most 128 MiB of HBM per device.

```python
import math
import jax
import jax.numpy as jnp
import numpy as np
from jax import lax

D = 512
HEADS = 4
TW = 512
BUCKETS = 16
HIST = 512
CAND = 256
ITEM_DEV = 512
LOOK = 768
OWNERS = 128
USERS = 128
ITEMS = 65536
CAP = 12


def draw_event_time(key, part):
    key = jax.random.fold_in(key, 7)
    gap_key, wait_key = jax.random.split(key)
    gap_top = 2 * (65536 // HIST)
    request_time = HIST * (gap_top - 1) + 64
    gaps = jax.random.randint(gap_key, (USERS, HIST), 0, gap_top)
    later = gaps[:, 1:]
    suffix = jnp.cumsum(later[:, ::-1], axis=1)[:, ::-1]
    suffix = jnp.concatenate([suffix, jnp.zeros((USERS, 1), jnp.int32)], axis=1)
    waiting = jax.random.randint(wait_key, (USERS, 1), 1, 64)
    history = request_time - waiting - suffix
    request = jnp.full((USERS, CAND), request_time, jnp.int32)
    return jnp.concatenate([history, request], axis=1).astype(jnp.int32)


def plant(array, own_key, low, top_value):
    place = [jax.random.randint(jax.random.fold_in(own_key, axis), (), 0, length) for axis, length in enumerate(array.shape)]
    widest = array.shape.index(max(array.shape))
    beside = place[:widest] + [(place[widest] + 1) % array.shape[widest]] + place[widest + 1:]
    return array.at[tuple(place)].set(low).at[tuple(beside)].set(top_value)


def block_levels(stream_key, shape, shards, smallest, largest):
    gain = 1.0
    for dim, shards_of in shards:
        heights = jax.random.uniform(jax.random.fold_in(jax.random.fold_in(stream_key, 6), dim), (shards_of,), jnp.float32, smallest / len(shards), largest / len(shards))
        gain = gain * jnp.repeat(jnp.exp(heights), shape[dim] // shards_of).reshape((-1,) + (1,) * (len(shape) - 1 - dim))
    return gain


def deal_out(own_key, own, number, rows, amount, top, limit, lean):
    ranking = jax.random.permutation(own_key, amount)
    heavy_load, usual = portions_of(amount, rows * top, limit, lean, True), portions_of(amount, rows * top, limit, lean, False)
    places = jnp.arange(amount)

    def named(sizes, turn):
        used = int((sizes > 0).sum())
        fixed = max(1, used // 4)
        moved = fixed + (places - fixed + turn * (used - fixed)) % max(1, amount - fixed)
        return jnp.zeros((amount,), jnp.int32).at[ranking[jnp.where(places < fixed, places, moved)]].set(jnp.asarray(sizes, jnp.int32))

    sizes = jnp.where(number % 4 == 0, named(heavy_load, number // 4), named(usual, number - number // 4 - 1))
    mixed = jax.random.permutation(jax.random.fold_in(own, 3), amount)
    giver, sink = mixed[0:amount // 2 * 2:2], mixed[1:amount // 2 * 2:2]
    slack = jnp.minimum(sizes[giver] - 1, limit - sizes[sink]) // 2
    slack = jnp.where((giver == ranking[0]) | (sink == ranking[0]) | (sizes[sink] == 0), 0, jnp.maximum(slack, 0))
    moved = jax.random.randint(jax.random.fold_in(own, 4), (amount // 2,), 0, 1 << 20) % (slack + 1)
    sizes = sizes.at[giver].add(-moved).at[sink].add(moved)
    items = jnp.searchsorted(jnp.cumsum(sizes), jnp.arange(rows * top), side="right").astype(jnp.int32)
    table = items.reshape(top, rows).T
    table = table[jax.random.permutation(jax.random.fold_in(own, 1), rows)]
    turn = jax.random.randint(jax.random.fold_in(own, 2), (rows, 1), 0, top)
    return jnp.take_along_axis(table, (jnp.arange(top)[None, :] + turn) % top, axis=1)


def portions_of(amount, total, bound, lean, full):
    portions = [(1 << 20) // math.isqrt(rank ** lean) + 1 for rank in range(1, amount + 1)]
    largest = bound if full else min(bound, max(-(-total // amount), total * portions[0] // sum(portions)))
    least = 1 if total - largest >= amount - 1 else 0
    holding, surplus = [largest] + [least] * (amount - 1), total - largest - least * (amount - 1)
    while surplus > 0:
        free = [i for i in range(1, amount) if holding[i] < largest] or [i for i in range(1, amount) if holding[i] < bound]
        mass, left = sum([portions[i] for i in free]), surplus
        for i in free:
            addition = min(bound - holding[i], max(1, left * portions[i] // mass), surplus)
            holding[i] = holding[i] + addition
            surplus = surplus - addition
    return np.array(holding)


def normal_values(key, shape, width, most, pieces=(), held_as=jnp.bfloat16):
    drawn = width * jax.random.normal(key, shape, jnp.float32)
    if pieces:
        drawn = drawn * block_levels(key, shape, pieces, -0.22, 0.18)
    return jnp.clip(drawn, -most, most).astype(held_as)


def setup_inputs(seed: int = 0) -> dict:
    arg_keys = jax.random.split(jax.random.key(seed), 13)
    table = normal_values(arg_keys[0], (ITEMS, D), 1.0, 6.0, ((0, 128),))
    tower_first = normal_values(arg_keys[1], (D, TW), D ** -0.5, 0.25)
    tower_second = normal_values(arg_keys[2], (TW, D), TW ** -0.5, 0.25)
    w_input = normal_values(arg_keys[3], (D, 4 * D), D ** -0.5, 0.25)
    w_output = normal_values(arg_keys[4], (D, D), D ** -0.5, 0.25)
    norm_gain = jnp.clip(1.0 + 0.18 * jax.random.normal(arg_keys[5], (D,), jnp.float32), 0.1, 1.9)
    head_vec = normal_values(arg_keys[6], (D,), D ** -0.5, 0.25, (), jnp.float32)
    time_bias = normal_values(arg_keys[7], (HEADS, BUCKETS), 0.5, 3.0, (), jnp.float32)
    look_owner_keys = jax.random.split(jax.random.fold_in(arg_keys[8], 1), USERS * LOOK // LOOK)
    look_owner_turns = jax.random.permutation(jax.random.fold_in(arg_keys[8], 3), USERS * LOOK // LOOK)
    look_owner = jax.vmap(lambda own, number: deal_out(jax.random.fold_in(arg_keys[8], 2), own, number, LOOK, OWNERS, 1, CAP, 2))(look_owner_keys, look_owner_turns).reshape((USERS, LOOK, 1))
    look_row = plant(jax.random.randint(arg_keys[9], (USERS, LOOK), 0, ITEM_DEV), jax.random.fold_in(arg_keys[9], 1), 0, ITEM_DEV - 1).astype(jnp.int32)
    event_time = draw_event_time(jax.random.fold_in(arg_keys[12], 71), 0)
    labels = plant((jax.random.randint(arg_keys[11], (USERS, LOOK), 0, 4) < 1).astype(jnp.int32), jax.random.fold_in(arg_keys[11], 1), 0, 1)
    return dict(table=table, tower_first=tower_first, tower_second=tower_second, w_input=w_input, w_output=w_output, norm_gain=norm_gain, head_vec=head_vec, time_bias=time_bias, look_owner=look_owner, look_row=look_row, event_time=event_time, labels=labels)


EPS = 1e-06

def tower_block(item_rows, first, second):
    hidden_items = jax.nn.silu(jnp.dot(item_rows.astype(jnp.bfloat16), first, preferred_element_type=jnp.float32)).astype(jnp.bfloat16)
    return item_rows + jnp.dot(hidden_items, second, preferred_element_type=jnp.float32)

def user_loss_fn(token_rows, first, second, norm_gain, head_vec, time_bias, stamps, clicked):
    head_count, bucket_count = time_bias.shape
    positions, features = token_rows.shape
    head_size = features // head_count
    mean_sq = lax.optimization_barrier(jnp.mean(token_rows * token_rows, axis=1, keepdims=True))
    normed = (token_rows * lax.rsqrt(mean_sq + EPS) * norm_gain).astype(jnp.bfloat16)
    proj = jax.nn.silu(jnp.dot(normed, first, preferred_element_type=jnp.float32)).astype(jnp.bfloat16)
    gates, values, queries, keys = jnp.split(proj, 4, axis=1)
    query_heads = queries.reshape(positions, head_count, head_size).astype(jnp.float32)
    key_heads = keys.reshape(positions, head_count, head_size).astype(jnp.float32)
    value_heads = values.reshape(positions, head_count, head_size).astype(jnp.float32)
    time_gap = stamps[:, None] - stamps[None, :HIST]
    time_term = jnp.zeros((head_count, positions, HIST), jnp.float32)
    for bucket in range(bucket_count):
        hit = (time_gap >= 2 ** bucket - 1).astype(jnp.float32)
        time_term = time_term + time_bias[:, bucket][:, None, None] * hit[None]
    score_scale = 1.0 / math.sqrt(head_size)
    scores = jnp.einsum('ihd,jhd->hij', query_heads, key_heads[:HIST]) * score_scale + time_term
    allowed = jnp.arange(HIST)[None, :] <= jnp.arange(positions)[:, None]
    weights = (jnp.where(allowed[None], jax.nn.silu(scores), 0.0) / HIST).astype(jnp.bfloat16)
    attended = jnp.einsum('hij,jhd->ihd', weights.astype(jnp.float32), value_heads[:HIST])
    own_score = lax.optimization_barrier(jnp.sum(query_heads * key_heads, axis=2)) * score_scale + time_bias[:, 0][None, :]
    is_cand = (jnp.arange(positions) >= HIST)[:, None]
    own_weight = (jnp.where(is_cand, jax.nn.silu(own_score), 0.0) / HIST).astype(jnp.bfloat16)
    attended = attended + own_weight.astype(jnp.float32)[:, :, None] * value_heads
    attended = attended.reshape(positions, features)
    centered = attended - lax.optimization_barrier(jnp.mean(attended, axis=1, keepdims=True))
    spread = lax.rsqrt(lax.optimization_barrier(jnp.mean(centered * centered, axis=1, keepdims=True)) + EPS)
    mixed_rows = (centered * spread * gates.astype(jnp.float32)).astype(jnp.bfloat16)
    output = token_rows + jnp.dot(mixed_rows, second, preferred_element_type=jnp.float32)
    logits = jnp.dot(output, head_vec, precision=lax.Precision.HIGHEST)
    return jnp.mean(jax.nn.softplus(logits) - clicked.astype(jnp.float32) * logits)

def reference(table, tower_first, tower_second, w_input, w_output, norm_gain, head_vec, time_bias, look_owner, look_row, event_time, labels):
    blocks = table.astype(jnp.float32).reshape(-1, ITEM_DEV, D)

    def embed_block(item_rows):
        return tower_block(item_rows, tower_first, tower_second).astype(jnp.bfloat16)
    item_embed = lax.map(embed_block, blocks).reshape(ITEMS, D)
    item_ids = (look_owner[:, :, 0] * ITEM_DEV + look_row).astype(jnp.int32)

    def per_user(totals, inputs):
        ids_user, stamps, clicked = inputs
        token_rows = item_embed[ids_user].astype(jnp.float32)

        def local_loss(rows_in, first, second):
            return user_loss_fn(rows_in, first, second, norm_gain, head_vec, time_bias, stamps, clicked)
        loss_value, back_fn = jax.vjp(local_loss, token_rows, w_input, w_output)
        token_grad, input_term, output_term = back_fn(jnp.ones((), jnp.float32))
        return ((totals[0] + input_term.astype(jnp.float32), totals[1] + output_term.astype(jnp.float32)), (loss_value, token_grad))
    zeros_init = (jnp.zeros((D, 4 * D), jnp.float32), jnp.zeros((D, D), jnp.float32))
    (input_grad, output_grad), (user_loss, token_grad) = lax.scan(per_user, zeros_init, (item_ids, event_time, labels))
    embed_grad = jnp.zeros((ITEMS, D), jnp.float32).at[item_ids.reshape(-1)].add(token_grad.reshape(-1, D))

    def per_block(totals, inputs):
        item_rows, row_grads = inputs
        unused, back_fn = jax.vjp(tower_block, item_rows, tower_first, tower_second)
        rows_term, first_term, second_term = back_fn(row_grads)
        return ((totals[0] + first_term.astype(jnp.float32), totals[1] + second_term.astype(jnp.float32)), rows_term)
    tower_init = (jnp.zeros((D, TW), jnp.float32), jnp.zeros((TW, D), jnp.float32))
    (first_grad, second_grad), table_blocks = lax.scan(per_block, tower_init, (blocks, embed_grad.reshape(-1, ITEM_DEV, D)))
    table_grad = table_blocks.reshape(ITEMS, D)
    return (table_grad, first_grad, second_grad, input_grad, output_grad, user_loss)
```

```python
import math

import jax
import jax.numpy as jnp
from jax import lax
from jax.experimental import pallas as pl
from jax.experimental.pallas import tpu as pltpu
from jax.sharding import PartitionSpec as P

D = 512
HEADS = 4
HD = 128
HIST = 512
LOOK = 768
BUCKETS = 16
EPS = 1e-06
F32 = jnp.float32
BF16 = jnp.bfloat16
RB = 128
NEG = -1e30


def nn(a, b):
    return lax.dot_general(a, b, (((1,), (0,)), ((), ())), preferred_element_type=F32)


def nt(a, b):
    return lax.dot_general(a, b, (((1,), (1,)), ((), ())), preferred_element_type=F32)


def sigmoid(x):
    return 0.5 + 0.5 * jnp.tanh(0.5 * x)


def keys_of(start):
    return min(HIST, start + RB)


def hstu_kernel(
    tok_ref, w1_ref, w2_ref, gain_ref, head_ref, tb_ref, stamp_row_ref, stamp_col_ref, label_ref,
    tgrad_ref, iterm_ref, uvec_ref, loss_ref,
    normed, proj, dsl, idx, wts, dwt, att, dp, dkv,
):
    gain = gain_ref[...]
    head = head_ref[...]
    scale = 1.0 / math.sqrt(HD)
    for s in range(0, LOOK, RB):
        rows = pl.ds(s, RB)
        t = tok_ref[rows, :].astype(F32)
        r = lax.rsqrt(jnp.mean(t * t, axis=1, keepdims=True) + EPS)
        normed[rows, :] = (t * r * gain).astype(BF16)
    for c in range(0, 4 * D, 256):
        cols = pl.ds(c, 256)
        for s in range(0, LOOK, RB):
            rows = pl.ds(s, RB)
            p = nn(normed[rows, :], w1_ref[:, cols])
            sg = sigmoid(p)
            y = p * sg
            proj[rows, cols] = y.astype(BF16)
            dsl[rows, cols] = (sg + y * (1.0 - sg)).astype(BF16)
    lane = lax.broadcasted_iota(jnp.int32, (HEADS, 128), 1)
    tab = jnp.zeros((HEADS, 128), F32)
    for k in range(BUCKETS):
        tab = tab + jnp.where(lane <= 31 - k, tb_ref[:, k : k + 1], 0.0)
    tab = jnp.where(lane == 33, NEG, tab)
    for s in range(0, LOOK, RB):
        rows = pl.ds(s, RB)
        ke = keys_of(s)
        gap = stamp_col_ref[rows, :] - stamp_row_ref[:, 0:ke]
        lz = lax.clz(gap + 1)
        if s < HIST:
            i_pos = s + lax.broadcasted_iota(jnp.int32, (RB, ke), 0)
            j_pos = lax.broadcasted_iota(jnp.int32, (RB, ke), 1)
            lz = jnp.where(j_pos <= i_pos, lz, 33)
        idx[rows, 0:ke] = lz
    for h in range(HEADS):
        hc = h * HD
        tab_h = jnp.broadcast_to(tab[h : h + 1, :], (RB, 128))
        for s in range(0, LOOK, RB):
            rows = pl.ds(s, RB)
            ke = keys_of(s)
            q = proj[rows, pl.ds(2 * D + hc, HD)]
            sc = nt(q, proj[0:ke, pl.ds(3 * D + hc, HD)]) * scale
            tt = [
                jnp.take_along_axis(tab_h, idx[rows, j : j + 128], axis=1)
                for j in range(0, ke, 128)
            ]
            sc = sc + jnp.concatenate(tt, axis=1)
            sg = sigmoid(sc)
            y = sc * sg
            w = (y * (1.0 / HIST)).astype(BF16)
            wts[h, rows, 0:ke] = w
            dwt[h, rows, 0:ke] = ((sg + y * (1.0 - sg)) * (1.0 / HIST)).astype(BF16)
            if ke < HIST:
                wts[h, rows, ke:HIST] = jnp.zeros((RB, HIST - ke), BF16)
            att[rows, pl.ds(hc, HD)] = nn(w, proj[0:ke, pl.ds(D + hc, HD)])
    own = {}
    for h in range(HEADS):
        hc = h * HD
        for s in range(HIST, LOOK, RB):
            rows = pl.ds(s, RB)
            q = proj[rows, pl.ds(2 * D + hc, HD)].astype(F32)
            k = proj[rows, pl.ds(3 * D + hc, HD)].astype(F32)
            v = proj[rows, pl.ds(D + hc, HD)].astype(F32)
            os = jnp.sum(q * k, axis=1, keepdims=True) * scale + tb_ref[h : h + 1, 0:1]
            sg = sigmoid(os)
            y = os * sg
            ow = (y * (1.0 / HIST)).astype(BF16).astype(F32)
            own[h, s] = (ow, (sg + y * (1.0 - sg)) * (1.0 / HIST))
            att[rows, pl.ds(hc, HD)] += ow * v
    h_hi = head.astype(BF16)
    h_mid = (head - h_hi.astype(F32)).astype(BF16)
    h_lo = (head - h_hi.astype(F32) - h_mid.astype(F32)).astype(BF16)
    parts = jnp.concatenate([h_hi, h_mid, h_lo, jnp.zeros((13, D), BF16)], axis=0)
    hw = jnp.sum(nt(parts, w2_ref[...]), axis=0, keepdims=True)
    loss = jnp.zeros((1, 1), F32)
    uvec = jnp.zeros((1, D), F32)
    dlogit = {}
    for s in range(0, LOOK, RB):
        rows = pl.ds(s, RB)
        a = att[rows, :]
        cen = a - jnp.mean(a, axis=1, keepdims=True)
        spread = lax.rsqrt(jnp.mean(cen * cen, axis=1, keepdims=True) + EPS)
        n = cen * spread
        g = proj[rows, 0:D].astype(F32)
        mixed = (n * g).astype(BF16).astype(F32)
        t = tok_ref[rows, :].astype(F32)
        logit = jnp.sum(t * head + mixed * hw, axis=1, keepdims=True)
        lab = label_ref[rows, :].astype(F32)
        soft = jnp.maximum(logit, 0.0) + jnp.log1p(jnp.exp(-jnp.abs(logit)))
        loss = loss + jnp.sum(soft - lab * logit, axis=0, keepdims=True)
        dl = (jax.nn.sigmoid(logit) - lab) * (1.0 / LOOK)
        dlogit[s] = dl
        uvec = uvec + jnp.sum(mixed * dl, axis=0, keepdims=True)
        dm = (dl * hw).astype(BF16).astype(F32)
        dg = dm * n
        dp[rows, 0:D] = (dg * dsl[rows, 0:D].astype(F32)).astype(BF16)
        dn = dm * g
        da = spread * (
            dn - jnp.mean(dn, axis=1, keepdims=True) - n * jnp.mean(dn * n, axis=1, keepdims=True)
        )
        att[rows, :] = da
    uvec_ref[...] = uvec
    loss_ref[...] = jnp.broadcast_to(loss * (1.0 / LOOK), loss_ref.shape)
    for h in range(HEADS):
        hc = h * HD
        for s in range(0, LOOK, RB):
            rows = pl.ds(s, RB)
            ke = keys_of(s)
            da = att[rows, pl.ds(hc, HD)]
            dw = nt(da.astype(BF16), proj[0:ke, pl.ds(D + hc, HD)])
            ds = (dw * dwt[h, rows, 0:ke].astype(F32) * scale).astype(BF16)
            dwt[h, rows, 0:ke] = ds
            if ke < HIST:
                dwt[h, rows, ke:HIST] = jnp.zeros((RB, HIST - ke), BF16)
            dq = nn(ds, proj[0:ke, pl.ds(3 * D + hc, HD)])
            if s >= HIST:
                q = proj[rows, pl.ds(2 * D + hc, HD)].astype(F32)
                k = proj[rows, pl.ds(3 * D + hc, HD)].astype(F32)
                v = proj[rows, pl.ds(D + hc, HD)].astype(F32)
                ow, osl = own[h, s]
                dos = jnp.sum(da * v, axis=1, keepdims=True) * osl * scale
                dq = dq + dos * k
                dcol = pl.ds(D + hc, HD)
                dp[rows, dcol] = (ow * da * dsl[rows, dcol].astype(F32)).astype(BF16)
                dcol = pl.ds(3 * D + hc, HD)
                dp[rows, dcol] = (dos * q * dsl[rows, dcol].astype(F32)).astype(BF16)
            dcol = pl.ds(2 * D + hc, HD)
            dp[rows, dcol] = (dq * dsl[rows, dcol].astype(F32)).astype(BF16)
        hist = pl.ds(0, HIST)
        dat = att[:, pl.ds(hc, HD)].T.astype(BF16)
        dcol = pl.ds(D + hc, HD)
        dp[hist, dcol] = (nn(dat, wts[h]).T * dsl[hist, dcol].astype(F32)).astype(BF16)
        qt = proj[:, pl.ds(2 * D + hc, HD)].astype(F32).T.astype(BF16)
        dcol = pl.ds(3 * D + hc, HD)
        dp[hist, dcol] = (nn(qt, dwt[h]).T * dsl[hist, dcol].astype(F32)).astype(BF16)
    for s in range(0, LOOK, RB):
        rows = pl.ds(s, RB)
        dnorm = nt(dp[rows, :], w1_ref[...])
        t = tok_ref[rows, :].astype(F32)
        r = lax.rsqrt(jnp.mean(t * t, axis=1, keepdims=True) + EPS)
        tn = dnorm * gain
        tgrad_ref[rows, :] = (
            dlogit[s] * head + r * tn - t * (r * r * r * jnp.mean(tn * t, axis=1, keepdims=True))
        ).astype(BF16)
    nrt = normed[...].astype(F32).T.astype(BF16)
    for c in range(0, 4 * D, 256):
        cols = pl.ds(c, 256)
        iterm_ref[:, cols] = nn(nrt, dp[:, cols]).astype(BF16)


def hstu(tok, w1, w2, gain, head, tb, stamps, labels):
    vm = pl.BlockSpec(memory_space=pltpu.VMEM)
    return pl.pallas_call(
        hstu_kernel,
        out_shape=(
            jax.ShapeDtypeStruct((LOOK, D), BF16),
            jax.ShapeDtypeStruct((D, 4 * D), BF16),
            jax.ShapeDtypeStruct((1, D), F32),
            jax.ShapeDtypeStruct((1, 128), F32),
        ),
        in_specs=[vm] * 9,
        out_specs=(vm,) * 4,
        scratch_shapes=[
            pltpu.VMEM((LOOK, D), BF16),
            pltpu.VMEM((LOOK, 4 * D), BF16),
            pltpu.VMEM((LOOK, 4 * D), BF16),
            pltpu.VMEM((LOOK, HIST), jnp.int32),
            pltpu.VMEM((HEADS, LOOK, HIST), BF16),
            pltpu.VMEM((HEADS, LOOK, HIST), BF16),
            pltpu.VMEM((LOOK, D), F32),
            pltpu.VMEM((LOOK, 4 * D), BF16),
            pltpu.VMEM((8, 128), F32),
        ],
        compiler_params=pltpu.CompilerParams(vmem_limit_bytes=56 * 2**20),
        cost_estimate=pl.CostEstimate(flops=8 * 10**9, bytes_accessed=8 * 2**20, transcendentals=4 * 10**6),
        name="hstu",
    )(
        tok, w1, w2, gain.reshape(1, D), head.reshape(1, D), tb,
        stamps.reshape(1, LOOK), stamps.reshape(LOOK, 1), labels.reshape(LOOK, 1),
    )


def tower_block(item_rows, first, second):
    hidden_items = jax.nn.silu(
        jnp.dot(item_rows.astype(jnp.bfloat16), first, preferred_element_type=jnp.float32)
    ).astype(jnp.bfloat16)
    return item_rows + jnp.dot(hidden_items, second, preferred_element_type=jnp.float32)


def body(
    table, tower_first, tower_second, w_input, w_output, norm_gain, head_vec, time_bias,
    look_owner, look_row, event_time, labels,
):
    n_user = lax.axis_size("user")
    n_item = lax.axis_size("item")
    owners = n_user * n_item
    lookups = look_row.shape[1]
    features = table.shape[1]
    capacity = 12
    owner_ids = look_owner[0, :, 0]
    targets = jnp.arange(owners, dtype=jnp.int32)
    onehot = (owner_ids[:, None] == targets[None, :]).astype(jnp.int32)
    position = jnp.sum(onehot * (jnp.cumsum(onehot, axis=0) - 1), axis=1)
    slot_index = owner_ids * capacity + position
    send_ids = (
        jnp.full((owners * capacity,), -1, jnp.int32)
        .at[slot_index]
        .set(look_row[0])
        .reshape(owners, capacity)
    )
    recv_ids = lax.all_to_all(send_ids, ("user", "item"), split_axis=0, concat_axis=0, tiled=True)
    item_rows = table.astype(jnp.float32)
    embed_f, tower_back = jax.vjp(tower_block, item_rows, tower_first, tower_second)
    embedding = embed_f.astype(jnp.bfloat16)
    is_live = recv_ids >= 0
    safe_rows = jnp.where(is_live, recv_ids, 0)
    replies = jnp.where(is_live[:, :, None], embedding[safe_rows], jnp.zeros((), jnp.bfloat16))
    back_rows = lax.all_to_all(replies, ("user", "item"), split_axis=0, concat_axis=0, tiled=True)
    tok = back_rows.reshape(owners * capacity, features)[slot_index]
    token_grad, input_term, uvec, loss = hstu(
        tok, w_input, w_output, norm_gain, head_vec, time_bias, event_time, labels
    )
    send_grad = (
        jnp.zeros((owners * capacity, features), BF16)
        .at[slot_index]
        .set(token_grad)
        .reshape(owners, capacity, features)
    )
    input_grad, uvec = lax.psum((input_term.astype(F32), uvec[0]), ("user", "item"))
    output_grad = uvec[:, None] * head_vec[None, :]
    recv_grad = lax.all_to_all(
        send_grad, ("user", "item"), split_axis=0, concat_axis=0, tiled=True
    ).astype(F32)
    live_grad = jnp.where(is_live[:, :, None], recv_grad, 0.0).reshape(owners * capacity, features)
    embed_grad = jnp.zeros_like(item_rows).at[safe_rows.reshape(-1)].add(live_grad)
    table_grad, first_term, second_term = tower_back(embed_grad)
    first_grad, second_grad = lax.psum(
        (first_term.astype(F32), second_term.astype(F32)), ("user", "item")
    )
    return (table_grad, first_grad, second_grad, input_grad, output_grad, loss[0, :1])


def solution(mesh):
    return jax.shard_map(
        body,
        mesh=mesh,
        in_specs=(
            P(("user", "item"), None), P(), P(), P(), P(), P(), P(), P(),
            P(("user", "item"), None, None), P(("user", "item"), None),
            P(("user", "item"), None), P(("user", "item"), None),
        ),
        out_specs=(P(("user", "item"), None), P(), P(), P(), P(), P(("user", "item"))),
        check_vma=False,
    )
```

```python
import math

import jax
import jax.numpy as jnp
from jax import lax
from jax.experimental import pallas as pl
from jax.experimental.pallas import tpu as pltpu
from jax.sharding import PartitionSpec as P

D = 512
HEADS = 4
HD = 128
HIST = 512
LOOK = 768
BUCKETS = 16
EPS = 1e-06
F32 = jnp.float32
BF16 = jnp.bfloat16
RB = 128
OWNERS = 128
SLOT = 16
USED = 12
PACK = 384
ROWS = OWNERS * SLOT
TILE = 256
NEG = -1e30


def nn(a, b):
    return lax.dot_general(a, b, (((1,), (0,)), ((), ())), preferred_element_type=F32)


def nt(a, b):
    return lax.dot_general(a, b, (((1,), (1,)), ((), ())), preferred_element_type=F32)


def sigmoid(x):
    return 0.5 + 0.5 * jnp.tanh(0.5 * x)


def column(row):
    return jnp.broadcast_to(row.astype(F32), (128, row.shape[1])).T


def keys_of(start):
    return min(HIST, start + RB)


def hstu_kernel(
    tok_ref, w1_ref, w2_ref, gain_ref, head_ref, tb_ref, stamp_row_ref, label_ref,
    tgrad_ref, iterm_ref, uvec_ref, loss_ref,
    normed, proj, dsl, idx, wts, dwt, att, dp,
):
    gain = gain_ref[...]
    head = head_ref[...]
    scale = 1.0 / math.sqrt(HD)
    for s in range(0, LOOK, RB):
        rows = pl.ds(s, RB)
        t = tok_ref[rows, :].astype(F32)
        r = lax.rsqrt(jnp.mean(t * t, axis=1, keepdims=True) + EPS)
        normed[rows, :] = (t * r * gain).astype(BF16)
    for c in range(0, 4 * D, 256):
        cols = pl.ds(c, 256)
        for s in range(0, LOOK, RB):
            rows = pl.ds(s, RB)
            p = nn(normed[rows, :], w1_ref[:, cols])
            sg = sigmoid(p)
            y = p * sg
            proj[rows, cols] = y.astype(BF16)
            dsl[rows, cols] = (sg + y * (1.0 - sg)).astype(BF16)
    lane = lax.broadcasted_iota(jnp.int32, (HEADS, 128), 1)
    tab = jnp.zeros((HEADS, 128), F32)
    for k in range(BUCKETS):
        tab = tab + jnp.where(lane <= 31 - k, tb_ref[:, k : k + 1], 0.0)
    tab = jnp.where(lane == 33, NEG, tab)
    stamp_col = column(stamp_row_ref[...]).astype(jnp.int32)
    for s in range(0, LOOK, RB):
        rows = pl.ds(s, RB)
        ke = keys_of(s)
        now = jnp.concatenate([stamp_col[s : s + RB, :]] * (ke // 128), axis=1)
        gap = now - stamp_row_ref[:, 0:ke]
        lz = lax.clz(gap + 1)
        if s < HIST:
            i_pos = s + lax.broadcasted_iota(jnp.int32, (RB, ke), 0)
            j_pos = lax.broadcasted_iota(jnp.int32, (RB, ke), 1)
            lz = jnp.where(j_pos <= i_pos, lz, 33)
        idx[rows, 0:ke] = lz
    for h in range(HEADS):
        hc = h * HD
        tab_h = jnp.broadcast_to(tab[h : h + 1, :], (RB, 128))
        for s in range(0, LOOK, RB):
            rows = pl.ds(s, RB)
            ke = keys_of(s)
            q = proj[rows, pl.ds(2 * D + hc, HD)]
            sc = nt(q, proj[0:ke, pl.ds(3 * D + hc, HD)]) * scale
            tt = [
                jnp.take_along_axis(tab_h, idx[rows, j : j + 128], axis=1)
                for j in range(0, ke, 128)
            ]
            sc = sc + jnp.concatenate(tt, axis=1)
            sg = sigmoid(sc)
            y = sc * sg
            w = (y * (1.0 / HIST)).astype(BF16)
            wts[h, rows, 0:ke] = w
            dwt[h, rows, 0:ke] = ((sg + y * (1.0 - sg)) * (1.0 / HIST)).astype(BF16)
            if ke < HIST:
                wts[h, rows, ke:HIST] = jnp.zeros((RB, HIST - ke), BF16)
            att[rows, pl.ds(hc, HD)] = nn(w, proj[0:ke, pl.ds(D + hc, HD)])
    own = {}
    for h in range(HEADS):
        hc = h * HD
        for s in range(HIST, LOOK, RB):
            rows = pl.ds(s, RB)
            q = proj[rows, pl.ds(2 * D + hc, HD)].astype(F32)
            k = proj[rows, pl.ds(3 * D + hc, HD)].astype(F32)
            v = proj[rows, pl.ds(D + hc, HD)].astype(F32)
            os = jnp.sum(q * k, axis=1, keepdims=True) * scale + tb_ref[h : h + 1, 0:1]
            sg = sigmoid(os)
            y = os * sg
            ow = (y * (1.0 / HIST)).astype(BF16).astype(F32)
            own[h, s] = (ow, (sg + y * (1.0 - sg)) * (1.0 / HIST))
            att[rows, pl.ds(hc, HD)] += ow * v
    h_hi = head.astype(BF16)
    h_mid = (head - h_hi.astype(F32)).astype(BF16)
    h_lo = (head - h_hi.astype(F32) - h_mid.astype(F32)).astype(BF16)
    parts = jnp.concatenate([h_hi, h_mid, h_lo, jnp.zeros((13, D), BF16)], axis=0)
    hw = jnp.sum(nt(parts, w2_ref[...]), axis=0, keepdims=True)
    label_col = column(label_ref[...])
    loss = jnp.zeros((1, 1), F32)
    uvec = jnp.zeros((1, D), F32)
    dlogit = {}
    for s in range(0, LOOK, RB):
        rows = pl.ds(s, RB)
        a = att[rows, :]
        cen = a - jnp.mean(a, axis=1, keepdims=True)
        spread = lax.rsqrt(jnp.mean(cen * cen, axis=1, keepdims=True) + EPS)
        n = cen * spread
        g = proj[rows, 0:D].astype(F32)
        mixed = (n * g).astype(BF16).astype(F32)
        t = tok_ref[rows, :].astype(F32)
        logit = jnp.sum(t * head + mixed * hw, axis=1, keepdims=True)
        lab = label_col[s : s + RB, 0:1]
        soft = jnp.maximum(logit, 0.0) + jnp.log1p(jnp.exp(-jnp.abs(logit)))
        loss = loss + jnp.sum(soft - lab * logit, axis=0, keepdims=True)
        dl = (jax.nn.sigmoid(logit) - lab) * (1.0 / LOOK)
        dlogit[s] = dl
        uvec = uvec + jnp.sum(mixed * dl, axis=0, keepdims=True)
        dm = (dl * hw).astype(BF16).astype(F32)
        dg = dm * n
        dp[rows, 0:D] = (dg * dsl[rows, 0:D].astype(F32)).astype(BF16)
        dn = dm * g
        da = spread * (
            dn - jnp.mean(dn, axis=1, keepdims=True) - n * jnp.mean(dn * n, axis=1, keepdims=True)
        )
        att[rows, :] = da
    uvec_ref[...] = uvec
    loss_ref[...] = jnp.broadcast_to(loss * (1.0 / LOOK), loss_ref.shape)
    for h in range(HEADS):
        hc = h * HD
        for s in range(0, LOOK, RB):
            rows = pl.ds(s, RB)
            ke = keys_of(s)
            da = att[rows, pl.ds(hc, HD)]
            dw = nt(da.astype(BF16), proj[0:ke, pl.ds(D + hc, HD)])
            ds = (dw * dwt[h, rows, 0:ke].astype(F32) * scale).astype(BF16)
            dwt[h, rows, 0:ke] = ds
            if ke < HIST:
                dwt[h, rows, ke:HIST] = jnp.zeros((RB, HIST - ke), BF16)
            dq = nn(ds, proj[0:ke, pl.ds(3 * D + hc, HD)])
            if s >= HIST:
                q = proj[rows, pl.ds(2 * D + hc, HD)].astype(F32)
                k = proj[rows, pl.ds(3 * D + hc, HD)].astype(F32)
                v = proj[rows, pl.ds(D + hc, HD)].astype(F32)
                ow, osl = own[h, s]
                dos = jnp.sum(da * v, axis=1, keepdims=True) * osl * scale
                dq = dq + dos * k
                dcol = pl.ds(D + hc, HD)
                dp[rows, dcol] = (ow * da * dsl[rows, dcol].astype(F32)).astype(BF16)
                dcol = pl.ds(3 * D + hc, HD)
                dp[rows, dcol] = (dos * q * dsl[rows, dcol].astype(F32)).astype(BF16)
            dcol = pl.ds(2 * D + hc, HD)
            dp[rows, dcol] = (dq * dsl[rows, dcol].astype(F32)).astype(BF16)
        hist = pl.ds(0, HIST)
        dat = att[:, pl.ds(hc, HD)].T.astype(BF16)
        dcol = pl.ds(D + hc, HD)
        dp[hist, dcol] = (nn(dat, wts[h]).T * dsl[hist, dcol].astype(F32)).astype(BF16)
        qt = proj[:, pl.ds(2 * D + hc, HD)].astype(F32).T.astype(BF16)
        dcol = pl.ds(3 * D + hc, HD)
        dp[hist, dcol] = (nn(qt, dwt[h]).T * dsl[hist, dcol].astype(F32)).astype(BF16)
    for s in range(0, LOOK, RB):
        rows = pl.ds(s, RB)
        dnorm = nt(dp[rows, :], w1_ref[...])
        t = tok_ref[rows, :].astype(F32)
        r = lax.rsqrt(jnp.mean(t * t, axis=1, keepdims=True) + EPS)
        tn = dnorm * gain
        tgrad_ref[rows, :] = (
            dlogit[s] * head + r * tn - t * (r * r * r * jnp.mean(tn * t, axis=1, keepdims=True))
        ).astype(BF16)
    nrt = normed[...].astype(F32).T.astype(BF16)
    for c in range(0, 4 * D, 256):
        cols = pl.ds(c, 256)
        iterm_ref[c // D, :, pl.ds(c % D, 256)] = nn(nrt, dp[:, cols]).astype(BF16)


def hstu(tok, w1, w2, gain, head, tb, stamps, labels):
    vm = pl.BlockSpec(memory_space=pltpu.VMEM)
    return pl.pallas_call(
        hstu_kernel,
        out_shape=(
            jax.ShapeDtypeStruct((LOOK, D), BF16),
            jax.ShapeDtypeStruct((4, D, D), BF16),
            jax.ShapeDtypeStruct((1, D), F32),
            jax.ShapeDtypeStruct((1, 128), F32),
        ),
        in_specs=[vm] * 8,
        out_specs=(vm,) * 4,
        scratch_shapes=[
            pltpu.VMEM((LOOK, D), BF16),
            pltpu.VMEM((LOOK, 4 * D), BF16),
            pltpu.VMEM((LOOK, 4 * D), BF16),
            pltpu.VMEM((LOOK, HIST), jnp.int32),
            pltpu.VMEM((HEADS, LOOK, HIST), BF16),
            pltpu.VMEM((HEADS, LOOK, HIST), BF16),
            pltpu.VMEM((LOOK, D), F32),
            pltpu.VMEM((LOOK, 4 * D), BF16),
        ],
        compiler_params=pltpu.CompilerParams(vmem_limit_bytes=56 * 2**20),
        cost_estimate=pl.CostEstimate(flops=8 * 10**9, bytes_accessed=8 * 2**20, transcendentals=4 * 10**6),
        name="hstu",
    )(
        tok, w1, w2, gain.reshape(1, D), head.reshape(1, D), tb,
        stamps.reshape(1, LOOK), labels.reshape(1, LOOK),
    )


def place():
    return lax.axis_index("user"), lax.axis_index("item")


def device(index):
    return (index // 16, index % 16)


def greet(me):
    barrier = pltpu.get_barrier_semaphore()

    @pl.loop(1, OWNERS)
    def _(k):
        pl.semaphore_signal(
            barrier, inc=1, device_id=device((me + k) % OWNERS), device_id_type=pl.DeviceIdType.MESH
        )


def meet():
    pl.semaphore_wait(pltpu.get_barrier_semaphore(), OWNERS - 1)


def row_in_slot(n):
    return lax.broadcasted_iota(jnp.int32, (n, 128), 0) % SLOT


def pack(y):
    r = row_in_slot(y.shape[0])
    last = y[:, PACK:D]
    out = [
        jnp.where(r >= USED, pltpu.roll(last, USED - 4 * b, 0), y[:, 128 * b : 128 * (b + 1)])
        for b in range(3)
    ]
    return jnp.concatenate(out, axis=1).astype(BF16)


def unpack_last(y):
    n = y.shape[0]
    r = row_in_slot(n)
    p = [pltpu.roll(y[:, 128 * b : 128 * (b + 1)].astype(F32), n - USED + 4 * b, 0) for b in range(3)]
    return jnp.where(r < 4, p[0], jnp.where(r < 8, p[1], p[2])).astype(BF16)


def chunk(ref, k):
    return ref.at[pl.ds(pl.multiple_of(k * SLOT, SLOT), SLOT), :]


def send_chunk(send, recv, k, target, send_sem, recv_sem):
    pltpu.make_async_remote_copy(
        src_ref=chunk(send, k),
        dst_ref=chunk(recv, k),
        send_sem=send_sem,
        recv_sem=recv_sem,
        device_id=device(target),
        device_id_type=pl.DeviceIdType.MESH,
    ).start()


def wait_bytes(ref, sem):
    pltpu.make_async_copy(ref, ref, sem).wait()


def silu_parts(p):
    sg = sigmoid(p)
    y = p * sg
    return y, sg + y * (1.0 - sg)


def front_kernel(
    owner_ref, row_ref, table_ref, first_ref, second_ref,
    tok_ref, slot_ref, idrow_ref,
    ids_send, ids_recv, embed, idq, send, recv, last, sems,
):
    user, item = place()
    me = user * 16 + item
    greet(me)
    j_row = (owner_ref[...] - me + OWNERS) % OWNERS
    named = lax.broadcasted_iota(jnp.int32, (OWNERS, LOOK), 0) == j_row
    named_b = named.astype(F32).astype(BF16)
    before = lax.broadcasted_iota(jnp.int32, (LOOK, LOOK), 0) < lax.broadcasted_iota(
        jnp.int32, (LOOK, LOOK), 1
    )
    earlier = nn(named_b, before.astype(F32).astype(BF16))
    rank = jnp.sum(jnp.where(named, earlier, 0.0), axis=0, keepdims=True)
    slot_ref[...] = j_row * SLOT + rank.astype(jnp.int32)
    lanes = lax.broadcasted_iota(jnp.int32, (LOOK, 128), 1).astype(F32)
    listed = jnp.where(column(rank) == lanes, column(row_ref[...]) - 256.0, 0.0)
    ids_send[:, 0, :] = nn(named_b, listed.astype(BF16))
    ids_recv[0] = ids_send[0]
    meet()

    def ids_copy(k):
        return pltpu.make_async_remote_copy(
            src_ref=ids_send.at[k],
            dst_ref=ids_recv.at[k],
            send_sem=sems.at[0],
            recv_sem=sems.at[1],
            device_id=device((me + k) % OWNERS),
            device_id_type=pl.DeviceIdType.MESH,
        )

    @pl.loop(1, OWNERS)
    def _(k):
        ids_copy(k).start()

    for s in range(0, D, 256):
        rows = pl.ds(s, 256)
        hidden, _ = silu_parts(nn(table_ref[rows, :], first_ref[...]))
        embed[rows, :] = (
            table_ref[rows, :].astype(F32) + nn(hidden.astype(BF16), second_ref[...])
        ).astype(BF16)
    others = pl.ds(1, OWNERS - 1)
    wait_bytes(ids_recv.at[others], sems.at[1])
    wait_bytes(ids_send.at[others], sems.at[0])
    ids = ids_recv[:, 0, :].astype(BF16)

    @pl.loop(0, ROWS // TILE)
    def _(t):
        base = t * TILE
        rows = pl.ds(pl.multiple_of(base, TILE), TILE)
        at = base + lax.broadcasted_iota(jnp.int32, (TILE, 128), 0)
        lane = lax.broadcasted_iota(jnp.int32, (TILE, 128), 1)
        spread = nn((at // SLOT == lane).astype(F32).astype(BF16), ids)
        r = at % SLOT
        mine = jnp.sum(jnp.where(r == lane, spread + 256.0, 0.0), axis=1, keepdims=True)
        mine = jnp.where(r < USED, mine, -1.0)
        idq[rows, :] = mine
        cols = lax.broadcasted_iota(jnp.int32, (TILE, 128), 1).astype(F32)
        pick = jnp.concatenate(
            [(mine == cols + 128.0 * b).astype(F32).astype(BF16) for b in range(4)], axis=1
        )
        send[rows, :] = pack(nn(pick, embed[...]))

        @pl.loop(0, TILE // SLOT)
        def _(i):
            k = t * (TILE // SLOT) + i

            @pl.when(k > 0)
            def _():
                send_chunk(send, recv, k, (me - k + OWNERS) % OWNERS, sems.at[2], sems.at[3])

    recv[0:SLOT, :] = send[0:SLOT, :]
    idrow_ref[...] = idq[...].T[0:8, :]
    slot_col = column(slot_ref[...])
    later = pl.ds(SLOT, ROWS - SLOT)
    wait_bytes(recv.at[later], sems.at[3])
    for s in range(0, ROWS, TILE):
        rows = pl.ds(s, TILE)
        last[rows, :] = unpack_last(recv[rows, :])
    for s in range(0, LOOK, RB):
        rows = pl.ds(s, RB)
        mark = slot_col[s : s + RB, :]
        cols = lax.broadcasted_iota(jnp.int32, (RB, 128), 1).astype(F32)
        pick = jnp.concatenate(
            [(mark == cols + float(b)).astype(F32).astype(BF16) for b in range(0, ROWS, 128)],
            axis=1,
        )
        tok_ref[rows, 0:PACK] = nn(pick, recv[...]).astype(BF16)
        tok_ref[rows, PACK:D] = nn(pick, last[...]).astype(BF16)
    wait_bytes(send.at[later], sems.at[2])


VM = pl.BlockSpec(memory_space=pltpu.VMEM)


def front(owner, row, table, first, second):
    return pl.pallas_call(
        front_kernel,
        out_shape=(
            jax.ShapeDtypeStruct((LOOK, D), BF16),
            jax.ShapeDtypeStruct((1, LOOK), jnp.int32),
            jax.ShapeDtypeStruct((8, ROWS), F32),
        ),
        in_specs=[VM] * 5,
        out_specs=(VM,) * 3,
        scratch_shapes=[
            pltpu.VMEM((OWNERS, 1, 128), F32),
            pltpu.VMEM((OWNERS, 1, 128), F32),
            pltpu.VMEM((D, D), BF16),
            pltpu.VMEM((ROWS, 128), F32),
            pltpu.VMEM((ROWS, PACK), BF16),
            pltpu.VMEM((ROWS, PACK), BF16),
            pltpu.VMEM((ROWS, 128), BF16),
            pltpu.SemaphoreType.DMA((4,)),
        ],
        compiler_params=pltpu.CompilerParams(
            vmem_limit_bytes=48 * 2**20, collective_id=0, has_side_effects=True
        ),
        cost_estimate=pl.CostEstimate(
            flops=4 * 10**9, bytes_accessed=8 * 2**20, transcendentals=10**6
        ),
        name="front",
    )(owner, row, table, first, second)


BLOCKS = 6
EARLY = (0, 1, 2, 3)
LATE = (4, 5)
ORDER = ("xyz", "yzx", "zxy", "xyz", "yzx", "zxy")
H1 = D // 8
H2 = H1 // 4


def back_kernel(
    tgrad_ref, slot_ref, idrow_ref, iterm_ref, uvec_ref, table_ref, first_ref, second_ref,
    tablegrad_ref, sums_ref, usum_ref,
    send, recv, last, terms, core_in, half, in1, part1, in2, part2, in3, u_held, u_in,
    hidden_t, table_t, slope,
    sems, send_sems, recv_sems, u_sems,
):
    user, item = place()
    me = user * 16 + item
    greet(me)
    z, core = user // 2, user % 2
    x, y = item // 4, item % 4
    own = {"x": x, "y": y, "z": z}

    def peer(axis, d):
        if axis == "c":
            return (z * 2 + 1 - core, item)
        to = (own[axis] + d) % 4
        if axis == "x":
            return (user, to * 4 + y)
        if axis == "y":
            return (user, x * 4 + to)
        return (to * 2 + core, item)

    def copy(src, dst, to, send_sem, recv_sem):
        return pltpu.make_async_remote_copy(
            src_ref=src, dst_ref=dst, send_sem=send_sem, recv_sem=recv_sem,
            device_id=to, device_id_type=pl.DeviceIdType.MESH,
        )

    def at(n, size):
        return pl.ds(pl.multiple_of(n * size, size), size)

    def term(b):
        return iterm_ref.at[b] if b in EARLY else terms.at[b - 4]

    def copies(b, stage):
        if stage in (0, 7):
            if stage == 0:
                src, dst = term(b).at[at(1 - core, 256), :], core_in.at[b]
            else:
                src = dst = sums_ref.at[b, at(core, 256), :]
            return [copy(src, dst, peer("c", 1), send_sems.at[b, stage, 0], recv_sems.at[b, stage, 0])]
        axes = ORDER[b]
        a0, a1, a2 = (own[a] for a in axes)
        step = stage - 1 if stage < 4 else 6 - stage
        out = []
        for d in (1, 2, 3):
            to = (own[axes[step]] + d) % 4
            if stage == 1:
                src, dst = half.at[b, at(to, 64), :], in1.at[b, d - 1]
            elif stage == 2:
                src, dst = part1.at[b, :, at(to, 128)], in2.at[b, d - 1]
            elif stage == 3:
                src, dst = part2.at[b, at(to, 16), :], in3.at[b, d - 1]
            elif stage == 4:
                src = dst = sums_ref.at[b, pl.ds(pl.multiple_of(core * 256 + a0 * 64 + a2 * 16, 16), 16), at(a1, 128)]
            elif stage == 5:
                src = dst = sums_ref.at[b, pl.ds(pl.multiple_of(core * 256 + a0 * 64, 64), 64), at(a1, 128)]
            else:
                src = dst = sums_ref.at[b, pl.ds(pl.multiple_of(core * 256 + a0 * 64, 64), 64), :]
            out.append(
                copy(src, dst, peer(axes[step], d), send_sems.at[b, stage, d - 1], recv_sems.at[b, stage, d - 1])
            )
        return out

    def start(b, stage):
        for c in copies(b, stage):
            c.start()

    def finish(b, stage):
        for c in copies(b, stage):
            c.wait_recv()
        a0, a1, a2 = (own[a] for a in ORDER[b])
        if stage == 0:
            half[b] = (term(b)[at(core, 256), :].astype(F32) + core_in[b].astype(F32)).astype(BF16)
        elif stage == 1:
            part1[b] = add4(half[b, at(a0, 64), :], in1, b)
        elif stage == 2:
            part2[b] = add4(part1[b, :, at(a1, 128)], in2, b)
        elif stage == 3:
            rows = pl.ds(pl.multiple_of(core * 256 + a0 * 64 + a2 * 16, 16), 16)
            sums_ref[b, rows, at(a1, 128)] = add4(part2[b, at(a2, 16), :], in3, b)

    def add4(mine, arrived, b):
        total = mine.astype(F32)
        for d in range(3):
            total = total + arrived[b, d].astype(F32)
        return total.astype(BF16)

    def u_copies(stage):
        axis = "cxyz"[stage]
        return [
            copy(u_held.at[stage], u_in.at[stage, d - 1], peer(axis, d), u_sems.at[0, stage, d - 1], u_sems.at[1, stage, d - 1])
            for d in ((1,) if stage == 0 else (1, 2, 3))
        ]

    def u_start(stage):
        for c in u_copies(stage):
            c.start()

    def u_finish(stage):
        total = u_held[stage]
        for d, c in enumerate(u_copies(stage)):
            c.wait_recv()
            total = total + u_in[stage, d]
        if stage < 3:
            u_held[stage + 1] = total
        else:
            usum_ref[...] = total

    slots = slot_ref[...]
    tgrad = tgrad_ref[...]

    @pl.loop(0, ROWS // TILE)
    def _(t):
        base = t * TILE
        rows = pl.ds(pl.multiple_of(base, TILE), TILE)
        pick = base + lax.broadcasted_iota(jnp.int32, (TILE, LOOK), 0) == slots
        send[rows, :] = pack(nn(pick.astype(F32).astype(BF16), tgrad))

    u_held[0] = uvec_ref[...]
    recv[0:SLOT, :] = send[0:SLOT, :]
    meet()
    for b in EARLY:
        start(b, 0)
    u_start(0)

    @pl.loop(1, OWNERS)
    def _(k):
        send_chunk(send, recv, k, (me + k) % OWNERS, sems.at[0], sems.at[1])

    for s in range(0, D, 256):
        rows = pl.ds(s, 256)
        tab = table_ref[rows, :]
        hidden, dh = silu_parts(nn(tab, first_ref[...]))
        slope[rows, :] = dh
        hidden_t[:, rows] = hidden.T.astype(BF16)
        table_t[:, rows] = tab.astype(F32).T.astype(BF16)
    for b in EARLY:
        finish(b, 0)
        start(b, 1)
    u_finish(0)
    u_start(1)
    later = pl.ds(SLOT, ROWS - SLOT)
    wait_bytes(recv.at[later], sems.at[1])
    for s in range(0, ROWS, TILE):
        rows = pl.ds(s, TILE)
        last[rows, :] = unpack_last(recv[rows, :])
    for s in range(0, D, 128):
        rows = pl.ds(s, 128)
        sub = (s + lax.broadcasted_iota(jnp.int32, (128, 128), 0)).astype(F32)
        pick = jnp.concatenate(
            [
                (sub == idrow_ref[0:1, q : q + 128]).astype(F32).astype(BF16)
                for q in range(0, ROWS, 128)
            ],
            axis=1,
        )
        tablegrad_ref[rows, 0:PACK] = nn(pick, recv[...])
        tablegrad_ref[rows, PACK:D] = nn(pick, last[...])
    de = tablegrad_ref[...].astype(BF16)
    terms[1] = nn(hidden_t[...], de).astype(BF16)
    start(5, 0)
    dpre = (nt(de, second_ref[...]) * slope[...]).astype(BF16)
    terms[0] = nn(table_t[...], dpre).astype(BF16)
    start(4, 0)
    for b in EARLY:
        finish(b, 1)
        start(b, 2)
    u_finish(1)
    u_start(2)
    tablegrad_ref[...] += nt(dpre, first_ref[...])
    for b in LATE:
        finish(b, 0)
        start(b, 1)
    for stage in range(2, 7):
        for b in EARLY:
            finish(b, stage)
            start(b, stage + 1)
        if stage < 4:
            u_finish(stage)
        if stage < 3:
            u_start(stage + 1)
        for b in LATE:
            finish(b, stage - 1)
            start(b, stage)
    for b in LATE:
        finish(b, 6)
        start(b, 7)
    for b in EARLY + LATE:
        finish(b, 7)
    wait_bytes(send.at[later], sems.at[0])
    for stage in range(4):
        for c in u_copies(stage):
            c.wait_send()
    for b in EARLY + LATE:
        for stage in range(8):
            for c in copies(b, stage):
                c.wait_send()


def back(tgrad, slots, idrow, iterm, uvec, table, first, second):
    dma = pltpu.SemaphoreType.DMA
    return pl.pallas_call(
        back_kernel,
        out_shape=(
            jax.ShapeDtypeStruct((D, D), F32),
            jax.ShapeDtypeStruct((BLOCKS, D, D), BF16),
            jax.ShapeDtypeStruct((1, D), F32),
        ),
        in_specs=[VM] * 8,
        out_specs=(VM,) * 3,
        scratch_shapes=[
            pltpu.VMEM((ROWS, PACK), BF16),
            pltpu.VMEM((ROWS, PACK), BF16),
            pltpu.VMEM((ROWS, 128), BF16),
            pltpu.VMEM((2, D, D), BF16),
            pltpu.VMEM((BLOCKS, 256, D), BF16),
            pltpu.VMEM((BLOCKS, 256, D), BF16),
            pltpu.VMEM((BLOCKS, 3, 64, D), BF16),
            pltpu.VMEM((BLOCKS, 64, D), BF16),
            pltpu.VMEM((BLOCKS, 3, 64, 128), BF16),
            pltpu.VMEM((BLOCKS, 64, 128), BF16),
            pltpu.VMEM((BLOCKS, 3, 16, 128), BF16),
            pltpu.VMEM((4, 1, D), F32),
            pltpu.VMEM((4, 3, 1, D), F32),
            pltpu.VMEM((D, D), BF16),
            pltpu.VMEM((D, D), BF16),
            pltpu.VMEM((D, D), F32),
            dma((2,)),
            dma((BLOCKS, 8, 3)),
            dma((BLOCKS, 8, 3)),
            dma((2, 4, 3)),
        ],
        compiler_params=pltpu.CompilerParams(
            vmem_limit_bytes=48 * 2**20, collective_id=1, has_side_effects=True
        ),
        cost_estimate=pl.CostEstimate(
            flops=4 * 10**9, bytes_accessed=8 * 2**20, transcendentals=10**6
        ),
        name="back",
    )(tgrad, slots, idrow, iterm, uvec, table, first, second)


def body(
    table, tower_first, tower_second, w_input, w_output, norm_gain, head_vec, time_bias,
    look_owner, look_row, event_time, labels,
):
    tok, slots, idrow = front(
        look_owner.reshape(1, LOOK), look_row, table, tower_first, tower_second
    )
    tgrad, iterm, uvec, loss = hstu(
        tok, w_input, w_output, norm_gain, head_vec, time_bias, event_time, labels
    )
    table_grad, sums, usum = back(
        tgrad, slots, idrow, iterm, uvec, table, tower_first, tower_second
    )
    sums = sums.astype(F32)
    input_grad = jnp.concatenate([sums[b] for b in range(4)], axis=1)
    output_grad = usum[0][:, None] * head_vec[None, :]
    return (table_grad, sums[4], sums[5], input_grad, output_grad, loss[0, :1])


def solution(mesh):
    return jax.shard_map(
        body,
        mesh=mesh,
        in_specs=(
            P(("user", "item"), None), P(), P(), P(), P(), P(), P(), P(),
            P(("user", "item"), None, None), P(("user", "item"), None),
            P(("user", "item"), None), P(("user", "item"), None),
        ),
        out_specs=(P(("user", "item"), None), P(), P(), P(), P(), P(("user", "item"))),
        check_vma=False,
    )
```

```python
import math

import jax
import jax.numpy as jnp
from jax import lax
from jax.experimental import pallas as pl
from jax.experimental.pallas import tpu as pltpu
from jax.sharding import PartitionSpec as P

D = 512
HEADS = 4
HD = 128
HIST = 512
LOOK = 768
BUCKETS = 16
EPS = 1e-06
F32 = jnp.float32
BF16 = jnp.bfloat16
RB = 128
OWNERS = 128
SLOT = 16
USED = 12
PACK = 384
ROWS = OWNERS * SLOT
TILE = 512
STEP = 37
UNSTEP = 45
NEG = -1e30


def nn(a, b):
    return lax.dot_general(a, b, (((1,), (0,)), ((), ())), preferred_element_type=F32)


def nt(a, b):
    return lax.dot_general(a, b, (((1,), (1,)), ((), ())), preferred_element_type=F32)


def sigmoid(x):
    return 0.5 + 0.5 * jnp.tanh(0.5 * x)


def column(row):
    return jnp.broadcast_to(row.astype(F32), (128, row.shape[1])).T


def keys_of(start):
    return min(HIST, start + RB)


def place():
    return lax.axis_index("user"), lax.axis_index("item")


def device(index):
    return (index // 16, index % 16)


def greet(me):
    barrier = pltpu.get_barrier_semaphore()

    @pl.loop(1, OWNERS)
    def _(k):
        pl.semaphore_signal(
            barrier, inc=1, device_id=device((me + k) % OWNERS), device_id_type=pl.DeviceIdType.MESH
        )


def meet():
    pl.semaphore_wait(pltpu.get_barrier_semaphore(), OWNERS - 1)


def row_in_slot(n):
    return lax.broadcasted_iota(jnp.int32, (n, 128), 0) % SLOT


def pack(y):
    r = row_in_slot(y.shape[0])
    last = y[:, PACK:D]
    out = [
        jnp.where(r >= USED, pltpu.roll(last, USED - 4 * b, 0), y[:, 128 * b : 128 * (b + 1)])
        for b in range(3)
    ]
    return jnp.concatenate(out, axis=1).astype(BF16)


def unpack_last(y):
    n = y.shape[0]
    r = row_in_slot(n)
    p = [pltpu.roll(y[:, 128 * b : 128 * (b + 1)].astype(F32), n - USED + 4 * b, 0) for b in range(3)]
    return jnp.where(r < 4, p[0], jnp.where(r < 8, p[1], p[2])).astype(BF16)


def chunk(ref, k):
    return ref.at[pl.ds(pl.multiple_of(k * SLOT, SLOT), SLOT), :]


def send_chunk(send, recv, k, target, send_sem, recv_sem):
    pltpu.make_async_remote_copy(
        src_ref=chunk(send, k),
        dst_ref=chunk(recv, k),
        send_sem=send_sem,
        recv_sem=recv_sem,
        device_id=device(target),
        device_id_type=pl.DeviceIdType.MESH,
    ).start()


def wait_bytes(ref, sem):
    pltpu.make_async_copy(ref, ref, sem).wait()


def silu_parts(p):
    sg = sigmoid(p)
    y = p * sg
    return y, sg + y * (1.0 - sg)


GROUPS = 3
ORDER = ("xyz", "yzx", "zxy")


def step_kernel(
    owner_ref, row_ref, stamp_row_ref, label_ref, gain_ref, head_ref, tb_ref,
    table_hbm, first_hbm, second_hbm, w1_hbm, w2_hbm,
    tablegrad_ref, sums_ref, usum_ref, loss_ref,
    table_ref, first_ref, second_ref, w1_ref, w2_ref,
    ids_send, ids_recv, idq, idrow, send, recv, back_recv, last, rows_held, hidden, slope, tok_ref,
    normed, proj, dsl, idx, wts, dwt, att, dp, de, dpre,
    terms, core_in, half, in1, part1, in2, u_held, u_in,
    load_sems, sems, send_sems, recv_sems, u_sems,
):
    user, item = place()
    me = user * 16 + item
    loads = [
        pltpu.make_async_copy(src, dst, load_sems.at[n])
        for n, (src, dst) in enumerate(
            ((table_hbm, table_ref), (first_hbm, first_ref), (w1_hbm, w1_ref), (w2_hbm, w2_ref), (second_hbm, second_ref))
        )
    ]
    for load in loads:
        load.start()

    def arrive(n):
        loads[n].wait()

    greet(me)
    j_row = (UNSTEP * (owner_ref[...] - me + OWNERS)) % OWNERS
    named = lax.broadcasted_iota(jnp.int32, (OWNERS, LOOK), 0) == j_row
    named_b = named.astype(F32).astype(BF16)
    before = lax.broadcasted_iota(jnp.int32, (LOOK, LOOK), 0) < lax.broadcasted_iota(
        jnp.int32, (LOOK, LOOK), 1
    )
    earlier = nn(named_b, before.astype(F32).astype(BF16))
    rank = jnp.sum(jnp.where(named, earlier, 0.0), axis=0, keepdims=True)
    slots = j_row * SLOT + rank.astype(jnp.int32)
    lanes = lax.broadcasted_iota(jnp.int32, (LOOK, 128), 1).astype(F32)
    listed = jnp.where(column(rank) == lanes, column(row_ref[...]) - 256.0, 0.0)
    ids_send[:, 0, :] = nn(named_b, listed.astype(BF16))
    ids_recv[0] = ids_send[0]
    meet()

    @pl.loop(1, OWNERS)
    def _(k):
        pltpu.make_async_remote_copy(
            src_ref=ids_send.at[k],
            dst_ref=ids_recv.at[k],
            send_sem=sems.at[0],
            recv_sem=sems.at[1],
            device_id=device((me + STEP * k) % OWNERS),
            device_id_type=pl.DeviceIdType.MESH,
        ).start()

    slot_col = column(slots)
    others = pl.ds(1, OWNERS - 1)
    later = pl.ds(SLOT, ROWS - SLOT)
    arrive(0)
    wait_bytes(ids_recv.at[others], sems.at[1])
    wait_bytes(ids_send.at[others], sems.at[0])
    ids = ids_recv[:, 0, :].astype(BF16)

    @pl.loop(0, ROWS // TILE)
    def _(t):
        base = t * TILE
        rows = pl.ds(pl.multiple_of(base, TILE), TILE)
        at = base + lax.broadcasted_iota(jnp.int32, (TILE, 128), 0)
        lane = lax.broadcasted_iota(jnp.int32, (TILE, 128), 1)
        spread = nn((at // SLOT == lane).astype(F32).astype(BF16), ids)
        r = at % SLOT
        mine = jnp.sum(jnp.where(r == lane, spread + 256.0, 0.0), axis=1, keepdims=True)
        mine = jnp.where(r < USED, mine, -1.0)
        idq[rows, :] = mine
        cols = lane.astype(F32)
        pick = jnp.concatenate(
            [(mine == cols + 128.0 * b).astype(F32).astype(BF16) for b in range(4)], axis=1
        )
        send[rows, :] = pack(nn(pick, table_ref[...]))

        @pl.loop(0, TILE // SLOT)
        def _(i):
            k = t * (TILE // SLOT) + i

            @pl.when(k > 0)
            def _():
                target = (me - (STEP * k) % OWNERS + OWNERS) % OWNERS
                send_chunk(send, recv, k, target, sems.at[2], sems.at[3])

    recv[0:SLOT, :] = send[0:SLOT, :]
    idrow[...] = idq[...].T[0:8, :]
    arrive(1)
    arrive(4)
    wait_bytes(recv.at[later], sems.at[3])
    for s in range(0, ROWS, 256):
        rows = pl.ds(s, 256)
        last[rows, :] = unpack_last(recv[rows, :])
    for s in range(0, LOOK, RB):
        rows = pl.ds(s, RB)
        mark = slot_col[s : s + RB, :]
        cols = lax.broadcasted_iota(jnp.int32, (RB, 128), 1).astype(F32)
        pick = jnp.concatenate(
            [(mark == cols + float(b)).astype(F32).astype(BF16) for b in range(0, ROWS, 128)],
            axis=1,
        )
        rows_held[rows, 0:PACK] = nn(pick, recv[...]).astype(BF16)
        rows_held[rows, PACK:D] = nn(pick, last[...]).astype(BF16)
    for s in range(0, LOOK, 256):
        rows = pl.ds(s, 256)
        held = rows_held[rows, :]
        hid, dh = silu_parts(nn(held, first_ref[...]))
        hid = hid.astype(BF16)
        hidden[rows, :] = hid
        slope[rows, :] = dh
        tok_ref[rows, :] = (held.astype(F32) + nn(hid, second_ref[...])).astype(BF16)
    wait_bytes(send.at[later], sems.at[2])
    gain = gain_ref[...]
    head = head_ref[...]
    scale = 1.0 / math.sqrt(HD)
    arrive(2)
    for s in range(0, LOOK, RB):
        rows = pl.ds(s, RB)
        t = tok_ref[rows, :].astype(F32)
        r = lax.rsqrt(jnp.mean(t * t, axis=1, keepdims=True) + EPS)
        normed[rows, :] = (t * r * gain).astype(BF16)
    for c in range(0, 4 * D, 256):
        cols = pl.ds(c, 256)
        for s in range(0, LOOK, RB):
            rows = pl.ds(s, RB)
            p = nn(normed[rows, :], w1_ref[:, cols])
            sg = sigmoid(p)
            y = p * sg
            proj[rows, cols] = y.astype(BF16)
            dsl[rows, cols] = (sg + y * (1.0 - sg)).astype(BF16)
    lane = lax.broadcasted_iota(jnp.int32, (HEADS, 128), 1)
    tab = jnp.zeros((HEADS, 128), F32)
    for k in range(BUCKETS):
        tab = tab + jnp.where(lane <= 31 - k, tb_ref[:, k : k + 1], 0.0)
    tab = jnp.where(lane == 33, NEG, tab)
    stamp_col = column(stamp_row_ref[...]).astype(jnp.int32)
    for s in range(0, LOOK, RB):
        rows = pl.ds(s, RB)
        ke = keys_of(s)
        now = jnp.concatenate([stamp_col[s : s + RB, :]] * (ke // 128), axis=1)
        gap = now - stamp_row_ref[:, 0:ke]
        lz = lax.clz(gap + 1)
        if s < HIST:
            i_pos = s + lax.broadcasted_iota(jnp.int32, (RB, ke), 0)
            j_pos = lax.broadcasted_iota(jnp.int32, (RB, ke), 1)
            lz = jnp.where(j_pos <= i_pos, lz, 33)
        idx[rows, 0:ke] = lz
    for h in range(HEADS):
        hc = h * HD
        tab_h = jnp.broadcast_to(tab[h : h + 1, :], (RB, 128))
        for s in range(0, LOOK, RB):
            rows = pl.ds(s, RB)
            ke = keys_of(s)
            q = proj[rows, pl.ds(2 * D + hc, HD)]
            sc = nt(q, proj[0:ke, pl.ds(3 * D + hc, HD)]) * scale
            tt = [
                jnp.take_along_axis(tab_h, idx[rows, j : j + 128], axis=1)
                for j in range(0, ke, 128)
            ]
            sc = sc + jnp.concatenate(tt, axis=1)
            sg = sigmoid(sc)
            y = sc * sg
            w = (y * (1.0 / HIST)).astype(BF16)
            wts[h, rows, 0:ke] = w
            dwt[h, rows, 0:ke] = ((sg + y * (1.0 - sg)) * (1.0 / HIST)).astype(BF16)
            if ke < HIST:
                wts[h, rows, ke:HIST] = jnp.zeros((RB, HIST - ke), BF16)
            att[rows, pl.ds(hc, HD)] = nn(w, proj[0:ke, pl.ds(D + hc, HD)])
    own = {}
    for h in range(HEADS):
        hc = h * HD
        for s in range(HIST, LOOK, RB):
            rows = pl.ds(s, RB)
            q = proj[rows, pl.ds(2 * D + hc, HD)].astype(F32)
            k = proj[rows, pl.ds(3 * D + hc, HD)].astype(F32)
            v = proj[rows, pl.ds(D + hc, HD)].astype(F32)
            os = jnp.sum(q * k, axis=1, keepdims=True) * scale + tb_ref[h : h + 1, 0:1]
            sg = sigmoid(os)
            y = os * sg
            ow = (y * (1.0 / HIST)).astype(BF16).astype(F32)
            own[h, s] = (ow, (sg + y * (1.0 - sg)) * (1.0 / HIST))
            att[rows, pl.ds(hc, HD)] += ow * v
    h_hi = head.astype(BF16)
    h_mid = (head - h_hi.astype(F32)).astype(BF16)
    h_lo = (head - h_hi.astype(F32) - h_mid.astype(F32)).astype(BF16)
    parts = jnp.concatenate([h_hi, h_mid, h_lo, jnp.zeros((13, D), BF16)], axis=0)
    arrive(3)
    hw = jnp.sum(nt(parts, w2_ref[...]), axis=0, keepdims=True)
    label_col = column(label_ref[...])
    loss = jnp.zeros((1, 1), F32)
    uvec = jnp.zeros((1, D), F32)
    dlogit = {}
    for s in range(0, LOOK, RB):
        rows = pl.ds(s, RB)
        a = att[rows, :]
        cen = a - jnp.mean(a, axis=1, keepdims=True)
        spread = lax.rsqrt(jnp.mean(cen * cen, axis=1, keepdims=True) + EPS)
        n = cen * spread
        g = proj[rows, 0:D].astype(F32)
        mixed = (n * g).astype(BF16).astype(F32)
        t = tok_ref[rows, :].astype(F32)
        logit = jnp.sum(t * head + mixed * hw, axis=1, keepdims=True)
        lab = label_col[s : s + RB, 0:1]
        soft = jnp.maximum(logit, 0.0) + jnp.log1p(jnp.exp(-jnp.abs(logit)))
        loss = loss + jnp.sum(soft - lab * logit, axis=0, keepdims=True)
        dl = (jax.nn.sigmoid(logit) - lab) * (1.0 / LOOK)
        dlogit[s] = dl
        uvec = uvec + jnp.sum(mixed * dl, axis=0, keepdims=True)
        dm = (dl * hw).astype(BF16).astype(F32)
        dg = dm * n
        dp[rows, 0:D] = (dg * dsl[rows, 0:D].astype(F32)).astype(BF16)
        dn = dm * g
        da = spread * (
            dn - jnp.mean(dn, axis=1, keepdims=True) - n * jnp.mean(dn * n, axis=1, keepdims=True)
        )
        att[rows, :] = da
    u_held[0] = uvec
    loss_ref[...] = jnp.broadcast_to(loss * (1.0 / LOOK), loss_ref.shape)
    for h in range(HEADS):
        hc = h * HD
        for s in range(0, LOOK, RB):
            rows = pl.ds(s, RB)
            ke = keys_of(s)
            da = att[rows, pl.ds(hc, HD)]
            dw = nt(da.astype(BF16), proj[0:ke, pl.ds(D + hc, HD)])
            ds = (dw * dwt[h, rows, 0:ke].astype(F32) * scale).astype(BF16)
            dwt[h, rows, 0:ke] = ds
            if ke < HIST:
                dwt[h, rows, ke:HIST] = jnp.zeros((RB, HIST - ke), BF16)
            dq = nn(ds, proj[0:ke, pl.ds(3 * D + hc, HD)])
            if s >= HIST:
                q = proj[rows, pl.ds(2 * D + hc, HD)].astype(F32)
                k = proj[rows, pl.ds(3 * D + hc, HD)].astype(F32)
                v = proj[rows, pl.ds(D + hc, HD)].astype(F32)
                ow, osl = own[h, s]
                dos = jnp.sum(da * v, axis=1, keepdims=True) * osl * scale
                dq = dq + dos * k
                dcol = pl.ds(D + hc, HD)
                dp[rows, dcol] = (ow * da * dsl[rows, dcol].astype(F32)).astype(BF16)
                dcol = pl.ds(3 * D + hc, HD)
                dp[rows, dcol] = (dos * q * dsl[rows, dcol].astype(F32)).astype(BF16)
            dcol = pl.ds(2 * D + hc, HD)
            dp[rows, dcol] = (dq * dsl[rows, dcol].astype(F32)).astype(BF16)
        hist = pl.ds(0, HIST)
        dat = att[:, pl.ds(hc, HD)].T.astype(BF16)
        dcol = pl.ds(D + hc, HD)
        dp[hist, dcol] = (nn(dat, wts[h]).T * dsl[hist, dcol].astype(F32)).astype(BF16)
        qt = proj[:, pl.ds(2 * D + hc, HD)].astype(F32).T.astype(BF16)
        dcol = pl.ds(3 * D + hc, HD)
        dp[hist, dcol] = (nn(qt, dwt[h]).T * dsl[hist, dcol].astype(F32)).astype(BF16)
    z, core = user // 2, user % 2
    x, y = item // 4, item % 4
    own = {"x": x, "y": y, "z": z}

    def peer(**to):
        c = {**own, **to}
        return (c["z"] * 2 + to.get("core", core), c["x"] * 4 + c["y"])

    def copy(src, dst, to, send_sem, recv_sem):
        return pltpu.make_async_remote_copy(
            src_ref=src, dst_ref=dst, send_sem=send_sem, recv_sem=recv_sem,
            device_id=to, device_id_type=pl.DeviceIdType.MESH,
        )

    def at(n, size):
        return pl.ds(pl.multiple_of(n * size, size), size)

    def quarter(q):
        return at(q // 4, 16), at(q % 4, 128)

    def group(g):
        return pl.ds(2 * g, 2)

    def square(g):
        a0, a1, a2 = (own[a] for a in ORDER[g])
        rows = pl.ds(pl.multiple_of(core * 256 + a0 * 64 + a1 * 16, 16), 16)
        return (group(g), rows, at(a2, 128))

    def copies(g, stage):
        axis, plane = ORDER[g][0], ORDER[g][1:]
        a0 = own[axis]
        q = own[plane[0]] * 4 + own[plane[1]]
        todo = []
        if stage == 0:
            todo.append((terms.at[group(g), at(1 - core, 256), :], core_in.at[group(g)], peer(core=1 - core)))
        elif stage == 5:
            place_of = sums_ref.at[group(g), at(core, 256), :]
            todo.append((place_of, place_of, peer(core=1 - core)))
        elif stage in (1, 4):
            for d in (1, 2, 3):
                to = (a0 + d) % 4
                if stage == 1:
                    src, dst = half.at[group(g), at(to, 64), :], in1.at[g, d - 1]
                else:
                    src = dst = sums_ref.at[group(g), at(core * 4 + a0, 64), :]
                todo.append((src, dst, peer(**{axis: to})))
        else:
            for e in range(1, 16):
                to = (q + e) % 16
                if stage == 2:
                    r, c = quarter(to)
                    src, dst = part1.at[group(g), r, c], in2.at[g, e - 1]
                else:
                    src = dst = sums_ref.at[square(g)]
                todo.append((src, dst, peer(**{plane[0]: to // 4, plane[1]: to % 4})))
        return [
            copy(src, dst, to, send_sems.at[g, stage, n], recv_sems.at[g, stage, n])
            for n, (src, dst, to) in enumerate(todo)
        ]

    def start(g, stage):
        for c in copies(g, stage):
            c.start()

    def finish(g, stage):
        for c in copies(g, stage):
            c.wait_recv()
        a0, a1, a2 = (own[a] for a in ORDER[g])
        if stage == 0:
            for b in (2 * g, 2 * g + 1):
                half[b] = (terms[b, at(core, 256), :].astype(F32) + core_in[b].astype(F32)).astype(BF16)
        elif stage == 1:
            total = half[group(g), at(a0, 64), :].astype(F32)
            for d in range(3):
                total = total + in1[g, d].astype(F32)
            part1[group(g)] = total.astype(BF16)
        elif stage == 2:
            total = part1[group(g), at(a1, 16), at(a2, 128)].astype(F32)
            for e in range(15):
                total = total + in2[g, e].astype(F32)
            sums_ref[square(g)] = total.astype(BF16)

    def u_copies(stage):
        if stage == 0:
            peers = [peer(core=1 - core)]
        else:
            a = "xyz"[stage - 1]
            peers = [peer(**{a: (own[a] + d) % 4}) for d in (1, 2, 3)]
        return [
            copy(u_held.at[stage], u_in.at[stage, n], to, u_sems.at[0, stage, n], u_sems.at[1, stage, n])
            for n, to in enumerate(peers)
        ]

    def u_start(stage):
        for c in u_copies(stage):
            c.start()

    def u_finish(stage):
        total = u_held[stage]
        for n, c in enumerate(u_copies(stage)):
            c.wait_recv()
            total = total + u_in[stage, n]
        if stage < 3:
            u_held[stage + 1] = total
        else:
            usum_ref[...] = total

    u_start(0)
    nrt = normed[...].astype(F32).T.astype(BF16)
    for b in range(4):
        for c in range(0, D, 256):
            terms[b, :, pl.ds(c, 256)] = nn(nrt, dp[:, pl.ds(b * D + c, 256)]).astype(BF16)
        if b % 2:
            start(b // 2, 0)
    for s in range(0, LOOK, RB):
        rows = pl.ds(s, RB)
        dnorm = nt(dp[rows, :], w1_ref[...])
        t = tok_ref[rows, :].astype(F32)
        r = lax.rsqrt(jnp.mean(t * t, axis=1, keepdims=True) + EPS)
        tn = dnorm * gain
        tg = dlogit[s] * head + r * tn - t * (r * r * r * jnp.mean(tn * t, axis=1, keepdims=True))
        tgb = tg.astype(BF16)
        de[rows, :] = tgb
        dpr = (nt(tgb, second_ref[...]) * slope[rows, :]).astype(BF16)
        dpre[rows, :] = dpr
        att[rows, :] = tg + nt(dpr, first_ref[...])
    for g in (0, 1):
        finish(g, 0)
        start(g, 1)
    u_finish(0)
    u_start(1)
    row_grad = att[...].astype(BF16)

    @pl.loop(0, ROWS // TILE)
    def _(t):
        base = t * TILE
        rows = pl.ds(pl.multiple_of(base, TILE), TILE)
        pick = base + lax.broadcasted_iota(jnp.int32, (TILE, LOOK), 0) == slots
        send[rows, :] = pack(nn(pick.astype(F32).astype(BF16), row_grad))

        @pl.loop(0, TILE // SLOT)
        def _(i):
            k = t * (TILE // SLOT) + i

            @pl.when(k > 0)
            def _():
                send_chunk(send, back_recv, k, (me + STEP * k) % OWNERS, sems.at[4], sems.at[5])

    back_recv[0:SLOT, :] = send[0:SLOT, :]
    terms[5] = nn(hidden[...].astype(F32).T.astype(BF16), de[...]).astype(BF16)
    terms[4] = nn(rows_held[...].astype(F32).T.astype(BF16), dpre[...]).astype(BF16)
    start(2, 0)
    for g in (0, 1):
        finish(g, 1)
        start(g, 2)
    u_finish(1)
    u_start(2)
    finish(2, 0)
    start(2, 1)
    for g in (0, 1):
        finish(g, 2)
        start(g, 3)
    u_finish(2)
    u_start(3)
    finish(2, 1)
    start(2, 2)
    for g in (0, 1):
        finish(g, 3)
        start(g, 4)
    finish(2, 2)
    start(2, 3)
    u_finish(3)
    wait_bytes(back_recv.at[later], sems.at[5])
    for s in range(0, ROWS, 256):
        rows = pl.ds(s, 256)
        last[rows, :] = unpack_last(back_recv[rows, :])
    for s in range(0, D, 128):
        rows = pl.ds(s, 128)
        sub = (s + lax.broadcasted_iota(jnp.int32, (128, 128), 0)).astype(F32)
        pick = jnp.concatenate(
            [
                (sub == idrow[0:1, q : q + 128]).astype(F32).astype(BF16)
                for q in range(0, ROWS, 128)
            ],
            axis=1,
        )
        tablegrad_ref[rows, 0:PACK] = nn(pick, back_recv[...])
        tablegrad_ref[rows, PACK:D] = nn(pick, last[...])
    finish(2, 3)
    start(2, 4)
    for g in (0, 1):
        finish(g, 4)
        start(g, 5)
    finish(2, 4)
    start(2, 5)
    for g in range(GROUPS):
        finish(g, 5)
    wait_bytes(send.at[later], sems.at[4])
    for stage in range(4):
        for c in u_copies(stage):
            c.wait_send()
    for g in range(GROUPS):
        for stage in range(6):
            for c in copies(g, stage):
                c.wait_send()


VM = pl.BlockSpec(memory_space=pltpu.VMEM)
ANY = pl.BlockSpec(memory_space=pl.ANY)


def train_step(*args):
    dma = pltpu.SemaphoreType.DMA
    return pl.pallas_call(
        step_kernel,
        out_shape=(
            jax.ShapeDtypeStruct((D, D), F32),
            jax.ShapeDtypeStruct((2 * GROUPS, D, D), BF16),
            jax.ShapeDtypeStruct((1, D), F32),
            jax.ShapeDtypeStruct((1, 128), F32),
        ),
        in_specs=[VM] * 7 + [ANY] * 5,
        out_specs=(VM,) * 4,
        scratch_shapes=[
            pltpu.VMEM((D, D), BF16),
            pltpu.VMEM((D, D), BF16),
            pltpu.VMEM((D, D), BF16),
            pltpu.VMEM((D, 4 * D), BF16),
            pltpu.VMEM((D, D), BF16),
            pltpu.VMEM((OWNERS, 1, 128), F32),
            pltpu.VMEM((OWNERS, 1, 128), F32),
            pltpu.VMEM((ROWS, 128), F32),
            pltpu.VMEM((8, ROWS), F32),
            pltpu.VMEM((ROWS, PACK), BF16),
            pltpu.VMEM((ROWS, PACK), BF16),
            pltpu.VMEM((ROWS, PACK), BF16),
            pltpu.VMEM((ROWS, 128), BF16),
            pltpu.VMEM((LOOK, D), BF16),
            pltpu.VMEM((LOOK, D), BF16),
            pltpu.VMEM((LOOK, D), F32),
            pltpu.VMEM((LOOK, D), BF16),
            pltpu.VMEM((LOOK, D), BF16),
            pltpu.VMEM((LOOK, 4 * D), BF16),
            pltpu.VMEM((LOOK, 4 * D), BF16),
            pltpu.VMEM((LOOK, HIST), jnp.int32),
            pltpu.VMEM((HEADS, LOOK, HIST), BF16),
            pltpu.VMEM((HEADS, LOOK, HIST), BF16),
            pltpu.VMEM((LOOK, D), F32),
            pltpu.VMEM((LOOK, 4 * D), BF16),
            pltpu.VMEM((LOOK, D), BF16),
            pltpu.VMEM((LOOK, D), BF16),
            pltpu.VMEM((2 * GROUPS, D, D), BF16),
            pltpu.VMEM((2 * GROUPS, 256, D), BF16),
            pltpu.VMEM((2 * GROUPS, 256, D), BF16),
            pltpu.VMEM((GROUPS, 3, 2, 64, D), BF16),
            pltpu.VMEM((2 * GROUPS, 64, D), BF16),
            pltpu.VMEM((GROUPS, 15, 2, 16, 128), BF16),
            pltpu.VMEM((4, 1, D), F32),
            pltpu.VMEM((4, 3, 1, D), F32),
            dma((5,)),
            dma((6,)),
            dma((GROUPS, 6, 15)),
            dma((GROUPS, 6, 15)),
            dma((2, 4, 3)),
        ],
        compiler_params=pltpu.CompilerParams(
            vmem_limit_bytes=60 * 2**20, collective_id=0, has_side_effects=True
        ),
        cost_estimate=pl.CostEstimate(
            flops=14 * 10**9, bytes_accessed=10 * 2**20, transcendentals=5 * 10**6
        ),
        name="step",
    )(*args)


def finish_kernel(tablegrad_ref, sums_ref, usum_ref, head_ref, table_ref, first_ref, second_ref, input_ref, output_ref):
    table_ref[...] = tablegrad_ref[...]
    first_ref[...] = sums_ref[4].astype(F32)
    second_ref[...] = sums_ref[5].astype(F32)
    for b in range(4):
        input_ref[:, pl.ds(b * D, D)] = sums_ref[b].astype(F32)
    output_ref[...] = column(usum_ref[...])[:, 0:1] * head_ref[...]


def outputs(tablegrad, sums, usum, head):
    n = 128

    def rows(width):
        return pl.BlockSpec((n, width), lambda i: (i, 0))

    def shape(width):
        return jax.ShapeDtypeStruct((D, width), F32)

    return pl.pallas_call(
        finish_kernel,
        grid=(D // n,),
        out_shape=(shape(D), shape(D), shape(D), shape(4 * D), shape(D)),
        in_specs=[
            rows(D),
            pl.BlockSpec((2 * GROUPS, n, D), lambda i: (0, i, 0)),
            pl.BlockSpec((1, n), lambda i: (0, i)),
            pl.BlockSpec((1, D), lambda i: (0, 0)),
        ],
        out_specs=(rows(D), rows(D), rows(D), rows(4 * D), rows(D)),
        compiler_params=pltpu.CompilerParams(vmem_limit_bytes=60 * 2**20),
        name="outputs",
    )(tablegrad, sums, usum, head)


def body(
    table, tower_first, tower_second, w_input, w_output, norm_gain, head_vec, time_bias,
    look_owner, look_row, event_time, labels,
):
    head = head_vec.reshape(1, D)
    tablegrad, sums, usum, loss = train_step(
        look_owner.reshape(1, LOOK), look_row, event_time, labels, norm_gain.reshape(1, D), head,
        time_bias, table, tower_first, tower_second, w_input, w_output,
    )
    table_grad, first_grad, second_grad, input_grad, output_grad = outputs(tablegrad, sums, usum, head)
    return (table_grad, first_grad, second_grad, input_grad, output_grad, loss[0, :1])


def solution(mesh):
    return jax.shard_map(
        body,
        mesh=mesh,
        in_specs=(
            P(("user", "item"), None), P(), P(), P(), P(), P(), P(), P(),
            P(("user", "item"), None, None), P(("user", "item"), None),
            P(("user", "item"), None), P(("user", "item"), None),
        ),
        out_specs=(P(("user", "item"), None), P(), P(), P(), P(), P(("user", "item"))),
        check_vma=False,
    )
```

```python
import math

import jax
import jax.numpy as jnp
from jax import lax
from jax.experimental import pallas as pl
from jax.experimental.pallas import tpu as pltpu
from jax.sharding import PartitionSpec as P

D = 512
HEADS = 4
HD = 128
HIST = 512
LOOK = 768
BUCKETS = 16
EPS = 1e-06
F32 = jnp.float32
BF16 = jnp.bfloat16
RB = 128
OWNERS = 128
SLOT = 16
USED = 12
PACK = 384
ROWS = OWNERS * SLOT
TILE = 512
STEP = 37
UNSTEP = 45
NEG = -1e30


def nn(a, b):
    return lax.dot_general(a, b, (((1,), (0,)), ((), ())), preferred_element_type=F32)


def nt(a, b):
    return lax.dot_general(a, b, (((1,), (1,)), ((), ())), preferred_element_type=F32)


def sigmoid(x):
    return 0.5 + 0.5 * jnp.tanh(0.5 * x)


def column(row):
    return jnp.broadcast_to(row.astype(F32), (128, row.shape[1])).T


def keys_of(start):
    return min(HIST, start + RB)


def place():
    return lax.axis_index("user"), lax.axis_index("item")


def device(index):
    return (index // 16, index % 16)


def greet():
    barrier = pltpu.get_barrier_semaphore()

    user, item = place()

    def hail(du, di):
        to = ((user + du) % 8, (item + di) % 16)
        pl.semaphore_signal(barrier, inc=1, device_id=to, device_id_type=pl.DeviceIdType.MESH)

    for di in range(1, 16):
        hail(0, di)
    for di in range(16):

        @pl.loop(1, 8)
        def _(du):
            hail(du, di)


def meet():
    pl.semaphore_wait(pltpu.get_barrier_semaphore(), OWNERS - 1)


def row_in_slot(n):
    return lax.broadcasted_iota(jnp.int32, (n, 128), 0) % SLOT


def pack(y):
    r = row_in_slot(y.shape[0])
    last = y[:, PACK:D]
    out = [
        jnp.where(r >= USED, pltpu.roll(last, USED - 4 * b, 0), y[:, 128 * b : 128 * (b + 1)])
        for b in range(3)
    ]
    return jnp.concatenate(out, axis=1).astype(BF16)


def unpack_last(y):
    n = y.shape[0]
    r = row_in_slot(n)
    p = [pltpu.roll(y[:, 128 * b : 128 * (b + 1)].astype(F32), n - USED + 4 * b, 0) for b in range(3)]
    return jnp.where(r < 4, p[0], jnp.where(r < 8, p[1], p[2])).astype(BF16)


def chunk(ref, k):
    return ref.at[pl.ds(pl.multiple_of(k * SLOT, SLOT), SLOT), :]


def send_chunk(send, recv, k, target, send_sem, recv_sem):
    pltpu.make_async_remote_copy(
        src_ref=chunk(send, k),
        dst_ref=chunk(recv, k),
        send_sem=send_sem,
        recv_sem=recv_sem,
        device_id=device(target),
        device_id_type=pl.DeviceIdType.MESH,
    ).start()


def wait_bytes(ref, sem):
    pltpu.make_async_copy(ref, ref, sem).wait()


def silu_parts(p):
    sg = sigmoid(p)
    y = p * sg
    return y, sg + y * (1.0 - sg)


GROUPS = 3
ORDER = ("xyz", "yzx", "zxy")


def step_kernel(
    owner_ref, row_ref, stamp_row_ref, label_ref, gain_ref, head_ref, tb_ref,
    table_hbm, first_hbm, second_hbm, w1_hbm, w2_hbm,
    tablegrad_hbm, sums_hbm, usum_ref, loss_ref,
    sums_ref, table_ref, first_ref, second_ref, w1_ref, w2_ref,
    ids_send, ids_recv, idq, idrow, send, recv, back_recv, last, rows_held, hidden, slope, tok_ref,
    normed, proj, dsl, idx, wts, dwt, att, dp, de, dpre,
    terms, core_in, half, in1, part1, in2, u_held, u_in,
    load_sems, out_sems, sems, send_sems, recv_sems, u_sems,
):
    user, item = place()
    me = user * 16 + item
    loads = [
        pltpu.make_async_copy(src, dst, load_sems.at[n])
        for n, (src, dst) in enumerate(
            ((table_hbm, table_ref), (first_hbm, first_ref), (w1_hbm, w1_ref), (w2_hbm, w2_ref), (second_hbm, second_ref))
        )
    ]
    for load in loads:
        load.start()

    def arrive(n):
        loads[n].wait()

    greet()
    j_row = (UNSTEP * (owner_ref[...] - me + OWNERS)) % OWNERS
    named = lax.broadcasted_iota(jnp.int32, (OWNERS, LOOK), 0) == j_row
    named_b = named.astype(F32).astype(BF16)
    before = lax.broadcasted_iota(jnp.int32, (LOOK, LOOK), 0) < lax.broadcasted_iota(
        jnp.int32, (LOOK, LOOK), 1
    )
    earlier = nn(named_b, before.astype(F32).astype(BF16))
    rank = jnp.sum(jnp.where(named, earlier, 0.0), axis=0, keepdims=True)
    slots = j_row * SLOT + rank.astype(jnp.int32)
    lanes = lax.broadcasted_iota(jnp.int32, (LOOK, 128), 1).astype(F32)
    listed = jnp.where(column(rank) == lanes, column(row_ref[...]) - 256.0, 0.0)
    ids_send[:, 0, :] = nn(named_b, listed.astype(BF16))
    ids_recv[0] = ids_send[0]
    meet()

    @pl.loop(1, OWNERS)
    def _(k):
        pltpu.make_async_remote_copy(
            src_ref=ids_send.at[k],
            dst_ref=ids_recv.at[k],
            send_sem=sems.at[0],
            recv_sem=sems.at[1],
            device_id=device((me + STEP * k) % OWNERS),
            device_id_type=pl.DeviceIdType.MESH,
        ).start()

    slot_col = column(slots)
    others = pl.ds(1, OWNERS - 1)
    later = pl.ds(SLOT, ROWS - SLOT)
    arrive(0)
    wait_bytes(ids_recv.at[others], sems.at[1])
    wait_bytes(ids_send.at[others], sems.at[0])
    ids = ids_recv[:, 0, :].astype(BF16)

    def fresh(t):
        return max(1, t * (TILE // SLOT)), (t + 1) * (TILE // SLOT)

    for t in range(ROWS // TILE):
        base = t * TILE
        rows = pl.ds(base, TILE)
        slot_at = base + lax.broadcasted_iota(jnp.int32, (TILE, 128), 0)
        lane = lax.broadcasted_iota(jnp.int32, (TILE, 128), 1)
        spread = nn((slot_at // SLOT == lane).astype(F32).astype(BF16), ids)
        r = slot_at % SLOT
        mine = jnp.sum(jnp.where(r == lane, spread + 256.0, 0.0), axis=1, keepdims=True)
        mine = jnp.where(r < USED, mine, -1.0)
        idq[rows, :] = mine
        cols = lane.astype(F32)
        pick = jnp.concatenate(
            [(mine == cols + 128.0 * b).astype(F32).astype(BF16) for b in range(4)], axis=1
        )
        send[rows, :] = pack(nn(pick, table_ref[...]))

        @pl.loop(*fresh(t))
        def _(k):
            target = (me - (STEP * k) % OWNERS + OWNERS) % OWNERS
            send_chunk(send, recv, k, target, sems.at[2], sems.at[3])

    recv[0:SLOT, :] = send[0:SLOT, :]
    idrow[...] = idq[...].T[0:8, :]
    for s in range(0, LOOK, RB):
        mark = slot_col[s : s + RB, :]
        cols = lax.broadcasted_iota(jnp.int32, (RB, 128), 1).astype(F32)
        for b in range(0, ROWS, 128):
            dp[pl.ds(s, RB), pl.ds(b, 128)] = (mark == cols + float(b)).astype(F32).astype(BF16)
    arrive(1)
    arrive(4)
    wait_bytes(recv.at[later], sems.at[3])
    for s in range(0, ROWS, 256):
        rows = pl.ds(s, 256)
        last[rows, :] = unpack_last(recv[rows, :])
    for s in range(0, LOOK, 256):
        rows = pl.ds(s, 256)
        rows_held[rows, 0:PACK] = nn(dp[rows, :], recv[...]).astype(BF16)
        rows_held[rows, PACK:D] = nn(dp[rows, :], last[...]).astype(BF16)
    for s in range(0, LOOK, 256):
        rows = pl.ds(s, 256)
        held = rows_held[rows, :]
        hid, dh = silu_parts(nn(held, first_ref[...]))
        hid = hid.astype(BF16)
        hidden[rows, :] = hid
        slope[rows, :] = dh
        tok_ref[rows, :] = (held.astype(F32) + nn(hid, second_ref[...])).astype(BF16)
    wait_bytes(send.at[later], sems.at[2])
    gain = gain_ref[...]
    head = head_ref[...]
    scale = 1.0 / math.sqrt(HD)
    arrive(2)
    for s in range(0, LOOK, RB):
        rows = pl.ds(s, RB)
        t = tok_ref[rows, :].astype(F32)
        r = lax.rsqrt(jnp.mean(t * t, axis=1, keepdims=True) + EPS)
        normed[rows, :] = (t * r * gain).astype(BF16)
    for c in range(0, 4 * D, 256):
        cols = pl.ds(c, 256)
        for s in range(0, LOOK, RB):
            rows = pl.ds(s, RB)
            p = nn(normed[rows, :], w1_ref[:, cols])
            sg = sigmoid(p)
            y = p * sg
            proj[rows, cols] = y.astype(BF16)
            dsl[rows, cols] = (sg + y * (1.0 - sg)).astype(BF16)
    lane = lax.broadcasted_iota(jnp.int32, (HEADS, 128), 1)
    tab = jnp.zeros((HEADS, 128), F32)
    for k in range(BUCKETS):
        tab = tab + jnp.where(lane <= 31 - k, tb_ref[:, k : k + 1], 0.0)
    tab = jnp.where(lane == 33, NEG, tab)
    stamp_col = column(stamp_row_ref[...]).astype(jnp.int32)
    for s in range(0, LOOK, RB):
        rows = pl.ds(s, RB)
        ke = keys_of(s)
        now = jnp.concatenate([stamp_col[s : s + RB, :]] * (ke // 128), axis=1)
        gap = now - stamp_row_ref[:, 0:ke]
        lz = lax.clz(gap + 1)
        if s < HIST:
            i_pos = s + lax.broadcasted_iota(jnp.int32, (RB, ke), 0)
            j_pos = lax.broadcasted_iota(jnp.int32, (RB, ke), 1)
            lz = jnp.where(j_pos <= i_pos, lz, 33)
        idx[rows, 0:ke] = lz
    for h in range(HEADS):
        hc = h * HD
        tab_h = jnp.broadcast_to(tab[h : h + 1, :], (RB, 128))
        for s in range(0, LOOK, RB):
            rows = pl.ds(s, RB)
            ke = keys_of(s)
            q = proj[rows, pl.ds(2 * D + hc, HD)]
            sc = nt(q, proj[0:ke, pl.ds(3 * D + hc, HD)]) * scale
            tt = [
                jnp.take_along_axis(tab_h, idx[rows, j : j + 128], axis=1)
                for j in range(0, ke, 128)
            ]
            sc = sc + jnp.concatenate(tt, axis=1)
            sg = sigmoid(sc)
            y = sc * sg
            w = (y * (1.0 / HIST)).astype(BF16)
            wts[h, rows, 0:ke] = w
            dwt[h, rows, 0:ke] = ((sg + y * (1.0 - sg)) * (1.0 / HIST)).astype(BF16)
            if ke < HIST:
                wts[h, rows, ke:HIST] = jnp.zeros((RB, HIST - ke), BF16)
            att[rows, pl.ds(hc, HD)] = nn(w, proj[0:ke, pl.ds(D + hc, HD)])
    own = {}
    for h in range(HEADS):
        hc = h * HD
        for s in range(HIST, LOOK, RB):
            rows = pl.ds(s, RB)
            q = proj[rows, pl.ds(2 * D + hc, HD)].astype(F32)
            k = proj[rows, pl.ds(3 * D + hc, HD)].astype(F32)
            v = proj[rows, pl.ds(D + hc, HD)].astype(F32)
            os = jnp.sum(q * k, axis=1, keepdims=True) * scale + tb_ref[h : h + 1, 0:1]
            sg = sigmoid(os)
            y = os * sg
            ow = (y * (1.0 / HIST)).astype(BF16).astype(F32)
            own[h, s] = (ow, (sg + y * (1.0 - sg)) * (1.0 / HIST))
            att[rows, pl.ds(hc, HD)] += ow * v
    h_hi = head.astype(BF16)
    h_mid = (head - h_hi.astype(F32)).astype(BF16)
    h_lo = (head - h_hi.astype(F32) - h_mid.astype(F32)).astype(BF16)
    parts = jnp.concatenate([h_hi, h_mid, h_lo, jnp.zeros((13, D), BF16)], axis=0)
    arrive(3)
    hw = jnp.sum(nt(parts, w2_ref[...]), axis=0, keepdims=True)
    label_col = column(label_ref[...])
    loss = jnp.zeros((1, 1), F32)
    uvec = jnp.zeros((1, D), F32)
    dlogit = {}
    for s in range(0, LOOK, RB):
        rows = pl.ds(s, RB)
        a = att[rows, :]
        cen = a - jnp.mean(a, axis=1, keepdims=True)
        spread = lax.rsqrt(jnp.mean(cen * cen, axis=1, keepdims=True) + EPS)
        n = cen * spread
        g = proj[rows, 0:D].astype(F32)
        mixed = (n * g).astype(BF16).astype(F32)
        t = tok_ref[rows, :].astype(F32)
        logit = jnp.sum(t * head + mixed * hw, axis=1, keepdims=True)
        lab = label_col[s : s + RB, 0:1]
        soft = jnp.maximum(logit, 0.0) + jnp.log1p(jnp.exp(-jnp.abs(logit)))
        loss = loss + jnp.sum(soft - lab * logit, axis=0, keepdims=True)
        dl = (jax.nn.sigmoid(logit) - lab) * (1.0 / LOOK)
        dlogit[s] = dl
        uvec = uvec + jnp.sum(mixed * dl, axis=0, keepdims=True)
        dm = (dl * hw).astype(BF16).astype(F32)
        dg = dm * n
        dp[rows, 0:D] = (dg * dsl[rows, 0:D].astype(F32)).astype(BF16)
        dn = dm * g
        da = spread * (
            dn - jnp.mean(dn, axis=1, keepdims=True) - n * jnp.mean(dn * n, axis=1, keepdims=True)
        )
        att[rows, :] = da
    u_held[0] = uvec
    loss_ref[...] = jnp.broadcast_to(loss * (1.0 / LOOK), loss_ref.shape)
    for h in range(HEADS):
        hc = h * HD
        for s in range(0, LOOK, RB):
            rows = pl.ds(s, RB)
            ke = keys_of(s)
            da = att[rows, pl.ds(hc, HD)]
            dw = nt(da.astype(BF16), proj[0:ke, pl.ds(D + hc, HD)])
            ds = (dw * dwt[h, rows, 0:ke].astype(F32) * scale).astype(BF16)
            dwt[h, rows, 0:ke] = ds
            if ke < HIST:
                dwt[h, rows, ke:HIST] = jnp.zeros((RB, HIST - ke), BF16)
            dq = nn(ds, proj[0:ke, pl.ds(3 * D + hc, HD)])
            if s >= HIST:
                q = proj[rows, pl.ds(2 * D + hc, HD)].astype(F32)
                k = proj[rows, pl.ds(3 * D + hc, HD)].astype(F32)
                v = proj[rows, pl.ds(D + hc, HD)].astype(F32)
                ow, osl = own[h, s]
                dos = jnp.sum(da * v, axis=1, keepdims=True) * osl * scale
                dq = dq + dos * k
                dcol = pl.ds(D + hc, HD)
                dp[rows, dcol] = (ow * da * dsl[rows, dcol].astype(F32)).astype(BF16)
                dcol = pl.ds(3 * D + hc, HD)
                dp[rows, dcol] = (dos * q * dsl[rows, dcol].astype(F32)).astype(BF16)
            dcol = pl.ds(2 * D + hc, HD)
            dp[rows, dcol] = (dq * dsl[rows, dcol].astype(F32)).astype(BF16)
        hist = pl.ds(0, HIST)
        dat = att[:, pl.ds(hc, HD)].T.astype(BF16)
        dcol = pl.ds(D + hc, HD)
        dp[hist, dcol] = (nn(dat, wts[h]).T * dsl[hist, dcol].astype(F32)).astype(BF16)
        qt = proj[:, pl.ds(2 * D + hc, HD)].astype(F32).T.astype(BF16)
        dcol = pl.ds(3 * D + hc, HD)
        dp[hist, dcol] = (nn(qt, dwt[h]).T * dsl[hist, dcol].astype(F32)).astype(BF16)
    z, core = user // 2, user % 2
    x, y = item // 4, item % 4
    own = {"x": x, "y": y, "z": z}

    def peer(**to):
        c = {**own, **to}
        return (c["z"] * 2 + to.get("core", core), c["x"] * 4 + c["y"])

    def copy(src, dst, to, send_sem, recv_sem):
        return pltpu.make_async_remote_copy(
            src_ref=src, dst_ref=dst, send_sem=send_sem, recv_sem=recv_sem,
            device_id=to, device_id_type=pl.DeviceIdType.MESH,
        )

    def at(n, size):
        return pl.ds(pl.multiple_of(n * size, size), size)

    def quarter(q):
        return at(q // 4, 16), at(q % 4, 128)

    def group(g):
        return pl.ds(2 * g, 2)

    def square(g):
        a0, a1, a2 = (own[a] for a in ORDER[g])
        rows = pl.ds(pl.multiple_of(core * 256 + a0 * 64 + a1 * 16, 16), 16)
        return (group(g), rows, at(a2, 128))

    def copies(g, stage):
        axis, plane = ORDER[g][0], ORDER[g][1:]
        a0 = own[axis]
        q = own[plane[0]] * 4 + own[plane[1]]
        todo = []
        if stage == 0:
            todo.append((terms.at[group(g), at(1 - core, 256), :], core_in.at[group(g)], peer(core=1 - core)))
        elif stage == 5:
            half_of = (group(g), at(core, 256))
            todo.append((sums_ref.at[half_of], sums_hbm.at[half_of], peer(core=1 - core)))
        elif stage in (1, 4):
            for d in (1, 2, 3):
                to = (a0 + d) % 4
                if stage == 1:
                    src, dst = half.at[group(g), at(to, 64), :], in1.at[g, d - 1]
                else:
                    src = dst = sums_ref.at[group(g), at(core * 4 + a0, 64), :]
                todo.append((src, dst, peer(**{axis: to})))
        else:
            for e in range(1, 16):
                to = (q + e) % 16
                if stage == 2:
                    r, c = quarter(to)
                    src, dst = part1.at[group(g), r, c], in2.at[g, e - 1]
                else:
                    src = dst = sums_ref.at[square(g)]
                todo.append((src, dst, peer(**{plane[0]: to // 4, plane[1]: to % 4})))
        return [
            copy(src, dst, to, send_sems.at[g, stage, n], recv_sems.at[g, stage, n])
            for n, (src, dst, to) in enumerate(todo)
        ]

    def own_half(g):
        half_of = (group(g), at(core, 256))
        return pltpu.make_async_copy(sums_ref.at[half_of], sums_hbm.at[half_of], out_sems.at[g])

    def start(g, stage):
        for c in copies(g, stage):
            c.start()
        if stage == 5:
            own_half(g).start()

    def finish(g, stage):
        for c in copies(g, stage):
            c.wait_recv()
        a0, a1, a2 = (own[a] for a in ORDER[g])
        if stage == 0:
            for b in (2 * g, 2 * g + 1):
                half[b] = (terms[b, at(core, 256), :].astype(F32) + core_in[b].astype(F32)).astype(BF16)
        elif stage == 1:
            total = half[group(g), at(a0, 64), :].astype(F32)
            for d in range(3):
                total = total + in1[g, d].astype(F32)
            part1[group(g)] = total.astype(BF16)
        elif stage == 2:
            total = part1[group(g), at(a1, 16), at(a2, 128)].astype(F32)
            for e in range(15):
                total = total + in2[g, e].astype(F32)
            sums_ref[square(g)] = total.astype(BF16)

    def u_copies(stage):
        if stage == 0:
            peers = [peer(core=1 - core)]
        else:
            a = "xyz"[stage - 1]
            peers = [peer(**{a: (own[a] + d) % 4}) for d in (1, 2, 3)]
        return [
            copy(u_held.at[stage], u_in.at[stage, n], to, u_sems.at[0, stage, n], u_sems.at[1, stage, n])
            for n, to in enumerate(peers)
        ]

    def u_start(stage):
        for c in u_copies(stage):
            c.start()

    def u_finish(stage):
        total = u_held[stage]
        for n, c in enumerate(u_copies(stage)):
            c.wait_recv()
            total = total + u_in[stage, n]
        if stage < 3:
            u_held[stage + 1] = total
        else:
            usum_ref[...] = total

    u_start(0)
    nrt = normed[...].astype(F32).T.astype(BF16)
    for b in range(4):
        for c in range(0, D, 256):
            terms[b, :, pl.ds(c, 256)] = nn(nrt, dp[:, pl.ds(b * D + c, 256)]).astype(BF16)
        if b % 2:
            start(b // 2, 0)
    for s in range(0, LOOK, RB):
        rows = pl.ds(s, RB)
        dnorm = nt(dp[rows, :], w1_ref[...])
        t = tok_ref[rows, :].astype(F32)
        r = lax.rsqrt(jnp.mean(t * t, axis=1, keepdims=True) + EPS)
        tn = dnorm * gain
        tg = dlogit[s] * head + r * tn - t * (r * r * r * jnp.mean(tn * t, axis=1, keepdims=True))
        tgb = tg.astype(BF16)
        de[rows, :] = tgb
        dpr = (nt(tgb, second_ref[...]) * slope[rows, :]).astype(BF16)
        dpre[rows, :] = dpr
        att[rows, :] = tg + nt(dpr, first_ref[...])
    terms[5] = nn(hidden[...].astype(F32).T.astype(BF16), de[...]).astype(BF16)
    terms[4] = nn(rows_held[...].astype(F32).T.astype(BF16), dpre[...]).astype(BF16)
    start(2, 0)
    for g in (0, 1):
        finish(g, 0)
        start(g, 1)
    u_finish(0)
    u_start(1)
    row_grad = att[...].astype(BF16)

    for t in range(ROWS // TILE):
        base = t * TILE
        rows = pl.ds(base, TILE)
        pick = base + lax.broadcasted_iota(jnp.int32, (TILE, LOOK), 0) == slots
        send[rows, :] = pack(nn(pick.astype(F32).astype(BF16), row_grad))

        @pl.loop(*fresh(t))
        def _(k):
            send_chunk(send, back_recv, k, (me + STEP * k) % OWNERS, sems.at[4], sems.at[5])

        if t == 0:
            finish(2, 0)
            start(2, 1)
    back_recv[0:SLOT, :] = send[0:SLOT, :]
    for g in (0, 1):
        finish(g, 1)
        start(g, 2)
    u_finish(1)
    u_start(2)
    finish(2, 1)
    start(2, 2)
    for s in range(0, D, 128):
        sub = (s + lax.broadcasted_iota(jnp.int32, (128, 128), 0)).astype(F32)
        for q in range(0, ROWS, 128):
            proj[pl.ds(s, 128), pl.ds(q, 128)] = (
                (sub == idrow[0:1, q : q + 128]).astype(F32).astype(BF16)
            )
    for stage in (2, 3):
        for g in range(GROUPS):
            finish(g, stage)
            start(g, stage + 1)
        u_finish(stage)
        if stage == 2:
            u_start(3)
    wait_bytes(back_recv.at[later], sems.at[5])
    for s in range(0, ROWS, 256):
        rows = pl.ds(s, 256)
        last[rows, :] = unpack_last(back_recv[rows, :])
    for s in range(0, D, 256):
        rows = pl.ds(s, 256)
        att[rows, 0:PACK] = nn(proj[rows, :], back_recv[...])
        att[rows, PACK:D] = nn(proj[rows, :], last[...])
    table_out = pltpu.make_async_copy(att.at[pl.ds(0, D), :], tablegrad_hbm, out_sems.at[3])
    table_out.start()
    for g in range(GROUPS):
        finish(g, 4)
        start(g, 5)
    for g in range(GROUPS):
        finish(g, 5)
        own_half(g).wait()
    table_out.wait()
    wait_bytes(send.at[later], sems.at[4])
    for stage in range(4):
        for c in u_copies(stage):
            c.wait_send()
    for g in range(GROUPS):
        for stage in range(6):
            for c in copies(g, stage):
                c.wait_send()


VM = pl.BlockSpec(memory_space=pltpu.VMEM)
ANY = pl.BlockSpec(memory_space=pl.ANY)


def train_step(*args):
    dma = pltpu.SemaphoreType.DMA
    return pl.pallas_call(
        step_kernel,
        out_shape=(
            jax.ShapeDtypeStruct((D, D), F32),
            jax.ShapeDtypeStruct((2 * GROUPS, D, D), BF16),
            jax.ShapeDtypeStruct((1, D), F32),
            jax.ShapeDtypeStruct((1, 128), F32),
        ),
        in_specs=[VM] * 7 + [ANY] * 5,
        out_specs=(ANY, ANY, VM, VM),
        scratch_shapes=[
            pltpu.VMEM((2 * GROUPS, D, D), BF16),
            pltpu.VMEM((D, D), BF16),
            pltpu.VMEM((D, D), BF16),
            pltpu.VMEM((D, D), BF16),
            pltpu.VMEM((D, 4 * D), BF16),
            pltpu.VMEM((D, D), BF16),
            pltpu.VMEM((OWNERS, 1, 128), F32),
            pltpu.VMEM((OWNERS, 1, 128), F32),
            pltpu.VMEM((ROWS, 128), F32),
            pltpu.VMEM((8, ROWS), F32),
            pltpu.VMEM((ROWS, PACK), BF16),
            pltpu.VMEM((ROWS, PACK), BF16),
            pltpu.VMEM((ROWS, PACK), BF16),
            pltpu.VMEM((ROWS, 128), BF16),
            pltpu.VMEM((LOOK, D), BF16),
            pltpu.VMEM((LOOK, D), BF16),
            pltpu.VMEM((LOOK, D), F32),
            pltpu.VMEM((LOOK, D), BF16),
            pltpu.VMEM((LOOK, D), BF16),
            pltpu.VMEM((LOOK, 4 * D), BF16),
            pltpu.VMEM((LOOK, 4 * D), BF16),
            pltpu.VMEM((LOOK, HIST), jnp.int32),
            pltpu.VMEM((HEADS, LOOK, HIST), BF16),
            pltpu.VMEM((HEADS, LOOK, HIST), BF16),
            pltpu.VMEM((LOOK, D), F32),
            pltpu.VMEM((LOOK, 4 * D), BF16),
            pltpu.VMEM((LOOK, D), BF16),
            pltpu.VMEM((LOOK, D), BF16),
            pltpu.VMEM((2 * GROUPS, D, D), BF16),
            pltpu.VMEM((2 * GROUPS, 256, D), BF16),
            pltpu.VMEM((2 * GROUPS, 256, D), BF16),
            pltpu.VMEM((GROUPS, 3, 2, 64, D), BF16),
            pltpu.VMEM((2 * GROUPS, 64, D), BF16),
            pltpu.VMEM((GROUPS, 15, 2, 16, 128), BF16),
            pltpu.VMEM((4, 1, D), F32),
            pltpu.VMEM((4, 3, 1, D), F32),
            dma((5,)),
            dma((4,)),
            dma((6,)),
            dma((GROUPS, 6, 15)),
            dma((GROUPS, 6, 15)),
            dma((2, 4, 3)),
        ],
        compiler_params=pltpu.CompilerParams(
            vmem_limit_bytes=60 * 2**20, collective_id=0, has_side_effects=True
        ),
        cost_estimate=pl.CostEstimate(
            flops=14 * 10**9, bytes_accessed=10 * 2**20, transcendentals=5 * 10**6
        ),
        name="step",
    )(*args)


def finish_kernel(tablegrad_ref, sums_ref, usum_ref, head_ref, table_ref, first_ref, second_ref, input_ref, output_ref):
    table_ref[...] = tablegrad_ref[...]
    first_ref[...] = sums_ref[4].astype(F32)
    second_ref[...] = sums_ref[5].astype(F32)
    for b in range(4):
        input_ref[:, pl.ds(b * D, D)] = sums_ref[b].astype(F32)
    output_ref[...] = column(usum_ref[...])[:, 0:1] * head_ref[...]


def outputs(tablegrad, sums, usum, head):
    n = 128

    def rows(width):
        return pl.BlockSpec((n, width), lambda i: (i, 0))

    def shape(width):
        return jax.ShapeDtypeStruct((D, width), F32)

    return pl.pallas_call(
        finish_kernel,
        grid=(D // n,),
        out_shape=(shape(D), shape(D), shape(D), shape(4 * D), shape(D)),
        in_specs=[
            rows(D),
            pl.BlockSpec((2 * GROUPS, n, D), lambda i: (0, i, 0)),
            pl.BlockSpec((1, n), lambda i: (0, i)),
            pl.BlockSpec((1, D), lambda i: (0, 0)),
        ],
        out_specs=(rows(D), rows(D), rows(D), rows(4 * D), rows(D)),
        compiler_params=pltpu.CompilerParams(vmem_limit_bytes=60 * 2**20),
        name="outputs",
    )(tablegrad, sums, usum, head)


def body(
    table, tower_first, tower_second, w_input, w_output, norm_gain, head_vec, time_bias,
    look_owner, look_row, event_time, labels,
):
    head = head_vec.reshape(1, D)
    tablegrad, sums, usum, loss = train_step(
        look_owner.reshape(1, LOOK), look_row, event_time, labels, norm_gain.reshape(1, D), head,
        time_bias, table, tower_first, tower_second, w_input, w_output,
    )
    table_grad, first_grad, second_grad, input_grad, output_grad = outputs(tablegrad, sums, usum, head)
    return (table_grad, first_grad, second_grad, input_grad, output_grad, loss[0, :1])


def solution(mesh):
    return jax.shard_map(
        body,
        mesh=mesh,
        in_specs=(
            P(("user", "item"), None), P(), P(), P(), P(), P(), P(), P(),
            P(("user", "item"), None, None), P(("user", "item"), None),
            P(("user", "item"), None), P(("user", "item"), None),
        ),
        out_specs=(P(("user", "item"), None), P(), P(), P(), P(), P(("user", "item"))),
        check_vma=False,
    )
```

```python
import math

import jax
import jax.numpy as jnp
from jax import lax
from jax.experimental import pallas as pl
from jax.experimental.pallas import tpu as pltpu
from jax.sharding import PartitionSpec as P

D = 512
HEADS = 4
HD = 128
HIST = 512
LOOK = 768
BUCKETS = 16
EPS = 1e-06
F32 = jnp.float32
BF16 = jnp.bfloat16
RB = 128
OWNERS = 128
SLOT = 16
USED = 12
PACK = 384
ROWS = OWNERS * SLOT
TILE = 512
STEP = 37
UNSTEP = 45
NEG = -1e30


def nn(a, b):
    return lax.dot_general(a, b, (((1,), (0,)), ((), ())), preferred_element_type=F32)


def nt(a, b):
    return lax.dot_general(a, b, (((1,), (1,)), ((), ())), preferred_element_type=F32)


def sigmoid(x):
    return 0.5 + 0.5 * jnp.tanh(0.5 * x)


def column(row):
    return jnp.broadcast_to(row.astype(F32), (128, row.shape[1])).T


def keys_of(start):
    return min(HIST, start + RB)


def place():
    return lax.axis_index("user"), lax.axis_index("item")


def device(index):
    return (index // 16, index % 16)


def greet():
    barrier = pltpu.get_barrier_semaphore()

    user, item = place()

    def hail(du, di):
        to = ((user + du) % 8, (item + di) % 16)
        pl.semaphore_signal(barrier, inc=1, device_id=to, device_id_type=pl.DeviceIdType.MESH)

    for di in range(1, 16):
        hail(0, di)
    for di in range(16):

        @pl.loop(1, 8)
        def _(du):
            hail(du, di)


def meet():
    pl.semaphore_wait(pltpu.get_barrier_semaphore(), OWNERS - 1)


def row_in_slot(n):
    return lax.broadcasted_iota(jnp.int32, (n, 128), 0) % SLOT


def pack(y):
    r = row_in_slot(y.shape[0])
    last = y[:, PACK:D]
    out = [
        jnp.where(r >= USED, pltpu.roll(last, USED - 4 * b, 0), y[:, 128 * b : 128 * (b + 1)])
        for b in range(3)
    ]
    return jnp.concatenate(out, axis=1).astype(BF16)


def unpack_last(y):
    n = y.shape[0]
    r = row_in_slot(n)
    p = [pltpu.roll(y[:, 128 * b : 128 * (b + 1)].astype(F32), n - USED + 4 * b, 0) for b in range(3)]
    return jnp.where(r < 4, p[0], jnp.where(r < 8, p[1], p[2])).astype(BF16)


def chunk(ref, k):
    return ref.at[pl.ds(pl.multiple_of(k * SLOT, SLOT), SLOT), :]


def send_chunk(send, recv, k, target, send_sem, recv_sem):
    pltpu.make_async_remote_copy(
        src_ref=chunk(send, k),
        dst_ref=chunk(recv, k),
        send_sem=send_sem,
        recv_sem=recv_sem,
        device_id=device(target),
        device_id_type=pl.DeviceIdType.MESH,
    ).start()


def wait_bytes(ref, sem):
    pltpu.make_async_copy(ref, ref, sem).wait()


def silu_parts(p):
    sg = sigmoid(p)
    y = p * sg
    return y, sg + y * (1.0 - sg)


GROUPS = 3
ORDER = ("xyz", "yzx", "zxy")
BATCH = 8
PLAN = {
    0: (2, 0), 3: (0, 1), 4: (1, 1), 5: (2, 1), 6: (0, 2), 7: (1, 2), 8: (2, 2),
    9: (0, 3), 10: (1, 3), 11: (2, 3), 14: (0, 4), 15: (1, 4),
}


def step_kernel(
    owner_ref, row_ref, stamp_row_ref, label_ref, gain_ref, head_ref, tb_ref,
    table_hbm, first_hbm, second_hbm, w1_hbm, w2_hbm,
    tablegrad_hbm, sums_hbm, usum_ref, loss_ref,
    sums_ref, table_ref, first_ref, second_ref, w1_ref, w2_ref,
    ids_send, ids_recv, idq, idrow, send, recv, back_recv, last, rows_held, hidden, slope, tok_ref,
    normed, proj, dsl, idx, wts, dwt, att, dp, de, dpre,
    terms, core_in, half, in1, part1, in2, u_held, u_in,
    load_sems, out_sems, sems, send_sems, recv_sems, u_sems,
):
    user, item = place()
    me = user * 16 + item
    loads = [
        pltpu.make_async_copy(src, dst, load_sems.at[n])
        for n, (src, dst) in enumerate(
            ((table_hbm, table_ref), (first_hbm, first_ref), (w1_hbm, w1_ref), (w2_hbm, w2_ref), (second_hbm, second_ref))
        )
    ]
    for load in loads:
        load.start()

    gain = gain_ref[...]
    head = head_ref[...]

    def arrive(n):
        loads[n].wait()

    greet()
    j_row = (UNSTEP * (owner_ref[...] - me + OWNERS)) % OWNERS
    named = lax.broadcasted_iota(jnp.int32, (OWNERS, LOOK), 0) == j_row
    named_b = named.astype(F32).astype(BF16)
    before = lax.broadcasted_iota(jnp.int32, (LOOK, LOOK), 0) < lax.broadcasted_iota(
        jnp.int32, (LOOK, LOOK), 1
    )
    earlier = nn(named_b, before.astype(F32).astype(BF16))
    rank = jnp.sum(jnp.where(named, earlier, 0.0), axis=0, keepdims=True)
    slots = j_row * SLOT + rank.astype(jnp.int32)
    lanes = lax.broadcasted_iota(jnp.int32, (LOOK, 128), 1).astype(F32)
    listed = jnp.where(column(rank) == lanes, column(row_ref[...]) - 256.0, 0.0)
    ids_send[:, 0, :] = nn(named_b, listed.astype(BF16))
    ids_recv[0] = ids_send[0]
    meet()

    @pl.loop(1, OWNERS)
    def _(k):
        pltpu.make_async_remote_copy(
            src_ref=ids_send.at[k],
            dst_ref=ids_recv.at[k],
            send_sem=sems.at[0],
            recv_sem=sems.at[1],
            device_id=device((me + STEP * k) % OWNERS),
            device_id_type=pl.DeviceIdType.MESH,
        ).start()

    slot_col = column(slots)
    others = pl.ds(1, OWNERS - 1)
    later = pl.ds(SLOT, ROWS - SLOT)
    arrive(0)
    wait_bytes(ids_recv.at[others], sems.at[1])
    wait_bytes(ids_send.at[others], sems.at[0])
    ids = ids_recv[:, 0, :].astype(BF16)

    def fresh(t):
        return max(1, t * (TILE // SLOT)), (t + 1) * (TILE // SLOT)

    for t in range(ROWS // TILE):
        base = t * TILE
        rows = pl.ds(base, TILE)
        slot_at = base + lax.broadcasted_iota(jnp.int32, (TILE, 128), 0)
        lane = lax.broadcasted_iota(jnp.int32, (TILE, 128), 1)
        spread = nn((slot_at // SLOT == lane).astype(F32).astype(BF16), ids)
        r = slot_at % SLOT
        mine = jnp.sum(jnp.where(r == lane, spread + 256.0, 0.0), axis=1, keepdims=True)
        mine = jnp.where(r < USED, mine, -1.0)
        idq[rows, :] = mine
        cols = lane.astype(F32)
        pick = jnp.concatenate(
            [(mine == cols + 128.0 * b).astype(F32).astype(BF16) for b in range(4)], axis=1
        )
        send[rows, :] = pack(nn(pick, table_ref[...]))

        @pl.loop(*fresh(t))
        def _(k):
            target = (me - (STEP * k) % OWNERS + OWNERS) % OWNERS
            send_chunk(send, recv, k, target, sems.at[2], sems.at[3])

    recv[0:SLOT, :] = send[0:SLOT, :]
    idrow[...] = idq[...].T[0:8, :]
    for s in range(0, LOOK, RB):
        mark = slot_col[s : s + RB, :]
        cols = lax.broadcasted_iota(jnp.int32, (RB, 128), 1).astype(F32)
        for b in range(0, ROWS, 128):
            dp[pl.ds(s, RB), pl.ds(b, 128)] = (mark == cols + float(b)).astype(F32).astype(BF16)
    lane = lax.broadcasted_iota(jnp.int32, (HEADS, 128), 1)
    tab = jnp.zeros((HEADS, 128), F32)
    for k in range(BUCKETS):
        tab = tab + jnp.where(lane <= 31 - k, tb_ref[:, k : k + 1], 0.0)
    tab = jnp.where(lane == 33, NEG, tab)
    stamp_col = column(stamp_row_ref[...]).astype(jnp.int32)
    for s in range(0, LOOK, RB):
        rows = pl.ds(s, RB)
        ke = keys_of(s)
        now = jnp.concatenate([stamp_col[s : s + RB, :]] * (ke // 128), axis=1)
        gap = now - stamp_row_ref[:, 0:ke]
        lz = lax.clz(gap + 1)
        if s < HIST:
            i_pos = s + lax.broadcasted_iota(jnp.int32, (RB, ke), 0)
            j_pos = lax.broadcasted_iota(jnp.int32, (RB, ke), 1)
            lz = jnp.where(j_pos <= i_pos, lz, 33)
        idx[rows, 0:ke] = lz
    h_hi = head.astype(BF16)
    h_mid = (head - h_hi.astype(F32)).astype(BF16)
    h_lo = (head - h_hi.astype(F32) - h_mid.astype(F32)).astype(BF16)
    parts = jnp.concatenate([h_hi, h_mid, h_lo, jnp.zeros((13, D), BF16)], axis=0)
    arrive(3)
    hw = jnp.sum(nt(parts, w2_ref[...]), axis=0, keepdims=True)
    arrive(1)
    arrive(4)
    wait_bytes(recv.at[later], sems.at[3])
    for s in range(0, ROWS, 256):
        rows = pl.ds(s, 256)
        last[rows, :] = unpack_last(recv[rows, :])
    for s in range(0, LOOK, 256):
        rows = pl.ds(s, 256)
        rows_held[rows, 0:PACK] = nn(dp[rows, :], recv[...]).astype(BF16)
        rows_held[rows, PACK:D] = nn(dp[rows, :], last[...]).astype(BF16)
    for s in range(0, LOOK, 256):
        rows = pl.ds(s, 256)
        held = rows_held[rows, :]
        hid, dh = silu_parts(nn(held, first_ref[...]))
        hid = hid.astype(BF16)
        hidden[rows, :] = hid
        slope[rows, :] = dh
        tok_ref[rows, :] = (held.astype(F32) + nn(hid, second_ref[...])).astype(BF16)
    wait_bytes(send.at[later], sems.at[2])
    scale = 1.0 / math.sqrt(HD)
    arrive(2)
    for s in range(0, LOOK, RB):
        rows = pl.ds(s, RB)
        t = tok_ref[rows, :].astype(F32)
        r = lax.rsqrt(jnp.mean(t * t, axis=1, keepdims=True) + EPS)
        normed[rows, :] = (t * r * gain).astype(BF16)
    for c in range(0, 4 * D, 256):
        cols = pl.ds(c, 256)
        for s in range(0, LOOK, RB):
            rows = pl.ds(s, RB)
            p = nn(normed[rows, :], w1_ref[:, cols])
            sg = sigmoid(p)
            y = p * sg
            proj[rows, cols] = y.astype(BF16)
            dsl[rows, cols] = (sg + y * (1.0 - sg)).astype(BF16)
    for h in range(HEADS):
        hc = h * HD
        tab_h = jnp.broadcast_to(tab[h : h + 1, :], (RB, 128))
        for s in range(0, LOOK, RB):
            rows = pl.ds(s, RB)
            ke = keys_of(s)
            q = proj[rows, pl.ds(2 * D + hc, HD)]
            sc = nt(q, proj[0:ke, pl.ds(3 * D + hc, HD)]) * scale
            tt = [
                jnp.take_along_axis(tab_h, idx[rows, j : j + 128], axis=1)
                for j in range(0, ke, 128)
            ]
            sc = sc + jnp.concatenate(tt, axis=1)
            sg = sigmoid(sc)
            y = sc * sg
            w = (y * (1.0 / HIST)).astype(BF16)
            wts[h, rows, 0:ke] = w
            dwt[h, rows, 0:ke] = ((sg + y * (1.0 - sg)) * (1.0 / HIST)).astype(BF16)
            if ke < HIST:
                wts[h, rows, ke:HIST] = jnp.zeros((RB, HIST - ke), BF16)
            att[rows, pl.ds(hc, HD)] = nn(w, proj[0:ke, pl.ds(D + hc, HD)])
    own = {}
    for h in range(HEADS):
        hc = h * HD
        for s in range(HIST, LOOK, RB):
            rows = pl.ds(s, RB)
            q = proj[rows, pl.ds(2 * D + hc, HD)].astype(F32)
            k = proj[rows, pl.ds(3 * D + hc, HD)].astype(F32)
            v = proj[rows, pl.ds(D + hc, HD)].astype(F32)
            os = jnp.sum(q * k, axis=1, keepdims=True) * scale + tb_ref[h : h + 1, 0:1]
            sg = sigmoid(os)
            y = os * sg
            ow = (y * (1.0 / HIST)).astype(BF16).astype(F32)
            own[h, s] = (ow, (sg + y * (1.0 - sg)) * (1.0 / HIST))
            att[rows, pl.ds(hc, HD)] += ow * v
    label_col = column(label_ref[...])
    loss = jnp.zeros((1, 1), F32)
    uvec = jnp.zeros((1, D), F32)
    dlogit = {}
    for s in range(0, LOOK, RB):
        rows = pl.ds(s, RB)
        a = att[rows, :]
        cen = a - jnp.mean(a, axis=1, keepdims=True)
        spread = lax.rsqrt(jnp.mean(cen * cen, axis=1, keepdims=True) + EPS)
        n = cen * spread
        g = proj[rows, 0:D].astype(F32)
        mixed = (n * g).astype(BF16).astype(F32)
        t = tok_ref[rows, :].astype(F32)
        logit = jnp.sum(t * head + mixed * hw, axis=1, keepdims=True)
        lab = label_col[s : s + RB, 0:1]
        soft = jnp.maximum(logit, 0.0) + jnp.log1p(jnp.exp(-jnp.abs(logit)))
        loss = loss + jnp.sum(soft - lab * logit, axis=0, keepdims=True)
        dl = (jax.nn.sigmoid(logit) - lab) * (1.0 / LOOK)
        dlogit[s] = dl
        uvec = uvec + jnp.sum(mixed * dl, axis=0, keepdims=True)
        dm = (dl * hw).astype(BF16).astype(F32)
        dg = dm * n
        dp[rows, 0:D] = (dg * dsl[rows, 0:D].astype(F32)).astype(BF16)
        dn = dm * g
        da = spread * (
            dn - jnp.mean(dn, axis=1, keepdims=True) - n * jnp.mean(dn * n, axis=1, keepdims=True)
        )
        att[rows, :] = da
    u_held[0] = uvec
    loss_ref[...] = jnp.broadcast_to(loss * (1.0 / LOOK), loss_ref.shape)
    for h in range(HEADS):
        hc = h * HD
        for s in range(0, LOOK, RB):
            rows = pl.ds(s, RB)
            ke = keys_of(s)
            da = att[rows, pl.ds(hc, HD)]
            dw = nt(da.astype(BF16), proj[0:ke, pl.ds(D + hc, HD)])
            ds = (dw * dwt[h, rows, 0:ke].astype(F32) * scale).astype(BF16)
            dwt[h, rows, 0:ke] = ds
            if ke < HIST:
                dwt[h, rows, ke:HIST] = jnp.zeros((RB, HIST - ke), BF16)
            dq = nn(ds, proj[0:ke, pl.ds(3 * D + hc, HD)])
            if s >= HIST:
                q = proj[rows, pl.ds(2 * D + hc, HD)].astype(F32)
                k = proj[rows, pl.ds(3 * D + hc, HD)].astype(F32)
                v = proj[rows, pl.ds(D + hc, HD)].astype(F32)
                ow, osl = own[h, s]
                dos = jnp.sum(da * v, axis=1, keepdims=True) * osl * scale
                dq = dq + dos * k
                dcol = pl.ds(D + hc, HD)
                dp[rows, dcol] = (ow * da * dsl[rows, dcol].astype(F32)).astype(BF16)
                dcol = pl.ds(3 * D + hc, HD)
                dp[rows, dcol] = (dos * q * dsl[rows, dcol].astype(F32)).astype(BF16)
            dcol = pl.ds(2 * D + hc, HD)
            dp[rows, dcol] = (dq * dsl[rows, dcol].astype(F32)).astype(BF16)
        hist = pl.ds(0, HIST)
        dat = att[:, pl.ds(hc, HD)].T.astype(BF16)
        dcol = pl.ds(D + hc, HD)
        dp[hist, dcol] = (nn(dat, wts[h]).T * dsl[hist, dcol].astype(F32)).astype(BF16)
        qt = proj[:, pl.ds(2 * D + hc, HD)].astype(F32).T.astype(BF16)
        dcol = pl.ds(3 * D + hc, HD)
        dp[hist, dcol] = (nn(qt, dwt[h]).T * dsl[hist, dcol].astype(F32)).astype(BF16)
    z, core = user // 2, user % 2
    x, y = item // 4, item % 4
    own = {"x": x, "y": y, "z": z}

    def peer(**to):
        c = {**own, **to}
        return (c["z"] * 2 + to.get("core", core), c["x"] * 4 + c["y"])

    def copy(src, dst, to, send_sem, recv_sem):
        return pltpu.make_async_remote_copy(
            src_ref=src, dst_ref=dst, send_sem=send_sem, recv_sem=recv_sem,
            device_id=to, device_id_type=pl.DeviceIdType.MESH,
        )

    def at(n, size):
        return pl.ds(pl.multiple_of(n * size, size), size)

    def quarter(q):
        return at(q // 4, 16), at(q % 4, 128)

    def group(g):
        return pl.ds(2 * g, 2)

    def square(g):
        a0, a1, a2 = (own[a] for a in ORDER[g])
        rows = pl.ds(pl.multiple_of(core * 256 + a0 * 64 + a1 * 16, 16), 16)
        return (group(g), rows, at(a2, 128))

    def copies(g, stage):
        axis, plane = ORDER[g][0], ORDER[g][1:]
        a0 = own[axis]
        q = own[plane[0]] * 4 + own[plane[1]]
        todo = []
        if stage == 0:
            todo.append((terms.at[group(g), at(1 - core, 256), :], core_in.at[group(g)], peer(core=1 - core)))
        elif stage == 5:
            half_of = (group(g), at(core, 256))
            todo.append((sums_ref.at[half_of], sums_hbm.at[half_of], peer(core=1 - core)))
        elif stage in (1, 4):
            for d in (1, 2, 3):
                to = (a0 + d) % 4
                if stage == 1:
                    src, dst = half.at[group(g), at(to, 64), :], in1.at[g, d - 1]
                else:
                    src = dst = sums_ref.at[group(g), at(core * 4 + a0, 64), :]
                todo.append((src, dst, peer(**{axis: to})))
        else:
            for e in range(1, 16):
                to = (q + e) % 16
                if stage == 2:
                    r, c = quarter(to)
                    src, dst = part1.at[group(g), r, c], in2.at[g, e - 1]
                else:
                    src = dst = sums_ref.at[square(g)]
                todo.append((src, dst, peer(**{plane[0]: to // 4, plane[1]: to % 4})))
        return [
            copy(src, dst, to, send_sems.at[g, stage, n], recv_sems.at[g, stage, n])
            for n, (src, dst, to) in enumerate(todo)
        ]

    def own_half(g):
        half_of = (group(g), at(core, 256))
        return pltpu.make_async_copy(sums_ref.at[half_of], sums_hbm.at[half_of], out_sems.at[g])

    def start(g, stage):
        for c in copies(g, stage):
            c.start()
        if stage == 5:
            own_half(g).start()

    def finish(g, stage):
        for c in copies(g, stage):
            c.wait_recv()
        a0, a1, a2 = (own[a] for a in ORDER[g])
        if stage == 0:
            for b in (2 * g, 2 * g + 1):
                half[b] = (terms[b, at(core, 256), :].astype(F32) + core_in[b].astype(F32)).astype(BF16)
        elif stage == 1:
            total = half[group(g), at(a0, 64), :].astype(F32)
            for d in range(3):
                total = total + in1[g, d].astype(F32)
            part1[group(g)] = total.astype(BF16)
        elif stage == 2:
            total = part1[group(g), at(a1, 16), at(a2, 128)].astype(F32)
            for e in range(15):
                total = total + in2[g, e].astype(F32)
            sums_ref[square(g)] = total.astype(BF16)

    def u_copies(stage):
        if stage == 0:
            peers = [peer(core=1 - core)]
        else:
            a = "xyz"[stage - 1]
            peers = [peer(**{a: (own[a] + d) % 4}) for d in (1, 2, 3)]
        return [
            copy(u_held.at[stage], u_in.at[stage, n], to, u_sems.at[0, stage, n], u_sems.at[1, stage, n])
            for n, to in enumerate(peers)
        ]

    def u_start(stage):
        for c in u_copies(stage):
            c.start()

    def u_finish(stage):
        total = u_held[stage]
        for n, c in enumerate(u_copies(stage)):
            c.wait_recv()
            total = total + u_in[stage, n]
        if stage < 3:
            u_held[stage + 1] = total
        else:
            usum_ref[...] = total

    u_start(0)
    nrt = normed[...].astype(F32).T.astype(BF16)
    for b in range(4):
        for c in range(0, D, 256):
            terms[b, :, pl.ds(c, 256)] = nn(nrt, dp[:, pl.ds(b * D + c, 256)]).astype(BF16)
        if b % 2:
            start(b // 2, 0)
    for s in range(0, LOOK, RB):
        rows = pl.ds(s, RB)
        dnorm = nt(dp[rows, :], w1_ref[...])
        t = tok_ref[rows, :].astype(F32)
        r = lax.rsqrt(jnp.mean(t * t, axis=1, keepdims=True) + EPS)
        tn = dnorm * gain
        tg = dlogit[s] * head + r * tn - t * (r * r * r * jnp.mean(tn * t, axis=1, keepdims=True))
        tgb = tg.astype(BF16)
        de[rows, :] = tgb
        dpr = (nt(tgb, second_ref[...]) * slope[rows, :]).astype(BF16)
        dpre[rows, :] = dpr
        att[rows, :] = tg + nt(dpr, first_ref[...])
    terms[5] = nn(hidden[...].astype(F32).T.astype(BF16), de[...]).astype(BF16)
    terms[4] = nn(rows_held[...].astype(F32).T.astype(BF16), dpre[...]).astype(BF16)
    start(2, 0)
    for g in (0, 1):
        finish(g, 0)
        start(g, 1)
    u_finish(0)
    u_start(1)
    row_grad = att[...].astype(BF16)

    for batch in range(OWNERS // BATCH):
        base = batch * BATCH * SLOT
        if base % TILE == 0:
            rows = pl.ds(base, TILE)
            pick = base + lax.broadcasted_iota(jnp.int32, (TILE, LOOK), 0) == slots
            send[rows, :] = pack(nn(pick.astype(F32).astype(BF16), row_grad))
        if batch == 0:
            back_recv[0:SLOT, :] = send[0:SLOT, :]

        @pl.loop(max(1, batch * BATCH), (batch + 1) * BATCH)
        def _(k):
            send_chunk(send, back_recv, k, (me + STEP * k) % OWNERS, sems.at[4], sems.at[5])

        if batch in PLAN:
            g, stage = PLAN[batch]
            finish(g, stage)
            start(g, stage + 1)
            if g == 2 and stage > 0:
                u_finish(stage)
                if stage < 3:
                    u_start(stage + 1)

    for s in range(0, D, 128):
        sub = (s + lax.broadcasted_iota(jnp.int32, (128, 128), 0)).astype(F32)
        for q in range(0, ROWS, 128):
            proj[pl.ds(s, 128), pl.ds(q, 128)] = (
                (sub == idrow[0:1, q : q + 128]).astype(F32).astype(BF16)
            )
    finish(2, 4)
    start(2, 5)
    wait_bytes(back_recv.at[later], sems.at[5])
    for s in range(0, ROWS, 256):
        rows = pl.ds(s, 256)
        last[rows, :] = unpack_last(back_recv[rows, :])
    for s in range(0, D, 256):
        rows = pl.ds(s, 256)
        att[rows, 0:PACK] = nn(proj[rows, :], back_recv[...])
        att[rows, PACK:D] = nn(proj[rows, :], last[...])
    table_out = pltpu.make_async_copy(att.at[pl.ds(0, D), :], tablegrad_hbm, out_sems.at[3])
    table_out.start()
    for g in range(GROUPS):
        finish(g, 5)
        own_half(g).wait()
    table_out.wait()
    wait_bytes(send.at[later], sems.at[4])
    for stage in range(4):
        for c in u_copies(stage):
            c.wait_send()
    for g in range(GROUPS):
        for stage in range(6):
            for c in copies(g, stage):
                c.wait_send()


VM = pl.BlockSpec(memory_space=pltpu.VMEM)
ANY = pl.BlockSpec(memory_space=pl.ANY)


def train_step(*args):
    dma = pltpu.SemaphoreType.DMA
    return pl.pallas_call(
        step_kernel,
        out_shape=(
            jax.ShapeDtypeStruct((D, D), F32),
            jax.ShapeDtypeStruct((2 * GROUPS, D, D), BF16),
            jax.ShapeDtypeStruct((1, D), F32),
            jax.ShapeDtypeStruct((1, 128), F32),
        ),
        in_specs=[VM] * 7 + [ANY] * 5,
        out_specs=(ANY, ANY, VM, VM),
        scratch_shapes=[
            pltpu.VMEM((2 * GROUPS, D, D), BF16),
            pltpu.VMEM((D, D), BF16),
            pltpu.VMEM((D, D), BF16),
            pltpu.VMEM((D, D), BF16),
            pltpu.VMEM((D, 4 * D), BF16),
            pltpu.VMEM((D, D), BF16),
            pltpu.VMEM((OWNERS, 1, 128), F32),
            pltpu.VMEM((OWNERS, 1, 128), F32),
            pltpu.VMEM((ROWS, 128), F32),
            pltpu.VMEM((8, ROWS), F32),
            pltpu.VMEM((ROWS, PACK), BF16),
            pltpu.VMEM((ROWS, PACK), BF16),
            pltpu.VMEM((ROWS, PACK), BF16),
            pltpu.VMEM((ROWS, 128), BF16),
            pltpu.VMEM((LOOK, D), BF16),
            pltpu.VMEM((LOOK, D), BF16),
            pltpu.VMEM((LOOK, D), F32),
            pltpu.VMEM((LOOK, D), BF16),
            pltpu.VMEM((LOOK, D), BF16),
            pltpu.VMEM((LOOK, 4 * D), BF16),
            pltpu.VMEM((LOOK, 4 * D), BF16),
            pltpu.VMEM((LOOK, HIST), jnp.int32),
            pltpu.VMEM((HEADS, LOOK, HIST), BF16),
            pltpu.VMEM((HEADS, LOOK, HIST), BF16),
            pltpu.VMEM((LOOK, D), F32),
            pltpu.VMEM((LOOK, 4 * D), BF16),
            pltpu.VMEM((LOOK, D), BF16),
            pltpu.VMEM((LOOK, D), BF16),
            pltpu.VMEM((2 * GROUPS, D, D), BF16),
            pltpu.VMEM((2 * GROUPS, 256, D), BF16),
            pltpu.VMEM((2 * GROUPS, 256, D), BF16),
            pltpu.VMEM((GROUPS, 3, 2, 64, D), BF16),
            pltpu.VMEM((2 * GROUPS, 64, D), BF16),
            pltpu.VMEM((GROUPS, 15, 2, 16, 128), BF16),
            pltpu.VMEM((4, 1, D), F32),
            pltpu.VMEM((4, 3, 1, D), F32),
            dma((5,)),
            dma((4,)),
            dma((6,)),
            dma((GROUPS, 6, 15)),
            dma((GROUPS, 6, 15)),
            dma((2, 4, 3)),
        ],
        compiler_params=pltpu.CompilerParams(
            vmem_limit_bytes=60 * 2**20, collective_id=0, has_side_effects=True
        ),
        cost_estimate=pl.CostEstimate(
            flops=14 * 10**9, bytes_accessed=10 * 2**20, transcendentals=5 * 10**6
        ),
        name="step",
    )(*args)


def finish_kernel(tablegrad_ref, sums_ref, usum_ref, head_ref, table_ref, first_ref, second_ref, input_ref, output_ref):
    table_ref[...] = tablegrad_ref[...]
    first_ref[...] = sums_ref[4].astype(F32)
    second_ref[...] = sums_ref[5].astype(F32)
    for b in range(4):
        input_ref[:, pl.ds(b * D, D)] = sums_ref[b].astype(F32)
    output_ref[...] = column(usum_ref[...])[:, 0:1] * head_ref[...]


def outputs(tablegrad, sums, usum, head):
    n = 128

    def rows(width):
        return pl.BlockSpec((n, width), lambda i: (i, 0))

    def shape(width):
        return jax.ShapeDtypeStruct((D, width), F32)

    return pl.pallas_call(
        finish_kernel,
        grid=(D // n,),
        out_shape=(shape(D), shape(D), shape(D), shape(4 * D), shape(D)),
        in_specs=[
            rows(D),
            pl.BlockSpec((2 * GROUPS, n, D), lambda i: (0, i, 0)),
            pl.BlockSpec((1, n), lambda i: (0, i)),
            pl.BlockSpec((1, D), lambda i: (0, 0)),
        ],
        out_specs=(rows(D), rows(D), rows(D), rows(4 * D), rows(D)),
        compiler_params=pltpu.CompilerParams(vmem_limit_bytes=60 * 2**20),
        name="outputs",
    )(tablegrad, sums, usum, head)


def body(
    table, tower_first, tower_second, w_input, w_output, norm_gain, head_vec, time_bias,
    look_owner, look_row, event_time, labels,
):
    head = head_vec.reshape(1, D)
    tablegrad, sums, usum, loss = train_step(
        look_owner.reshape(1, LOOK), look_row, event_time, labels, norm_gain.reshape(1, D), head,
        time_bias, table, tower_first, tower_second, w_input, w_output,
    )
    table_grad, first_grad, second_grad, input_grad, output_grad = outputs(tablegrad, sums, usum, head)
    return (table_grad, first_grad, second_grad, input_grad, output_grad, loss[0, :1])


def solution(mesh):
    return jax.shard_map(
        body,
        mesh=mesh,
        in_specs=(
            P(("user", "item"), None), P(), P(), P(), P(), P(), P(), P(),
            P(("user", "item"), None, None), P(("user", "item"), None),
            P(("user", "item"), None), P(("user", "item"), None),
        ),
        out_specs=(P(("user", "item"), None), P(), P(), P(), P(), P(("user", "item"))),
        check_vma=False,
    )
```

```python
import math

import jax
import jax.numpy as jnp
from jax import lax
from jax.experimental import pallas as pl
from jax.experimental.pallas import tpu as pltpu
from jax.sharding import PartitionSpec as P

D = 512
HEADS = 4
HD = 128
HIST = 512
LOOK = 768
BUCKETS = 16
EPS = 1e-06
F32 = jnp.float32
BF16 = jnp.bfloat16
RB = 128
OWNERS = 128
SLOT = 16
USED = 12
PACK = 384
ROWS = OWNERS * SLOT
TILE = 512
STEP = 37
UNSTEP = 45
NEG = -1e30


def nn(a, b):
    return lax.dot_general(a, b, (((1,), (0,)), ((), ())), preferred_element_type=F32)


def nt(a, b):
    return lax.dot_general(a, b, (((1,), (1,)), ((), ())), preferred_element_type=F32)


def sigmoid(x):
    return 0.5 + 0.5 * jnp.tanh(0.5 * x)


def column(row):
    return jnp.broadcast_to(row.astype(F32), (128, row.shape[1])).T


def keys_of(start):
    return min(HIST, start + RB)


def place():
    return lax.axis_index("user"), lax.axis_index("item")


def device(index):
    return (index // 16, index % 16)


def greet():
    barrier = pltpu.get_barrier_semaphore()

    user, item = place()

    def hail(du, di):
        to = ((user + du) % 8, (item + di) % 16)
        pl.semaphore_signal(barrier, inc=1, device_id=to, device_id_type=pl.DeviceIdType.MESH)

    for di in range(1, 16):
        hail(0, di)
    for di in range(16):

        @pl.loop(1, 8)
        def _(du):
            hail(du, di)


def meet():
    pl.semaphore_wait(pltpu.get_barrier_semaphore(), OWNERS - 1)


def row_in_slot(n):
    return lax.broadcasted_iota(jnp.int32, (n, 128), 0) % SLOT


def pack(y):
    r = row_in_slot(y.shape[0])
    last = y[:, PACK:D]
    out = [
        jnp.where(r >= USED, pltpu.roll(last, USED - 4 * b, 0), y[:, 128 * b : 128 * (b + 1)])
        for b in range(3)
    ]
    return jnp.concatenate(out, axis=1).astype(BF16)


def unpack_last(y):
    n = y.shape[0]
    r = row_in_slot(n)
    p = [pltpu.roll(y[:, 128 * b : 128 * (b + 1)].astype(F32), n - USED + 4 * b, 0) for b in range(3)]
    return jnp.where(r < 4, p[0], jnp.where(r < 8, p[1], p[2])).astype(BF16)


def chunk(ref, k):
    return ref.at[pl.ds(pl.multiple_of(k * SLOT, SLOT), SLOT), :]


def send_chunk(send, recv, k, target, send_sem, recv_sem):
    pltpu.make_async_remote_copy(
        src_ref=chunk(send, k),
        dst_ref=chunk(recv, k),
        send_sem=send_sem,
        recv_sem=recv_sem,
        device_id=device(target),
        device_id_type=pl.DeviceIdType.MESH,
    ).start()


def wait_bytes(ref, sem):
    pltpu.make_async_copy(ref, ref, sem).wait()


def silu_parts(p):
    sg = sigmoid(p)
    y = p * sg
    return y, sg + y * (1.0 - sg)


GROUPS = 3
ORDER = ("xyz", "yzx", "zxy")
BATCH = 8
PLAN = {
    0: (2, 0), 3: (0, 1), 4: (1, 1), 5: (2, 1), 6: (0, 2), 7: (1, 2), 8: (2, 2),
    9: (0, 3), 10: (1, 3), 11: (2, 3), 14: (0, 4), 15: (1, 4),
}


def step_kernel(
    owner_ref, row_ref, stamp_row_ref, label_ref, gain_ref, head_ref, tb_ref,
    table_hbm, first_hbm, second_hbm, w1_hbm, w2_hbm,
    tablegrad_hbm, sums_hbm, usum_ref, loss_ref,
    sums_ref, table_ref, first_ref, second_ref, w1_ref, w2_ref,
    ids_send, ids_recv, idq, idrow, send, recv, back_recv, rows_held, hidden, slope, tok_ref,
    normed, proj, dsl, idx, wts, dwt, att, dp, de, dpre,
    terms, core_in, half, in1, part1, in2, u_held, u_in,
    load_sems, out_sems, tile_sems, sems, send_sems, recv_sems, u_sems,
):
    user, item = place()
    me = user * 16 + item
    loads = [
        pltpu.make_async_copy(src, dst, load_sems.at[n])
        for n, (src, dst) in enumerate(
            ((table_hbm, table_ref), (first_hbm, first_ref), (w1_hbm, w1_ref), (w2_hbm, w2_ref), (second_hbm, second_ref))
        )
    ]
    for load in loads:
        load.start()

    gain = gain_ref[...]
    head = head_ref[...]

    def arrive(n):
        loads[n].wait()

    greet()
    j_row = (UNSTEP * (owner_ref[...] - me + OWNERS)) % OWNERS
    named = lax.broadcasted_iota(jnp.int32, (OWNERS, LOOK), 0) == j_row
    named_b = named.astype(F32).astype(BF16)
    before = lax.broadcasted_iota(jnp.int32, (LOOK, LOOK), 0) < lax.broadcasted_iota(
        jnp.int32, (LOOK, LOOK), 1
    )
    earlier = nn(named_b, before.astype(F32).astype(BF16))
    rank = jnp.sum(jnp.where(named, earlier, 0.0), axis=0, keepdims=True)
    slots = j_row * SLOT + rank.astype(jnp.int32)
    lanes = lax.broadcasted_iota(jnp.int32, (LOOK, 128), 1).astype(F32)
    listed = jnp.where(column(rank) == lanes, column(row_ref[...]) - 256.0, 0.0)
    ids_send[:, 0, :] = nn(named_b, listed.astype(BF16))
    ids_recv[0] = ids_send[0]
    meet()

    @pl.loop(1, OWNERS)
    def _(k):
        pltpu.make_async_remote_copy(
            src_ref=ids_send.at[k],
            dst_ref=ids_recv.at[k],
            send_sem=sems.at[0],
            recv_sem=sems.at[1],
            device_id=device((me + STEP * k) % OWNERS),
            device_id_type=pl.DeviceIdType.MESH,
        ).start()

    slot_col = column(slots)
    others = pl.ds(1, OWNERS - 1)
    later = pl.ds(SLOT, ROWS - SLOT)
    arrive(0)
    wait_bytes(ids_recv.at[others], sems.at[1])
    wait_bytes(ids_send.at[others], sems.at[0])
    ids = ids_recv[:, 0, :].astype(BF16)

    def fresh(t):
        return max(1, t * (TILE // SLOT)), (t + 1) * (TILE // SLOT)

    for t in range(ROWS // TILE):
        base = t * TILE
        rows = pl.ds(base, TILE)
        slot_at = base + lax.broadcasted_iota(jnp.int32, (TILE, 128), 0)
        lane = lax.broadcasted_iota(jnp.int32, (TILE, 128), 1)
        spread = nn((slot_at // SLOT == lane).astype(F32).astype(BF16), ids)
        r = slot_at % SLOT
        mine = jnp.sum(jnp.where(r == lane, spread + 256.0, 0.0), axis=1, keepdims=True)
        mine = jnp.where(r < USED, mine, -1.0)
        idq[rows, :] = mine
        cols = lane.astype(F32)
        pick = jnp.concatenate(
            [(mine == cols + 128.0 * b).astype(F32).astype(BF16) for b in range(4)], axis=1
        )
        send[rows, :] = pack(nn(pick, table_ref[...]))

        @pl.loop(*fresh(t))
        def _(k):
            target = (me - (STEP * k) % OWNERS + OWNERS) % OWNERS
            send_chunk(send, recv, k, target, sems.at[2], tile_sems.at[0, t])

    recv[0:SLOT, :] = send[0:SLOT, :]
    idrow[...] = idq[...].T[0:8, :]
    for s in range(0, LOOK, RB):
        mark = slot_col[s : s + RB, :]
        cols = lax.broadcasted_iota(jnp.int32, (RB, 128), 1).astype(F32)
        for b in range(0, ROWS, 128):
            dp[pl.ds(s, RB), pl.ds(b, 128)] = (mark == cols + float(b)).astype(F32).astype(BF16)
    lane = lax.broadcasted_iota(jnp.int32, (HEADS, 128), 1)
    tab = jnp.zeros((HEADS, 128), F32)
    for k in range(BUCKETS):
        tab = tab + jnp.where(lane <= 31 - k, tb_ref[:, k : k + 1], 0.0)
    tab = jnp.where(lane == 33, NEG, tab)
    stamp_col = column(stamp_row_ref[...]).astype(jnp.int32)
    for s in range(0, LOOK, RB):
        rows = pl.ds(s, RB)
        ke = keys_of(s)
        now = jnp.concatenate([stamp_col[s : s + RB, :]] * (ke // 128), axis=1)
        gap = now - stamp_row_ref[:, 0:ke]
        lz = lax.clz(gap + 1)
        if s < HIST:
            i_pos = s + lax.broadcasted_iota(jnp.int32, (RB, ke), 0)
            j_pos = lax.broadcasted_iota(jnp.int32, (RB, ke), 1)
            lz = jnp.where(j_pos <= i_pos, lz, 33)
        idx[rows, 0:ke] = lz
    h_hi = head.astype(BF16)
    h_mid = (head - h_hi.astype(F32)).astype(BF16)
    h_lo = (head - h_hi.astype(F32) - h_mid.astype(F32)).astype(BF16)
    parts = jnp.concatenate([h_hi, h_mid, h_lo, jnp.zeros((13, D), BF16)], axis=0)
    arrive(3)
    hw = jnp.sum(nt(parts, w2_ref[...]), axis=0, keepdims=True)
    arrive(1)
    arrive(4)
    def tile_of(ref, t):
        first = SLOT if t == 0 else 0
        arrived = pl.ds(t * TILE + first, TILE - first)
        wait_bytes(ref.at[arrived], tile_sems.at[0 if ref is recv else 1, t])
        held = ref[t * TILE : (t + 1) * TILE, :]
        return held, unpack_last(held)

    def add_tile(ref, pick_ref, t, n):
        held, end = tile_of(ref, t)
        for s in range(0, n, 256):
            rows = pl.ds(s, 256)
            pick = pick_ref[rows, t * TILE : (t + 1) * TILE]
            for cols, part in ((pl.ds(0, PACK), held), (pl.ds(PACK, 128), end)):
                if t == 0:
                    att[rows, cols] = nn(pick, part)
                else:
                    att[rows, cols] += nn(pick, part)

    for t in range(ROWS // TILE):
        add_tile(recv, dp, t, LOOK)
    rows_held[...] = att[...].astype(BF16)
    for s in range(0, LOOK, 256):
        rows = pl.ds(s, 256)
        held = rows_held[rows, :]
        hid, dh = silu_parts(nn(held, first_ref[...]))
        hid = hid.astype(BF16)
        hidden[rows, :] = hid
        slope[rows, :] = dh
        tok_ref[rows, :] = (held.astype(F32) + nn(hid, second_ref[...])).astype(BF16)
    wait_bytes(send.at[later], sems.at[2])
    scale = 1.0 / math.sqrt(HD)
    arrive(2)
    for s in range(0, LOOK, RB):
        rows = pl.ds(s, RB)
        t = tok_ref[rows, :].astype(F32)
        r = lax.rsqrt(jnp.mean(t * t, axis=1, keepdims=True) + EPS)
        normed[rows, :] = (t * r * gain).astype(BF16)
    for c in range(0, 4 * D, 256):
        cols = pl.ds(c, 256)
        for s in range(0, LOOK, RB):
            rows = pl.ds(s, RB)
            p = nn(normed[rows, :], w1_ref[:, cols])
            sg = sigmoid(p)
            y = p * sg
            proj[rows, cols] = y.astype(BF16)
            dsl[rows, cols] = (sg + y * (1.0 - sg)).astype(BF16)
    for h in range(HEADS):
        hc = h * HD
        tab_h = jnp.broadcast_to(tab[h : h + 1, :], (RB, 128))
        for s in range(0, LOOK, RB):
            rows = pl.ds(s, RB)
            ke = keys_of(s)
            q = proj[rows, pl.ds(2 * D + hc, HD)]
            sc = nt(q, proj[0:ke, pl.ds(3 * D + hc, HD)]) * scale
            tt = [
                jnp.take_along_axis(tab_h, idx[rows, j : j + 128], axis=1)
                for j in range(0, ke, 128)
            ]
            sc = sc + jnp.concatenate(tt, axis=1)
            sg = sigmoid(sc)
            y = sc * sg
            w = (y * (1.0 / HIST)).astype(BF16)
            wts[h, rows, 0:ke] = w
            dwt[h, rows, 0:ke] = ((sg + y * (1.0 - sg)) * (1.0 / HIST)).astype(BF16)
            if ke < HIST:
                wts[h, rows, ke:HIST] = jnp.zeros((RB, HIST - ke), BF16)
            att[rows, pl.ds(hc, HD)] = nn(w, proj[0:ke, pl.ds(D + hc, HD)])
    own = {}
    for h in range(HEADS):
        hc = h * HD
        for s in range(HIST, LOOK, RB):
            rows = pl.ds(s, RB)
            q = proj[rows, pl.ds(2 * D + hc, HD)].astype(F32)
            k = proj[rows, pl.ds(3 * D + hc, HD)].astype(F32)
            v = proj[rows, pl.ds(D + hc, HD)].astype(F32)
            os = jnp.sum(q * k, axis=1, keepdims=True) * scale + tb_ref[h : h + 1, 0:1]
            sg = sigmoid(os)
            y = os * sg
            ow = (y * (1.0 / HIST)).astype(BF16).astype(F32)
            own[h, s] = (ow, (sg + y * (1.0 - sg)) * (1.0 / HIST))
            att[rows, pl.ds(hc, HD)] += ow * v
    label_col = column(label_ref[...])
    loss = jnp.zeros((1, 1), F32)
    uvec = jnp.zeros((1, D), F32)
    dlogit = {}
    for s in range(0, LOOK, RB):
        rows = pl.ds(s, RB)
        a = att[rows, :]
        cen = a - jnp.mean(a, axis=1, keepdims=True)
        spread = lax.rsqrt(jnp.mean(cen * cen, axis=1, keepdims=True) + EPS)
        n = cen * spread
        g = proj[rows, 0:D].astype(F32)
        mixed = (n * g).astype(BF16).astype(F32)
        t = tok_ref[rows, :].astype(F32)
        logit = jnp.sum(t * head + mixed * hw, axis=1, keepdims=True)
        lab = label_col[s : s + RB, 0:1]
        soft = jnp.maximum(logit, 0.0) + jnp.log1p(jnp.exp(-jnp.abs(logit)))
        loss = loss + jnp.sum(soft - lab * logit, axis=0, keepdims=True)
        dl = (jax.nn.sigmoid(logit) - lab) * (1.0 / LOOK)
        dlogit[s] = dl
        uvec = uvec + jnp.sum(mixed * dl, axis=0, keepdims=True)
        dm = (dl * hw).astype(BF16).astype(F32)
        dg = dm * n
        dp[rows, 0:D] = (dg * dsl[rows, 0:D].astype(F32)).astype(BF16)
        dn = dm * g
        da = spread * (
            dn - jnp.mean(dn, axis=1, keepdims=True) - n * jnp.mean(dn * n, axis=1, keepdims=True)
        )
        att[rows, :] = da
    u_held[0] = uvec
    loss_ref[...] = jnp.broadcast_to(loss * (1.0 / LOOK), loss_ref.shape)
    for h in range(HEADS):
        hc = h * HD
        for s in range(0, LOOK, RB):
            rows = pl.ds(s, RB)
            ke = keys_of(s)
            da = att[rows, pl.ds(hc, HD)]
            dw = nt(da.astype(BF16), proj[0:ke, pl.ds(D + hc, HD)])
            ds = (dw * dwt[h, rows, 0:ke].astype(F32) * scale).astype(BF16)
            dwt[h, rows, 0:ke] = ds
            if ke < HIST:
                dwt[h, rows, ke:HIST] = jnp.zeros((RB, HIST - ke), BF16)
            dq = nn(ds, proj[0:ke, pl.ds(3 * D + hc, HD)])
            if s >= HIST:
                q = proj[rows, pl.ds(2 * D + hc, HD)].astype(F32)
                k = proj[rows, pl.ds(3 * D + hc, HD)].astype(F32)
                v = proj[rows, pl.ds(D + hc, HD)].astype(F32)
                ow, osl = own[h, s]
                dos = jnp.sum(da * v, axis=1, keepdims=True) * osl * scale
                dq = dq + dos * k
                dcol = pl.ds(D + hc, HD)
                dp[rows, dcol] = (ow * da * dsl[rows, dcol].astype(F32)).astype(BF16)
                dcol = pl.ds(3 * D + hc, HD)
                dp[rows, dcol] = (dos * q * dsl[rows, dcol].astype(F32)).astype(BF16)
            dcol = pl.ds(2 * D + hc, HD)
            dp[rows, dcol] = (dq * dsl[rows, dcol].astype(F32)).astype(BF16)
        hist = pl.ds(0, HIST)
        dat = att[:, pl.ds(hc, HD)].T.astype(BF16)
        dcol = pl.ds(D + hc, HD)
        dp[hist, dcol] = (nn(dat, wts[h]).T * dsl[hist, dcol].astype(F32)).astype(BF16)
        qt = proj[:, pl.ds(2 * D + hc, HD)].astype(F32).T.astype(BF16)
        dcol = pl.ds(3 * D + hc, HD)
        dp[hist, dcol] = (nn(qt, dwt[h]).T * dsl[hist, dcol].astype(F32)).astype(BF16)
    z, core = user // 2, user % 2
    x, y = item // 4, item % 4
    own = {"x": x, "y": y, "z": z}

    def peer(**to):
        c = {**own, **to}
        return (c["z"] * 2 + to.get("core", core), c["x"] * 4 + c["y"])

    def copy(src, dst, to, send_sem, recv_sem):
        return pltpu.make_async_remote_copy(
            src_ref=src, dst_ref=dst, send_sem=send_sem, recv_sem=recv_sem,
            device_id=to, device_id_type=pl.DeviceIdType.MESH,
        )

    def at(n, size):
        return pl.ds(pl.multiple_of(n * size, size), size)

    def quarter(q):
        return at(q // 4, 16), at(q % 4, 128)

    def group(g):
        return pl.ds(2 * g, 2)

    def square(g):
        a0, a1, a2 = (own[a] for a in ORDER[g])
        rows = pl.ds(pl.multiple_of(core * 256 + a0 * 64 + a1 * 16, 16), 16)
        return (group(g), rows, at(a2, 128))

    def copies(g, stage):
        axis, plane = ORDER[g][0], ORDER[g][1:]
        a0 = own[axis]
        q = own[plane[0]] * 4 + own[plane[1]]
        todo = []
        if stage == 0:
            todo.append((terms.at[group(g), at(1 - core, 256), :], core_in.at[group(g)], peer(core=1 - core)))
        elif stage == 5:
            half_of = (group(g), at(core, 256))
            todo.append((sums_ref.at[half_of], sums_hbm.at[half_of], peer(core=1 - core)))
        elif stage in (1, 4):
            for d in (1, 2, 3):
                to = (a0 + d) % 4
                if stage == 1:
                    src, dst = half.at[group(g), at(to, 64), :], in1.at[g, d - 1]
                else:
                    src = dst = sums_ref.at[group(g), at(core * 4 + a0, 64), :]
                todo.append((src, dst, peer(**{axis: to})))
        else:
            for e in range(1, 16):
                to = (q + e) % 16
                if stage == 2:
                    r, c = quarter(to)
                    src, dst = part1.at[group(g), r, c], in2.at[g, e - 1]
                else:
                    src = dst = sums_ref.at[square(g)]
                todo.append((src, dst, peer(**{plane[0]: to // 4, plane[1]: to % 4})))
        return [
            copy(src, dst, to, send_sems.at[g, stage, n], recv_sems.at[g, stage, n])
            for n, (src, dst, to) in enumerate(todo)
        ]

    def own_half(g):
        half_of = (group(g), at(core, 256))
        return pltpu.make_async_copy(sums_ref.at[half_of], sums_hbm.at[half_of], out_sems.at[g])

    def start(g, stage):
        for c in copies(g, stage):
            c.start()
        if stage == 5:
            own_half(g).start()

    def finish(g, stage):
        for c in copies(g, stage):
            c.wait_recv()
        a0, a1, a2 = (own[a] for a in ORDER[g])
        if stage == 0:
            for b in (2 * g, 2 * g + 1):
                half[b] = (terms[b, at(core, 256), :].astype(F32) + core_in[b].astype(F32)).astype(BF16)
        elif stage == 1:
            total = half[group(g), at(a0, 64), :].astype(F32)
            for d in range(3):
                total = total + in1[g, d].astype(F32)
            part1[group(g)] = total.astype(BF16)
        elif stage == 2:
            total = part1[group(g), at(a1, 16), at(a2, 128)].astype(F32)
            for e in range(15):
                total = total + in2[g, e].astype(F32)
            sums_ref[square(g)] = total.astype(BF16)

    def u_copies(stage):
        if stage == 0:
            peers = [peer(core=1 - core)]
        else:
            a = "xyz"[stage - 1]
            peers = [peer(**{a: (own[a] + d) % 4}) for d in (1, 2, 3)]
        return [
            copy(u_held.at[stage], u_in.at[stage, n], to, u_sems.at[0, stage, n], u_sems.at[1, stage, n])
            for n, to in enumerate(peers)
        ]

    def u_start(stage):
        for c in u_copies(stage):
            c.start()

    def u_finish(stage):
        total = u_held[stage]
        for n, c in enumerate(u_copies(stage)):
            c.wait_recv()
            total = total + u_in[stage, n]
        if stage < 3:
            u_held[stage + 1] = total
        else:
            usum_ref[...] = total

    u_start(0)
    nrt = normed[...].astype(F32).T.astype(BF16)
    for b in range(4):
        for c in range(0, D, 256):
            terms[b, :, pl.ds(c, 256)] = nn(nrt, dp[:, pl.ds(b * D + c, 256)]).astype(BF16)
        if b % 2:
            start(b // 2, 0)
    for s in range(0, LOOK, RB):
        rows = pl.ds(s, RB)
        dnorm = nt(dp[rows, :], w1_ref[...])
        t = tok_ref[rows, :].astype(F32)
        r = lax.rsqrt(jnp.mean(t * t, axis=1, keepdims=True) + EPS)
        tn = dnorm * gain
        tg = dlogit[s] * head + r * tn - t * (r * r * r * jnp.mean(tn * t, axis=1, keepdims=True))
        tgb = tg.astype(BF16)
        de[rows, :] = tgb
        dpr = (nt(tgb, second_ref[...]) * slope[rows, :]).astype(BF16)
        dpre[rows, :] = dpr
        att[rows, :] = tg + nt(dpr, first_ref[...])
    terms[5] = nn(hidden[...].astype(F32).T.astype(BF16), de[...]).astype(BF16)
    terms[4] = nn(rows_held[...].astype(F32).T.astype(BF16), dpre[...]).astype(BF16)
    start(2, 0)
    for g in (0, 1):
        finish(g, 0)
        start(g, 1)
    u_finish(0)
    u_start(1)
    de[...] = att[...].astype(BF16)
    row_grad = de[...]

    for batch in range(OWNERS // BATCH):
        base = batch * BATCH * SLOT
        if base % TILE == 0:
            rows = pl.ds(base, TILE)
            pick = base + lax.broadcasted_iota(jnp.int32, (TILE, LOOK), 0) == slots
            send[rows, :] = pack(nn(pick.astype(F32).astype(BF16), row_grad))
        if batch == 0:
            back_recv[0:SLOT, :] = send[0:SLOT, :]

        @pl.loop(max(1, batch * BATCH), (batch + 1) * BATCH)
        def _(k):
            send_chunk(send, back_recv, k, (me + STEP * k) % OWNERS, sems.at[4], tile_sems.at[1, base // TILE])

        if batch == 1:
            for s in range(0, D, 128):
                sub = (s + lax.broadcasted_iota(jnp.int32, (128, 128), 0)).astype(F32)
                for q in range(0, ROWS, 128):
                    proj[pl.ds(s, 128), pl.ds(q, 128)] = (
                        (sub == idrow[0:1, q : q + 128]).astype(F32).astype(BF16)
                    )
        if batch in (12, 13):
            add_tile(back_recv, proj, batch - 12, D)
        if batch in PLAN:
            g, stage = PLAN[batch]
            finish(g, stage)
            start(g, stage + 1)
            if g == 2 and stage > 0:
                u_finish(stage)
                if stage < 3:
                    u_start(stage + 1)

    finish(2, 4)
    start(2, 5)
    for t in (2, 3):
        add_tile(back_recv, proj, t, D)
    table_out = pltpu.make_async_copy(att.at[pl.ds(0, D), :], tablegrad_hbm, out_sems.at[3])
    table_out.start()
    for g in range(GROUPS):
        finish(g, 5)
        own_half(g).wait()
    table_out.wait()
    wait_bytes(send.at[later], sems.at[4])
    for stage in range(4):
        for c in u_copies(stage):
            c.wait_send()
    for g in range(GROUPS):
        for stage in range(6):
            for c in copies(g, stage):
                c.wait_send()


VM = pl.BlockSpec(memory_space=pltpu.VMEM)
ANY = pl.BlockSpec(memory_space=pl.ANY)


def train_step(*args):
    dma = pltpu.SemaphoreType.DMA
    return pl.pallas_call(
        step_kernel,
        out_shape=(
            jax.ShapeDtypeStruct((D, D), F32),
            jax.ShapeDtypeStruct((2 * GROUPS, D, D), BF16),
            jax.ShapeDtypeStruct((1, D), F32),
            jax.ShapeDtypeStruct((1, 128), F32),
        ),
        in_specs=[VM] * 7 + [ANY] * 5,
        out_specs=(ANY, ANY, VM, VM),
        scratch_shapes=[
            pltpu.VMEM((2 * GROUPS, D, D), BF16),
            pltpu.VMEM((D, D), BF16),
            pltpu.VMEM((D, D), BF16),
            pltpu.VMEM((D, D), BF16),
            pltpu.VMEM((D, 4 * D), BF16),
            pltpu.VMEM((D, D), BF16),
            pltpu.VMEM((OWNERS, 1, 128), F32),
            pltpu.VMEM((OWNERS, 1, 128), F32),
            pltpu.VMEM((ROWS, 128), F32),
            pltpu.VMEM((8, ROWS), F32),
            pltpu.VMEM((ROWS, PACK), BF16),
            pltpu.VMEM((ROWS, PACK), BF16),
            pltpu.VMEM((ROWS, PACK), BF16),
            pltpu.VMEM((LOOK, D), BF16),
            pltpu.VMEM((LOOK, D), BF16),
            pltpu.VMEM((LOOK, D), F32),
            pltpu.VMEM((LOOK, D), BF16),
            pltpu.VMEM((LOOK, D), BF16),
            pltpu.VMEM((LOOK, 4 * D), BF16),
            pltpu.VMEM((LOOK, 4 * D), BF16),
            pltpu.VMEM((LOOK, HIST), jnp.int32),
            pltpu.VMEM((HEADS, LOOK, HIST), BF16),
            pltpu.VMEM((HEADS, LOOK, HIST), BF16),
            pltpu.VMEM((LOOK, D), F32),
            pltpu.VMEM((LOOK, 4 * D), BF16),
            pltpu.VMEM((LOOK, D), BF16),
            pltpu.VMEM((LOOK, D), BF16),
            pltpu.VMEM((2 * GROUPS, D, D), BF16),
            pltpu.VMEM((2 * GROUPS, 256, D), BF16),
            pltpu.VMEM((2 * GROUPS, 256, D), BF16),
            pltpu.VMEM((GROUPS, 3, 2, 64, D), BF16),
            pltpu.VMEM((2 * GROUPS, 64, D), BF16),
            pltpu.VMEM((GROUPS, 15, 2, 16, 128), BF16),
            pltpu.VMEM((4, 1, D), F32),
            pltpu.VMEM((4, 3, 1, D), F32),
            dma((5,)),
            dma((4,)),
            dma((2, ROWS // TILE)),
            dma((5,)),
            dma((GROUPS, 6, 15)),
            dma((GROUPS, 6, 15)),
            dma((2, 4, 3)),
        ],
        compiler_params=pltpu.CompilerParams(
            vmem_limit_bytes=60 * 2**20, collective_id=0, has_side_effects=True
        ),
        cost_estimate=pl.CostEstimate(
            flops=14 * 10**9, bytes_accessed=10 * 2**20, transcendentals=5 * 10**6
        ),
        name="step",
    )(*args)


def finish_kernel(tablegrad_ref, sums_ref, usum_ref, head_ref, table_ref, first_ref, second_ref, input_ref, output_ref):
    table_ref[...] = tablegrad_ref[...]
    first_ref[...] = sums_ref[4].astype(F32)
    second_ref[...] = sums_ref[5].astype(F32)
    for b in range(4):
        input_ref[:, pl.ds(b * D, D)] = sums_ref[b].astype(F32)
    output_ref[...] = column(usum_ref[...])[:, 0:1] * head_ref[...]


def outputs(tablegrad, sums, usum, head):
    n = 128

    def rows(width):
        return pl.BlockSpec((n, width), lambda i: (i, 0))

    def shape(width):
        return jax.ShapeDtypeStruct((D, width), F32)

    return pl.pallas_call(
        finish_kernel,
        grid=(D // n,),
        out_shape=(shape(D), shape(D), shape(D), shape(4 * D), shape(D)),
        in_specs=[
            rows(D),
            pl.BlockSpec((2 * GROUPS, n, D), lambda i: (0, i, 0)),
            pl.BlockSpec((1, n), lambda i: (0, i)),
            pl.BlockSpec((1, D), lambda i: (0, 0)),
        ],
        out_specs=(rows(D), rows(D), rows(D), rows(4 * D), rows(D)),
        compiler_params=pltpu.CompilerParams(vmem_limit_bytes=60 * 2**20),
        name="outputs",
    )(tablegrad, sums, usum, head)


def body(
    table, tower_first, tower_second, w_input, w_output, norm_gain, head_vec, time_bias,
    look_owner, look_row, event_time, labels,
):
    head = head_vec.reshape(1, D)
    tablegrad, sums, usum, loss = train_step(
        look_owner.reshape(1, LOOK), look_row, event_time, labels, norm_gain.reshape(1, D), head,
        time_bias, table, tower_first, tower_second, w_input, w_output,
    )
    table_grad, first_grad, second_grad, input_grad, output_grad = outputs(tablegrad, sums, usum, head)
    return (table_grad, first_grad, second_grad, input_grad, output_grad, loss[0, :1])


def solution(mesh):
    return jax.shard_map(
        body,
        mesh=mesh,
        in_specs=(
            P(("user", "item"), None), P(), P(), P(), P(), P(), P(), P(),
            P(("user", "item"), None, None), P(("user", "item"), None),
            P(("user", "item"), None), P(("user", "item"), None),
        ),
        out_specs=(P(("user", "item"), None), P(), P(), P(), P(), P(("user", "item"))),
        check_vma=False,
    )
```

```python
import math

import jax
import jax.numpy as jnp
from jax import lax
from jax.experimental import pallas as pl
from jax.experimental.pallas import tpu as pltpu
from jax.sharding import PartitionSpec as P

D = 512
HEADS = 4
HD = 128
HIST = 512
LOOK = 768
BUCKETS = 16
EPS = 1e-06
F32 = jnp.float32
BF16 = jnp.bfloat16
RB = 128
OWNERS = 128
SLOT = 16
USED = 12
PACK = 384
ROWS = OWNERS * SLOT
TILE = 512
STEP = 37
UNSTEP = 45
NEG = -1e30


def nn(a, b):
    return lax.dot_general(a, b, (((1,), (0,)), ((), ())), preferred_element_type=F32)


def nt(a, b):
    return lax.dot_general(a, b, (((1,), (1,)), ((), ())), preferred_element_type=F32)


def sigmoid(x):
    return 0.5 + 0.5 * jnp.tanh(0.5 * x)


def column(row):
    return jnp.broadcast_to(row.astype(F32), (128, row.shape[1])).T


def keys_of(start):
    return min(HIST, start + RB)


def place():
    return lax.axis_index("user"), lax.axis_index("item")


def device(index):
    return (index // 16, index % 16)


def greet():
    barrier = pltpu.get_barrier_semaphore()

    user, item = place()

    def hail(du, di):
        to = ((user + du) % 8, (item + di) % 16)
        pl.semaphore_signal(barrier, inc=1, device_id=to, device_id_type=pl.DeviceIdType.MESH)

    for di in range(1, 16):
        hail(0, di)
    for di in range(16):

        @pl.loop(1, 8)
        def _(du):
            hail(du, di)


def meet():
    pl.semaphore_wait(pltpu.get_barrier_semaphore(), OWNERS - 1)


def row_in_slot(n):
    return lax.broadcasted_iota(jnp.int32, (n, 128), 0) % SLOT


def pack(y):
    r = row_in_slot(y.shape[0])
    last = y[:, PACK:D]
    out = [
        jnp.where(r >= USED, pltpu.roll(last, USED - 4 * b, 0), y[:, 128 * b : 128 * (b + 1)])
        for b in range(3)
    ]
    return jnp.concatenate(out, axis=1).astype(BF16)


def unpack_last(y):
    n = y.shape[0]
    r = row_in_slot(n)
    p = [pltpu.roll(y[:, 128 * b : 128 * (b + 1)].astype(F32), n - USED + 4 * b, 0) for b in range(3)]
    return jnp.where(r < 4, p[0], jnp.where(r < 8, p[1], p[2])).astype(BF16)


def chunk(ref, k):
    return ref.at[pl.ds(pl.multiple_of(k * SLOT, SLOT), SLOT), :]


def send_chunk(send, recv, k, target, send_sem, recv_sem):
    pltpu.make_async_remote_copy(
        src_ref=chunk(send, k),
        dst_ref=chunk(recv, k),
        send_sem=send_sem,
        recv_sem=recv_sem,
        device_id=device(target),
        device_id_type=pl.DeviceIdType.MESH,
    ).start()


def wait_bytes(ref, sem):
    pltpu.make_async_copy(ref, ref, sem).wait()


def silu_parts(p):
    sg = sigmoid(p)
    y = p * sg
    return y, sg + y * (1.0 - sg)


GROUPS = 3
ORDER = ("xyz", "yzx", "zxy")
BATCH = 8
PLAN = {
    0: (2, 0), 2: (0, 1), 3: (1, 1), 4: (2, 1), 5: (0, 2), 6: (1, 2), 7: (2, 2),
    8: (0, 3), 9: (1, 3), 10: (2, 3), 13: (0, 4), 14: (1, 4),
}


def step_kernel(
    owner_ref, row_ref, stamp_row_ref, label_ref, gain_ref, head_ref, tb_ref,
    table_hbm, first_hbm, second_hbm, w1_hbm, w2_hbm,
    tablegrad_hbm, sums_hbm, usum_ref, loss_ref,
    sums_ref, table_ref, first_ref, second_ref, w1_ref, w2_ref,
    ids_send, ids_recv, idq, idrow, send, recv, back_recv, rows_held, hidden, slope, tok_ref,
    normed, proj, dsl, idx, wts, dwt, att, dp, de, dpre,
    terms, core_in, half, in1, part1, in2, u_held, u_in,
    load_sems, out_sems, tile_sems, sems, send_sems, recv_sems, u_sems,
):
    user, item = place()
    me = user * 16 + item
    loads = [
        pltpu.make_async_copy(src, dst, load_sems.at[n])
        for n, (src, dst) in enumerate(
            ((table_hbm, table_ref), (first_hbm, first_ref), (w1_hbm, w1_ref), (w2_hbm, w2_ref), (second_hbm, second_ref))
        )
    ]
    for load in loads:
        load.start()

    gain = gain_ref[...]
    head = head_ref[...]

    def arrive(n):
        loads[n].wait()

    greet()
    j_row = (UNSTEP * (owner_ref[...] - me + OWNERS)) % OWNERS
    named = lax.broadcasted_iota(jnp.int32, (OWNERS, LOOK), 0) == j_row
    named_b = named.astype(F32).astype(BF16)
    before = lax.broadcasted_iota(jnp.int32, (LOOK, LOOK), 0) < lax.broadcasted_iota(
        jnp.int32, (LOOK, LOOK), 1
    )
    earlier = nn(named_b, before.astype(F32).astype(BF16))
    rank = jnp.sum(jnp.where(named, earlier, 0.0), axis=0, keepdims=True)
    slots = j_row * SLOT + rank.astype(jnp.int32)
    lanes = lax.broadcasted_iota(jnp.int32, (LOOK, 128), 1).astype(F32)
    listed = jnp.where(column(rank) == lanes, column(row_ref[...]) - 256.0, 0.0)
    ids_send[:, 0, :] = nn(named_b, listed.astype(BF16))
    ids_recv[0] = ids_send[0]
    meet()

    @pl.loop(1, OWNERS)
    def _(k):
        pltpu.make_async_remote_copy(
            src_ref=ids_send.at[k],
            dst_ref=ids_recv.at[k],
            send_sem=sems.at[0],
            recv_sem=sems.at[1],
            device_id=device((me + STEP * k) % OWNERS),
            device_id_type=pl.DeviceIdType.MESH,
        ).start()

    slot_col = column(slots)
    others = pl.ds(1, OWNERS - 1)
    later = pl.ds(SLOT, ROWS - SLOT)
    arrive(0)
    wait_bytes(ids_recv.at[others], sems.at[1])
    wait_bytes(ids_send.at[others], sems.at[0])
    ids = ids_recv[:, 0, :].astype(BF16)

    def fresh(t):
        return max(1, t * (TILE // SLOT)), (t + 1) * (TILE // SLOT)

    for t in range(ROWS // TILE):
        base = t * TILE
        rows = pl.ds(base, TILE)
        slot_at = base + lax.broadcasted_iota(jnp.int32, (TILE, 128), 0)
        lane = lax.broadcasted_iota(jnp.int32, (TILE, 128), 1)
        spread = nn((slot_at // SLOT == lane).astype(F32).astype(BF16), ids)
        r = slot_at % SLOT
        mine = jnp.sum(jnp.where(r == lane, spread + 256.0, 0.0), axis=1, keepdims=True)
        mine = jnp.where(r < USED, mine, -1.0)
        idq[rows, :] = mine
        cols = lane.astype(F32)
        pick = jnp.concatenate(
            [(mine == cols + 128.0 * b).astype(F32).astype(BF16) for b in range(4)], axis=1
        )
        send[rows, :] = pack(nn(pick, table_ref[...]))

        @pl.loop(*fresh(t))
        def _(k):
            target = (me - (STEP * k) % OWNERS + OWNERS) % OWNERS
            send_chunk(send, recv, k, target, sems.at[2], tile_sems.at[0, t])

    recv[0:SLOT, :] = send[0:SLOT, :]
    idrow[...] = idq[...].T[0:8, :]
    for s in range(0, LOOK, RB):
        mark = slot_col[s : s + RB, :]
        cols = lax.broadcasted_iota(jnp.int32, (RB, 128), 1).astype(F32)
        for b in range(0, ROWS, 128):
            dp[pl.ds(s, RB), pl.ds(b, 128)] = (mark == cols + float(b)).astype(F32).astype(BF16)
    lane = lax.broadcasted_iota(jnp.int32, (HEADS, 128), 1)
    tab = jnp.zeros((HEADS, 128), F32)
    for k in range(BUCKETS):
        tab = tab + jnp.where(lane <= 31 - k, tb_ref[:, k : k + 1], 0.0)
    tab = jnp.where(lane == 33, NEG, tab)
    stamp_col = column(stamp_row_ref[...]).astype(jnp.int32)
    for s in range(0, LOOK, RB):
        rows = pl.ds(s, RB)
        ke = keys_of(s)
        now = jnp.concatenate([stamp_col[s : s + RB, :]] * (ke // 128), axis=1)
        gap = now - stamp_row_ref[:, 0:ke]
        lz = lax.clz(gap + 1)
        if s < HIST:
            i_pos = s + lax.broadcasted_iota(jnp.int32, (RB, ke), 0)
            j_pos = lax.broadcasted_iota(jnp.int32, (RB, ke), 1)
            lz = jnp.where(j_pos <= i_pos, lz, 33)
        idx[rows, 0:ke] = lz
    h_hi = head.astype(BF16)
    h_mid = (head - h_hi.astype(F32)).astype(BF16)
    h_lo = (head - h_hi.astype(F32) - h_mid.astype(F32)).astype(BF16)
    parts = jnp.concatenate([h_hi, h_mid, h_lo, jnp.zeros((13, D), BF16)], axis=0)
    arrive(3)
    hw = jnp.sum(nt(parts, w2_ref[...]), axis=0, keepdims=True)
    arrive(1)
    arrive(4)
    def tile_of(ref, t):
        first = SLOT if t == 0 else 0
        arrived = pl.ds(t * TILE + first, TILE - first)
        wait_bytes(ref.at[arrived], tile_sems.at[0 if ref is recv else 1, t])
        held = ref[t * TILE : (t + 1) * TILE, :]
        return held, unpack_last(held)

    def add_tile(ref, pick_ref, t, n):
        held, end = tile_of(ref, t)
        for s in range(0, n, 256):
            rows = pl.ds(s, 256)
            pick = pick_ref[rows, t * TILE : (t + 1) * TILE]
            for cols, part in ((pl.ds(0, PACK), held), (pl.ds(PACK, 128), end)):
                if t == 0:
                    att[rows, cols] = nn(pick, part)
                else:
                    att[rows, cols] += nn(pick, part)

    for t in range(ROWS // TILE):
        add_tile(recv, dp, t, LOOK)
    rows_held[...] = att[...].astype(BF16)
    for s in range(0, LOOK, 256):
        rows = pl.ds(s, 256)
        held = rows_held[rows, :]
        hid, dh = silu_parts(nn(held, first_ref[...]))
        hid = hid.astype(BF16)
        hidden[rows, :] = hid
        slope[rows, :] = dh
        tok_ref[rows, :] = (held.astype(F32) + nn(hid, second_ref[...])).astype(BF16)
    wait_bytes(send.at[later], sems.at[2])
    scale = 1.0 / math.sqrt(HD)
    arrive(2)
    for s in range(0, LOOK, RB):
        rows = pl.ds(s, RB)
        t = tok_ref[rows, :].astype(F32)
        r = lax.rsqrt(jnp.mean(t * t, axis=1, keepdims=True) + EPS)
        normed[rows, :] = (t * r * gain).astype(BF16)
    for c in range(0, 4 * D, 256):
        cols = pl.ds(c, 256)
        for s in range(0, LOOK, RB):
            rows = pl.ds(s, RB)
            p = nn(normed[rows, :], w1_ref[:, cols])
            sg = sigmoid(p)
            y = p * sg
            proj[rows, cols] = y.astype(BF16)
            dsl[rows, cols] = (sg + y * (1.0 - sg)).astype(BF16)
    for h in range(HEADS):
        hc = h * HD
        tab_h = jnp.broadcast_to(tab[h : h + 1, :], (RB, 128))
        for s in range(0, LOOK, RB):
            rows = pl.ds(s, RB)
            ke = keys_of(s)
            q = proj[rows, pl.ds(2 * D + hc, HD)]
            sc = nt(q, proj[0:ke, pl.ds(3 * D + hc, HD)]) * scale
            tt = [
                jnp.take_along_axis(tab_h, idx[rows, j : j + 128], axis=1)
                for j in range(0, ke, 128)
            ]
            sc = sc + jnp.concatenate(tt, axis=1)
            sg = sigmoid(sc)
            y = sc * sg
            w = (y * (1.0 / HIST)).astype(BF16)
            wts[h, rows, 0:ke] = w
            dwt[h, rows, 0:ke] = ((sg + y * (1.0 - sg)) * (1.0 / HIST)).astype(BF16)
            if ke < HIST:
                wts[h, rows, ke:HIST] = jnp.zeros((RB, HIST - ke), BF16)
            att[rows, pl.ds(hc, HD)] = nn(w, proj[0:ke, pl.ds(D + hc, HD)])
    own = {}
    for h in range(HEADS):
        hc = h * HD
        for s in range(HIST, LOOK, RB):
            rows = pl.ds(s, RB)
            q = proj[rows, pl.ds(2 * D + hc, HD)].astype(F32)
            k = proj[rows, pl.ds(3 * D + hc, HD)].astype(F32)
            v = proj[rows, pl.ds(D + hc, HD)].astype(F32)
            os = jnp.sum(q * k, axis=1, keepdims=True) * scale + tb_ref[h : h + 1, 0:1]
            sg = sigmoid(os)
            y = os * sg
            ow = (y * (1.0 / HIST)).astype(BF16).astype(F32)
            own[h, s] = (ow, (sg + y * (1.0 - sg)) * (1.0 / HIST))
            att[rows, pl.ds(hc, HD)] += ow * v
    label_col = column(label_ref[...])
    loss = jnp.zeros((1, 1), F32)
    uvec = jnp.zeros((1, D), F32)
    dlogit = {}
    for s in range(0, LOOK, RB):
        rows = pl.ds(s, RB)
        a = att[rows, :]
        cen = a - jnp.mean(a, axis=1, keepdims=True)
        spread = lax.rsqrt(jnp.mean(cen * cen, axis=1, keepdims=True) + EPS)
        n = cen * spread
        g = proj[rows, 0:D].astype(F32)
        mixed = (n * g).astype(BF16).astype(F32)
        t = tok_ref[rows, :].astype(F32)
        logit = jnp.sum(t * head + mixed * hw, axis=1, keepdims=True)
        lab = label_col[s : s + RB, 0:1]
        soft = jnp.maximum(logit, 0.0) + jnp.log1p(jnp.exp(-jnp.abs(logit)))
        loss = loss + jnp.sum(soft - lab * logit, axis=0, keepdims=True)
        dl = (jax.nn.sigmoid(logit) - lab) * (1.0 / LOOK)
        dlogit[s] = dl
        uvec = uvec + jnp.sum(mixed * dl, axis=0, keepdims=True)
        dm = (dl * hw).astype(BF16).astype(F32)
        dg = dm * n
        dp[rows, 0:D] = (dg * dsl[rows, 0:D].astype(F32)).astype(BF16)
        dn = dm * g
        da = spread * (
            dn - jnp.mean(dn, axis=1, keepdims=True) - n * jnp.mean(dn * n, axis=1, keepdims=True)
        )
        att[rows, :] = da
    u_held[0] = uvec
    loss_ref[...] = jnp.broadcast_to(loss * (1.0 / LOOK), loss_ref.shape)
    for h in range(HEADS):
        hc = h * HD
        for s in range(0, LOOK, RB):
            rows = pl.ds(s, RB)
            ke = keys_of(s)
            da = att[rows, pl.ds(hc, HD)]
            dw = nt(da.astype(BF16), proj[0:ke, pl.ds(D + hc, HD)])
            ds = (dw * dwt[h, rows, 0:ke].astype(F32) * scale).astype(BF16)
            dwt[h, rows, 0:ke] = ds
            if ke < HIST:
                dwt[h, rows, ke:HIST] = jnp.zeros((RB, HIST - ke), BF16)
            dq = nn(ds, proj[0:ke, pl.ds(3 * D + hc, HD)])
            if s >= HIST:
                q = proj[rows, pl.ds(2 * D + hc, HD)].astype(F32)
                k = proj[rows, pl.ds(3 * D + hc, HD)].astype(F32)
                v = proj[rows, pl.ds(D + hc, HD)].astype(F32)
                ow, osl = own[h, s]
                dos = jnp.sum(da * v, axis=1, keepdims=True) * osl * scale
                dq = dq + dos * k
                dcol = pl.ds(D + hc, HD)
                dp[rows, dcol] = (ow * da * dsl[rows, dcol].astype(F32)).astype(BF16)
                dcol = pl.ds(3 * D + hc, HD)
                dp[rows, dcol] = (dos * q * dsl[rows, dcol].astype(F32)).astype(BF16)
            dcol = pl.ds(2 * D + hc, HD)
            dp[rows, dcol] = (dq * dsl[rows, dcol].astype(F32)).astype(BF16)
        hist = pl.ds(0, HIST)
        dat = att[:, pl.ds(hc, HD)].T.astype(BF16)
        dcol = pl.ds(D + hc, HD)
        dp[hist, dcol] = (nn(dat, wts[h]).T * dsl[hist, dcol].astype(F32)).astype(BF16)
        qt = proj[:, pl.ds(2 * D + hc, HD)].astype(F32).T.astype(BF16)
        dcol = pl.ds(3 * D + hc, HD)
        dp[hist, dcol] = (nn(qt, dwt[h]).T * dsl[hist, dcol].astype(F32)).astype(BF16)
    z, core = user // 2, user % 2
    x, y = item // 4, item % 4
    own = {"x": x, "y": y, "z": z}

    def peer(**to):
        c = {**own, **to}
        return (c["z"] * 2 + to.get("core", core), c["x"] * 4 + c["y"])

    def copy(src, dst, to, send_sem, recv_sem):
        return pltpu.make_async_remote_copy(
            src_ref=src, dst_ref=dst, send_sem=send_sem, recv_sem=recv_sem,
            device_id=to, device_id_type=pl.DeviceIdType.MESH,
        )

    def at(n, size):
        return pl.ds(pl.multiple_of(n * size, size), size)

    def quarter(q):
        return at(q // 4, 16), at(q % 4, 128)

    def group(g):
        return pl.ds(2 * g, 2)

    def square(g):
        a0, a1, a2 = (own[a] for a in ORDER[g])
        rows = pl.ds(pl.multiple_of(core * 256 + a0 * 64 + a1 * 16, 16), 16)
        return (group(g), rows, at(a2, 128))

    def copies(g, stage):
        axis, plane = ORDER[g][0], ORDER[g][1:]
        a0 = own[axis]
        q = own[plane[0]] * 4 + own[plane[1]]
        todo = []
        if stage == 0:
            todo.append((terms.at[group(g), at(1 - core, 256), :], core_in.at[group(g)], peer(core=1 - core)))
        elif stage == 5:
            half_of = (group(g), at(core, 256))
            todo.append((sums_ref.at[half_of], sums_hbm.at[half_of], peer(core=1 - core)))
        elif stage in (1, 4):
            for d in (1, 2, 3):
                to = (a0 + d) % 4
                if stage == 1:
                    src, dst = half.at[group(g), at(to, 64), :], in1.at[g, d - 1]
                else:
                    src = dst = sums_ref.at[group(g), at(core * 4 + a0, 64), :]
                todo.append((src, dst, peer(**{axis: to})))
        else:
            for e in range(1, 16):
                to = (q + e) % 16
                if stage == 2:
                    r, c = quarter(to)
                    src, dst = part1.at[group(g), r, c], in2.at[g, e - 1]
                else:
                    src = dst = sums_ref.at[square(g)]
                todo.append((src, dst, peer(**{plane[0]: to // 4, plane[1]: to % 4})))
        return [
            copy(src, dst, to, send_sems.at[g, stage, n], recv_sems.at[g, stage, n])
            for n, (src, dst, to) in enumerate(todo)
        ]

    def own_half(g):
        half_of = (group(g), at(core, 256))
        return pltpu.make_async_copy(sums_ref.at[half_of], sums_hbm.at[half_of], out_sems.at[g])

    def start(g, stage):
        for c in copies(g, stage):
            c.start()
        if stage == 5:
            own_half(g).start()

    def finish(g, stage):
        for c in copies(g, stage):
            c.wait_recv()
        a0, a1, a2 = (own[a] for a in ORDER[g])
        if stage == 0:
            for b in (2 * g, 2 * g + 1):
                half[b] = (terms[b, at(core, 256), :].astype(F32) + core_in[b].astype(F32)).astype(BF16)
        elif stage == 1:
            total = half[group(g), at(a0, 64), :].astype(F32)
            for d in range(3):
                total = total + in1[g, d].astype(F32)
            part1[group(g)] = total.astype(BF16)
        elif stage == 2:
            total = part1[group(g), at(a1, 16), at(a2, 128)].astype(F32)
            for e in range(15):
                total = total + in2[g, e].astype(F32)
            sums_ref[square(g)] = total.astype(BF16)

    def u_copies(stage):
        if stage == 0:
            peers = [peer(core=1 - core)]
        else:
            a = "xyz"[stage - 1]
            peers = [peer(**{a: (own[a] + d) % 4}) for d in (1, 2, 3)]
        return [
            copy(u_held.at[stage], u_in.at[stage, n], to, u_sems.at[0, stage, n], u_sems.at[1, stage, n])
            for n, to in enumerate(peers)
        ]

    def u_start(stage):
        for c in u_copies(stage):
            c.start()

    def u_finish(stage):
        total = u_held[stage]
        for n, c in enumerate(u_copies(stage)):
            c.wait_recv()
            total = total + u_in[stage, n]
        if stage < 3:
            u_held[stage + 1] = total
        else:
            usum_ref[...] = total

    u_start(0)
    nrt = normed[...].astype(F32).T.astype(BF16)
    for b in range(4):
        for c in range(0, D, 256):
            terms[b, :, pl.ds(c, 256)] = nn(nrt, dp[:, pl.ds(b * D + c, 256)]).astype(BF16)
        if b % 2:
            start(b // 2, 0)
    for s in range(0, LOOK, RB):
        rows = pl.ds(s, RB)
        dnorm = nt(dp[rows, :], w1_ref[...])
        t = tok_ref[rows, :].astype(F32)
        r = lax.rsqrt(jnp.mean(t * t, axis=1, keepdims=True) + EPS)
        tn = dnorm * gain
        tg = dlogit[s] * head + r * tn - t * (r * r * r * jnp.mean(tn * t, axis=1, keepdims=True))
        tgb = tg.astype(BF16)
        de[rows, :] = tgb
        dpr = (nt(tgb, second_ref[...]) * slope[rows, :]).astype(BF16)
        dpre[rows, :] = dpr
        att[rows, :] = tg + nt(dpr, first_ref[...])
    terms[5] = nn(hidden[...].astype(F32).T.astype(BF16), de[...]).astype(BF16)
    terms[4] = nn(rows_held[...].astype(F32).T.astype(BF16), dpre[...]).astype(BF16)
    start(2, 0)
    for g in (0, 1):
        finish(g, 0)
        start(g, 1)
    u_finish(0)
    u_start(1)
    de[...] = att[...].astype(BF16)
    row_grad = de[...]

    for batch in range(OWNERS // BATCH):
        base = batch * BATCH * SLOT
        if base % TILE == 0:
            rows = pl.ds(base, TILE)
            pick = base + lax.broadcasted_iota(jnp.int32, (TILE, LOOK), 0) == slots
            send[rows, :] = pack(nn(pick.astype(F32).astype(BF16), row_grad))
        if batch == 0:
            back_recv[0:SLOT, :] = send[0:SLOT, :]

        @pl.loop(max(1, batch * BATCH), (batch + 1) * BATCH)
        def _(k):
            send_chunk(send, back_recv, k, (me + STEP * k) % OWNERS, sems.at[4], tile_sems.at[1, base // TILE])

        if batch == 1:
            for s in range(0, D, 128):
                sub = (s + lax.broadcasted_iota(jnp.int32, (128, 128), 0)).astype(F32)
                for q in range(0, ROWS, 128):
                    proj[pl.ds(s, 128), pl.ds(q, 128)] = (
                        (sub == idrow[0:1, q : q + 128]).astype(F32).astype(BF16)
                    )
        if batch in (12, 13):
            add_tile(back_recv, proj, batch - 12, D)
        if batch in PLAN:
            g, stage = PLAN[batch]
            finish(g, stage)
            start(g, stage + 1)
            if g == 2 and stage > 0:
                u_finish(stage)
                if stage < 3:
                    u_start(stage + 1)

    finish(2, 4)
    start(2, 5)
    for t in (2, 3):
        add_tile(back_recv, proj, t, D)
    table_out = pltpu.make_async_copy(att.at[pl.ds(0, D), :], tablegrad_hbm, out_sems.at[3])
    table_out.start()
    for g in range(GROUPS):
        finish(g, 5)
        own_half(g).wait()
    table_out.wait()
    wait_bytes(send.at[later], sems.at[4])
    for stage in range(4):
        for c in u_copies(stage):
            c.wait_send()
    for g in range(GROUPS):
        for stage in range(6):
            for c in copies(g, stage):
                c.wait_send()


VM = pl.BlockSpec(memory_space=pltpu.VMEM)
ANY = pl.BlockSpec(memory_space=pl.ANY)


def train_step(*args):
    dma = pltpu.SemaphoreType.DMA
    return pl.pallas_call(
        step_kernel,
        out_shape=(
            jax.ShapeDtypeStruct((D, D), F32),
            jax.ShapeDtypeStruct((2 * GROUPS, D, D), BF16),
            jax.ShapeDtypeStruct((1, D), F32),
            jax.ShapeDtypeStruct((1, 128), F32),
        ),
        in_specs=[VM] * 7 + [ANY] * 5,
        out_specs=(ANY, ANY, VM, VM),
        scratch_shapes=[
            pltpu.VMEM((2 * GROUPS, D, D), BF16),
            pltpu.VMEM((D, D), BF16),
            pltpu.VMEM((D, D), BF16),
            pltpu.VMEM((D, D), BF16),
            pltpu.VMEM((D, 4 * D), BF16),
            pltpu.VMEM((D, D), BF16),
            pltpu.VMEM((OWNERS, 1, 128), F32),
            pltpu.VMEM((OWNERS, 1, 128), F32),
            pltpu.VMEM((ROWS, 128), F32),
            pltpu.VMEM((8, ROWS), F32),
            pltpu.VMEM((ROWS, PACK), BF16),
            pltpu.VMEM((ROWS, PACK), BF16),
            pltpu.VMEM((ROWS, PACK), BF16),
            pltpu.VMEM((LOOK, D), BF16),
            pltpu.VMEM((LOOK, D), BF16),
            pltpu.VMEM((LOOK, D), F32),
            pltpu.VMEM((LOOK, D), BF16),
            pltpu.VMEM((LOOK, D), BF16),
            pltpu.VMEM((LOOK, 4 * D), BF16),
            pltpu.VMEM((LOOK, 4 * D), BF16),
            pltpu.VMEM((LOOK, HIST), jnp.int32),
            pltpu.VMEM((HEADS, LOOK, HIST), BF16),
            pltpu.VMEM((HEADS, LOOK, HIST), BF16),
            pltpu.VMEM((LOOK, D), F32),
            pltpu.VMEM((LOOK, 4 * D), BF16),
            pltpu.VMEM((LOOK, D), BF16),
            pltpu.VMEM((LOOK, D), BF16),
            pltpu.VMEM((2 * GROUPS, D, D), BF16),
            pltpu.VMEM((2 * GROUPS, 256, D), BF16),
            pltpu.VMEM((2 * GROUPS, 256, D), BF16),
            pltpu.VMEM((GROUPS, 3, 2, 64, D), BF16),
            pltpu.VMEM((2 * GROUPS, 64, D), BF16),
            pltpu.VMEM((GROUPS, 15, 2, 16, 128), BF16),
            pltpu.VMEM((4, 1, D), F32),
            pltpu.VMEM((4, 3, 1, D), F32),
            dma((5,)),
            dma((4,)),
            dma((2, ROWS // TILE)),
            dma((5,)),
            dma((GROUPS, 6, 15)),
            dma((GROUPS, 6, 15)),
            dma((2, 4, 3)),
        ],
        compiler_params=pltpu.CompilerParams(
            vmem_limit_bytes=60 * 2**20, collective_id=0, has_side_effects=True
        ),
        cost_estimate=pl.CostEstimate(
            flops=14 * 10**9, bytes_accessed=10 * 2**20, transcendentals=5 * 10**6
        ),
        name="step",
    )(*args)


def finish_kernel(tablegrad_ref, sums_ref, usum_ref, head_ref, table_ref, first_ref, second_ref, input_ref, output_ref):
    table_ref[...] = tablegrad_ref[...]
    first_ref[...] = sums_ref[4].astype(F32)
    second_ref[...] = sums_ref[5].astype(F32)
    for b in range(4):
        input_ref[:, pl.ds(b * D, D)] = sums_ref[b].astype(F32)
    output_ref[...] = column(usum_ref[...])[:, 0:1] * head_ref[...]


def outputs(tablegrad, sums, usum, head):
    n = 128

    def rows(width):
        return pl.BlockSpec((n, width), lambda i: (i, 0))

    def shape(width):
        return jax.ShapeDtypeStruct((D, width), F32)

    return pl.pallas_call(
        finish_kernel,
        grid=(D // n,),
        out_shape=(shape(D), shape(D), shape(D), shape(4 * D), shape(D)),
        in_specs=[
            rows(D),
            pl.BlockSpec((2 * GROUPS, n, D), lambda i: (0, i, 0)),
            pl.BlockSpec((1, n), lambda i: (0, i)),
            pl.BlockSpec((1, D), lambda i: (0, 0)),
        ],
        out_specs=(rows(D), rows(D), rows(D), rows(4 * D), rows(D)),
        compiler_params=pltpu.CompilerParams(vmem_limit_bytes=60 * 2**20),
        name="outputs",
    )(tablegrad, sums, usum, head)


def body(
    table, tower_first, tower_second, w_input, w_output, norm_gain, head_vec, time_bias,
    look_owner, look_row, event_time, labels,
):
    head = head_vec.reshape(1, D)
    tablegrad, sums, usum, loss = train_step(
        look_owner.reshape(1, LOOK), look_row, event_time, labels, norm_gain.reshape(1, D), head,
        time_bias, table, tower_first, tower_second, w_input, w_output,
    )
    table_grad, first_grad, second_grad, input_grad, output_grad = outputs(tablegrad, sums, usum, head)
    return (table_grad, first_grad, second_grad, input_grad, output_grad, loss[0, :1])


def solution(mesh):
    return jax.shard_map(
        body,
        mesh=mesh,
        in_specs=(
            P(("user", "item"), None), P(), P(), P(), P(), P(), P(), P(),
            P(("user", "item"), None, None), P(("user", "item"), None),
            P(("user", "item"), None), P(("user", "item"), None),
        ),
        out_specs=(P(("user", "item"), None), P(), P(), P(), P(), P(("user", "item"))),
        check_vma=False,
    )
```
